128 devices in a mesh: dp: 4 (over y_hi, core), ctx: 32 (over y_lo, z, x).
Axes of the slice: x: 4, y: 4 (y_hi: 2, y_lo: 2; y = y_hi * 2 + y_lo), z: 4, core: 2. Of those that a mesh axis runs over, the one named last changes fastest.
Arguments:
- trunk_input: bfloat16 [4, 8192, 768], P('dp', 'ctx'), may hold values from -6 to 6
- tokens: int32 [4, 8192], P('dp', 'ctx'), may hold values from 0 to 3
- token_table: float32 [4, 768], replicated, may hold values from -3 to 3
- conv_weight: bfloat16 [2, 3, 768, 384], replicated, may hold values from -0.125 to 0.125
- out_weight: bfloat16 [2, 384, 768], replicated, may hold values from -0.3125 to 0.3125
- norm_gain: float32 [2, 768], replicated, may hold values from 0.1 to 1.9
- mid_gain: float32 [2, 384], replicated, may hold values from 0.1 to 1.9
- strand_perm: int32 [768], replicated, may hold values from 0 to 767, each once
- dilation: int32 [2], replicated, may hold values from 1 to 64, as said below
- out_cotangent: bfloat16 [4, 8192, 768], P('dp', 'ctx'), may hold values from -6 to 6
Outputs:
- block_output: bfloat16 [4, 8192, 768], P('dp', 'ctx')
- trunk_grad: bfloat16 [4, 8192, 768], P('dp', 'ctx')
- table_grad: float32 [4, 768], replicated
- conv_grad: float32 [2, 3, 768, 384], replicated
- out_weight_grad: float32 [2, 384, 768], replicated
- norm_gain_grad: float32 [2, 768], replicated
- mid_gain_grad: float32 [2, 384], replicated
The draws below stay inside these ranges and needn't reach their ends.
Inputs may be any that keep to these rules, and one draw needn't show every extreme that they name: Each block's dilation lies in 1 .. 64, and some block has exactly 64. `strand_perm`: each channel index appears once.
All inputs are finite; a program needn't handle non-finite values.
Results may differ from the reference program's by a relative error of at most 0.014.
Values may be sent and summed in bfloat16 or wider, within the bound.
A program may use at most 128 MiB of HBM per device.

```python
import jax
import jax.numpy as jnp
from jax import lax

C = 768
M = 384
LAYERS = 2
DMAX = 64
BINS = 8192
WINDOWS = 4


def draw_dilation(key, part):
    key_rates, key_pick = jax.random.split(key)
    dilations = jax.random.randint(key_rates, (LAYERS,), 1, DMAX + 1, dtype=jnp.int32)
    chosen = jax.random.randint(key_pick, (), 0, LAYERS, dtype=jnp.int32)
    return jnp.where(jnp.arange(LAYERS, dtype=jnp.int32) == chosen, jnp.int32(DMAX), dilations)


def plant(values, stream_key, low, high):
    longest = values.shape.index(max(values.shape))
    spots = []
    for shift in (0, 1):
        where = [jax.random.randint(jax.random.fold_in(stream_key, axis), (), 0, length) for axis, length in enumerate(values.shape)]
        where[longest] = (where[longest] + shift) % values.shape[longest]
        spots.append(tuple(where))
    return values.at[spots[0]].set(low).at[spots[1]].set(high)


def block_levels(stream_key, dims, pieces, smallest, top_value):
    def one(axis_at, blocks):
        draws = jax.random.uniform(jax.random.fold_in(jax.random.fold_in(stream_key, 6), axis_at), (blocks,), jnp.float32, smallest / len(pieces), top_value / len(pieces))
        return jnp.repeat(jnp.exp(draws), dims[axis_at] // blocks).reshape((-1,) + (1,) * (len(dims) - axis_at - 1))

    loudness = one(*pieces[0])
    for cut in pieces[1:]:
        loudness = loudness * one(*cut)
    return loudness


def normal_values(rng, extent, width, limit, pieces=(), kind=jnp.bfloat16):
    loudness = block_levels(rng, extent, pieces, -0.22, 0.18) if pieces else 1.0
    values = jax.random.normal(rng, extent, jnp.float32) * width * loudness
    return jnp.minimum(jnp.maximum(values, -limit), limit).astype(kind)


def setup_inputs(seed: int = 0) -> dict:
    key_list = jax.random.split(jax.random.key(seed), 11)
    return {
        "trunk_input": normal_values(key_list[0], (WINDOWS, BINS, C), 1.0, 6.0, ((0, 4), (1, 32))),
        "tokens": plant(jax.random.randint(key_list[1], (WINDOWS, BINS), 0, 4), jax.random.fold_in(key_list[1], 1), 0, 3).astype(jnp.int32),
        "token_table": normal_values(key_list[2], (4, C), 0.5, 3.0, (), jnp.float32),
        "conv_weight": normal_values(key_list[3], (LAYERS, 3, C, M), (3 * C) ** -0.5, 0.125),
        "out_weight": normal_values(key_list[4], (LAYERS, M, C), M ** -0.5, 0.3125),
        "norm_gain": jnp.clip(1.0 + 0.18 * jax.random.normal(key_list[5], (LAYERS, C), jnp.float32), 0.1, 1.9),
        "mid_gain": jnp.clip(1.0 + 0.18 * jax.random.normal(key_list[6], (LAYERS, M), jnp.float32), 0.1, 1.9),
        "strand_perm": jax.random.permutation(key_list[7], C).astype(jnp.int32),
        "dilation": draw_dilation(jax.random.fold_in(key_list[10], 71), 0),
        "out_cotangent": normal_values(key_list[9], (WINDOWS, BINS, C), 1.0, 6.0, ((0, 4), (1, 32))),
    }


epsilon = 1e-05
precise = lax.Precision.HIGHEST

def normed_act(values, scaling):
    centre = lax.optimization_barrier(jnp.mean(values, axis=-1, keepdims=True))
    shifted = values - centre
    spread = lax.optimization_barrier(jnp.mean(shifted * shifted, axis=-1, keepdims=True))
    return jax.nn.gelu(shifted * lax.rsqrt(spread + epsilon) * scaling, approximate=False)

def matmul(left, right):
    flat = left.reshape(-1, left.shape[-1])
    product = jnp.dot(flat, right, preferred_element_type=jnp.float32)
    return product.reshape(left.shape[:-1] + (right.shape[-1],))

def matmul_t(left, right):
    flat = left.reshape(-1, left.shape[-1])
    product = lax.dot_general(flat, right, (((1,), (1,)), ((), ())), preferred_element_type=jnp.float32)
    return product.reshape(left.shape[:-1] + (right.shape[0],))

def outer_sum(left, right):
    flat_left = left.reshape(-1, left.shape[-1])
    flat_right = right.reshape(-1, right.shape[-1])
    return lax.dot_general(flat_left, flat_right, (((0,), (0,)), ((), ())), preferred_element_type=jnp.float32)

def settle(values):
    return lax.optimization_barrier(values.astype(jnp.bfloat16)).astype(jnp.float32)

def three_taps(padded, dilate, length):
    offset_low = (DMAX - dilate).astype(jnp.int32)
    offset_high = (DMAX + dilate).astype(jnp.int32)
    before = lax.dynamic_slice_in_dim(padded, offset_low, length, 1)
    centre = padded[:, DMAX:DMAX + length]
    behind = lax.dynamic_slice_in_dim(padded, offset_high, length, 1)
    return (before, centre, behind)

def widen(values):
    return jnp.pad(values, ((0, 0), (DMAX, DMAX), (0, 0)))

def front(hidden, scaling):
    return normed_act(hidden.astype(jnp.float32), scaling).astype(jnp.bfloat16)

def middle(padded, conv_w, dilate, length):
    before, centre, behind = three_taps(padded, dilate, length)
    return matmul(before, conv_w[0]) + matmul(centre, conv_w[1]) + matmul(behind, conv_w[2])

def finish(mid_values, out_w, mid_scale):
    squashed = normed_act(mid_values, mid_scale).astype(jnp.bfloat16)
    return matmul(squashed, out_w)

def grad_back(mid_values, cotangent, out_w, mid_scale):
    squashed, act_vjp = jax.vjp(normed_act, mid_values, mid_scale)
    rounded = squashed.astype(jnp.bfloat16)
    d_out_w = outer_sum(rounded, cotangent)
    d_squashed = matmul_t(cotangent, out_w)
    d_mid, d_mid_scale = act_vjp(d_squashed)
    return (d_mid.astype(jnp.bfloat16), d_out_w, d_mid_scale)

def grad_front(padded_u, padded_dm, conv_w, dilate, length, hidden, scaling):
    u_before, u_centre, u_behind = three_taps(padded_u, dilate, length)
    d_before, d_centre, d_behind = three_taps(padded_dm, dilate, length)
    d_conv = jnp.stack([outer_sum(u_before, d_centre), outer_sum(u_centre, d_centre), outer_sum(u_behind, d_centre)])
    d_front = matmul_t(d_behind, conv_w[0]) + matmul_t(d_centre, conv_w[1]) + matmul_t(d_before, conv_w[2])
    primal_out, front_vjp = jax.vjp(normed_act, hidden.astype(jnp.float32), scaling)
    d_hidden, d_scaling = front_vjp(d_front)
    return (d_hidden, d_conv, d_scaling)

def reverse_strand(values, strand_perm):
    return jnp.take(values[:, ::-1], strand_perm, axis=2)

def restore_strand(values, inverse):
    return jnp.take(values[:, ::-1], inverse, axis=2)

def embed(one_hot, token_table):
    flat = one_hot.reshape(-1, 4)
    product = jnp.dot(flat, token_table, precision=precise, preferred_element_type=jnp.float32)
    return product.reshape(one_hot.shape[:-1] + (token_table.shape[-1],))

def reference(trunk_input, tokens, token_table, conv_weight, out_weight, norm_gain, mid_gain, strand_perm, dilation, out_cotangent):
    channels = trunk_input.shape[2]
    length = trunk_input.shape[1]
    inverse = jnp.zeros((channels,), jnp.int32).at[strand_perm].set(jnp.arange(channels, dtype=jnp.int32))
    one_hot = (tokens[..., None] == jnp.arange(4, dtype=jnp.int32)).astype(jnp.float32)
    hidden = (trunk_input.astype(jnp.float32) + embed(one_hot, token_table)).astype(jnp.bfloat16)
    saved = []
    for block_index in range(LAYERS):
        dilate = dilation[block_index]
        other = reverse_strand(hidden, strand_perm)
        padded_a = widen(front(hidden, norm_gain[block_index]))
        padded_b = widen(front(other, norm_gain[block_index]))
        mid_a = middle(padded_a, conv_weight[block_index], dilate, length)
        mid_b = middle(padded_b, conv_weight[block_index], dilate, length)
        result_a = settle(finish(mid_a, out_weight[block_index], mid_gain[block_index]))
        rounded_b = lax.optimization_barrier(finish(mid_b, out_weight[block_index], mid_gain[block_index]).astype(jnp.bfloat16))
        returned_b = restore_strand(rounded_b, inverse).astype(jnp.float32)
        saved.append((hidden, other, padded_a, padded_b, mid_a, mid_b))
        hidden = (hidden.astype(jnp.float32) + 0.5 * (result_a + returned_b)).astype(jnp.bfloat16)
    block_output = hidden
    grad = out_cotangent
    conv_list = [None] * LAYERS
    out_list = [None] * LAYERS
    gain_list = [None] * LAYERS
    mid_list = [None] * LAYERS
    for block_index in reversed(range(LAYERS)):
        dilate = dilation[block_index]
        hidden_in, other, padded_a, padded_b, mid_a, mid_b = saved[block_index]
        cotangent = (0.5 * grad.astype(jnp.float32)).astype(jnp.bfloat16)
        cotangent_b = reverse_strand(cotangent, strand_perm)
        dm_a, dwo_a, dmg_a = grad_back(mid_a, cotangent, out_weight[block_index], mid_gain[block_index])
        dm_b, dwo_b, dmg_b = grad_back(mid_b, cotangent_b, out_weight[block_index], mid_gain[block_index])
        dh_a, dconv_a, dgain_a = grad_front(padded_a, widen(dm_a), conv_weight[block_index], dilate, length, hidden_in, norm_gain[block_index])
        dh_b, dconv_b, dgain_b = grad_front(padded_b, widen(dm_b), conv_weight[block_index], dilate, length, other, norm_gain[block_index])
        back_b = restore_strand(lax.optimization_barrier(dh_b.astype(jnp.bfloat16)), inverse).astype(jnp.float32)
        grad = (grad.astype(jnp.float32) + settle(dh_a) + back_b).astype(jnp.bfloat16)
        conv_list[block_index] = dconv_a + dconv_b
        out_list[block_index] = dwo_a + dwo_b
        gain_list[block_index] = dgain_a + dgain_b
        mid_list[block_index] = dmg_a + dmg_b
    flat_hot = one_hot.reshape(-1, 4)
    flat_grad = grad.reshape(-1, grad.shape[-1]).astype(jnp.float32)
    table_grad = lax.dot_general(flat_hot, flat_grad, (((0,), (0,)), ((), ())), precision=precise, preferred_element_type=jnp.float32)
    return (block_output, grad, table_grad, jnp.stack(conv_list), jnp.stack(out_list), jnp.stack(gain_list), jnp.stack(mid_list))
```

```python
import jax
import jax.numpy as jnp
from jax import lax
from jax.sharding import PartitionSpec as P

LAYERS = 2
DMAX = 64


epsilon = 1e-05
precise = lax.Precision.HIGHEST


def with_halo(block, sides, width):
    for axis, dim in sides:
        count = lax.axis_size(axis)
        forward = [(i, i + 1) for i in range(count - 1)]
        backward = [(target, source) for source, target in forward]
        low = lax.ppermute(
            lax.slice_in_dim(block, block.shape[dim] - width, None, axis=dim), axis, forward
        )
        high = lax.ppermute(lax.slice_in_dim(block, 0, width, axis=dim), axis, backward)
        block = jnp.concatenate([low, block, high], axis=dim)
    return block


def normed_act(values, scaling):
    centre = jnp.mean(values, axis=-1, keepdims=True)
    shifted = values - centre
    spread = jnp.mean(shifted * shifted, axis=-1, keepdims=True)
    return jax.nn.gelu(shifted * lax.rsqrt(spread + epsilon) * scaling, approximate=False)


def matmul(left, right):
    flat = left.reshape(-1, left.shape[-1])
    product = jnp.dot(flat, right, preferred_element_type=jnp.float32)
    return product.reshape(left.shape[:-1] + (right.shape[-1],))


def matmul_t(left, right):
    flat = left.reshape(-1, left.shape[-1])
    product = lax.dot_general(
        flat, right, (((1,), (1,)), ((), ())), preferred_element_type=jnp.float32
    )
    return product.reshape(left.shape[:-1] + (right.shape[0],))


def outer_sum(left, right):
    flat_left = left.reshape(-1, left.shape[-1])
    flat_right = right.reshape(-1, right.shape[-1])
    return lax.dot_general(
        flat_left, flat_right, (((0,), (0,)), ((), ())), preferred_element_type=jnp.float32
    )


def settle(values):
    return lax.optimization_barrier(values.astype(jnp.bfloat16)).astype(jnp.float32)


def three_taps(padded, dilate, length):
    offset_low = DMAX - dilate
    offset_high = DMAX + dilate
    before = lax.dynamic_slice_in_dim(padded, offset_low, length, 1)
    centre = padded[:, DMAX : DMAX + length]
    behind = lax.dynamic_slice_in_dim(padded, offset_high, length, 1)
    return (before, centre, behind)


def front(hidden, scaling):
    return normed_act(hidden.astype(jnp.float32), scaling).astype(jnp.bfloat16)


def halo_pair(front_pair):
    return with_halo(front_pair, (("ctx", 2),), DMAX)


def middle(padded, conv_w, dilate, length):
    before, centre, behind = three_taps(padded, dilate, length)
    return matmul(before, conv_w[0]) + matmul(centre, conv_w[1]) + matmul(behind, conv_w[2])


def finish(mid_values, out_w, mid_scale):
    squashed = normed_act(mid_values, mid_scale).astype(jnp.bfloat16)
    return matmul(squashed, out_w)


def grad_back(mid_values, cotangent, out_w, mid_scale):
    squashed, act_vjp = jax.vjp(normed_act, mid_values, mid_scale)
    rounded = squashed.astype(jnp.bfloat16)
    d_out_w = outer_sum(rounded, cotangent)
    d_squashed = matmul_t(cotangent, out_w)
    d_mid, d_mid_scale = act_vjp(d_squashed)
    return (d_mid.astype(jnp.bfloat16), d_out_w, d_mid_scale)


def grad_front(padded_u, padded_dm, conv_w, dilate, length, hidden, scaling):
    u_before, u_centre, u_behind = three_taps(padded_u, dilate, length)
    d_before, d_centre, d_behind = three_taps(padded_dm, dilate, length)
    d_conv = jnp.stack(
        [
            outer_sum(u_before, d_centre),
            outer_sum(u_centre, d_centre),
            outer_sum(u_behind, d_centre),
        ]
    )
    d_front = (
        matmul_t(d_behind, conv_w[0])
        + matmul_t(d_centre, conv_w[1])
        + matmul_t(d_before, conv_w[2])
    )
    primal_out, front_vjp = jax.vjp(normed_act, hidden.astype(jnp.float32), scaling)
    d_hidden, d_scaling = front_vjp(d_front)
    return (d_hidden, d_conv, d_scaling)


def channel_matrix(strand_perm):
    rows = jnp.arange(strand_perm.shape[0], dtype=jnp.int32)[:, None]
    return (rows == strand_perm[None, :]).astype(jnp.bfloat16)


def relabel(values, matrix):
    return matmul(values, matrix).astype(jnp.bfloat16)


def relabel_back(values, matrix):
    return matmul_t(values, matrix).astype(jnp.bfloat16)


def embed(one_hot, token_table):
    flat = one_hot.reshape(-1, 4)
    product = jnp.dot(flat, token_table, precision=precise, preferred_element_type=jnp.float32)
    return product.reshape(one_hot.shape[:-1] + (token_table.shape[-1],))


def table_term(one_hot, grad):
    flat_hot = one_hot.reshape(-1, 4)
    flat_grad = grad.reshape(-1, grad.shape[-1]).astype(jnp.float32)
    return lax.dot_general(
        flat_hot,
        flat_grad,
        (((0,), (0,)), ((), ())),
        precision=precise,
        preferred_element_type=jnp.float32,
    )


def shards(
    trunk_input,
    tokens,
    token_table,
    conv_weight,
    out_weight,
    norm_gain,
    mid_gain,
    strand_perm,
    dilation,
    out_cotangent,
):
    length = trunk_input.shape[1]
    matrix = channel_matrix(strand_perm)
    one_hot = (tokens[..., None] == jnp.arange(4, dtype=jnp.int32)).astype(jnp.float32)
    hidden = (trunk_input.astype(jnp.float32) + embed(one_hot, token_table)).astype(jnp.bfloat16)
    saved = []
    for block_index in range(LAYERS):
        dilate = dilation[block_index]
        conv_main = conv_weight[block_index]
        out_main = out_weight[block_index]
        gain_main = norm_gain[block_index]
        mid_scale = mid_gain[block_index]
        other = relabel(hidden, matrix)
        conv_other = conv_main[::-1]
        out_other = out_main
        gain_other = gain_main
        padded_pair = halo_pair(jnp.stack([front(hidden, gain_main), front(other, gain_other)]))
        mid_a = middle(padded_pair[0], conv_main, dilate, length)
        mid_b = middle(padded_pair[1], conv_other, dilate, length)
        result_a = settle(finish(mid_a, out_main, mid_scale))
        rounded_b = lax.optimization_barrier(
            finish(mid_b, out_other, mid_scale).astype(jnp.bfloat16)
        )
        returned_b = relabel_back(rounded_b, matrix).astype(jnp.float32)
        saved.append((hidden, other, padded_pair, mid_a, mid_b, conv_other, out_other, gain_other))
        hidden = (hidden.astype(jnp.float32) + 0.5 * (result_a + returned_b)).astype(jnp.bfloat16)
    grad = out_cotangent
    conv_list = [None] * LAYERS
    out_list = [None] * LAYERS
    gain_list = [None] * LAYERS
    mid_list = [None] * LAYERS
    table_total = None
    for block_index in reversed(range(LAYERS)):
        dilate = dilation[block_index]
        conv_main = conv_weight[block_index]
        out_main = out_weight[block_index]
        gain_main = norm_gain[block_index]
        mid_scale = mid_gain[block_index]
        hidden_in, other, padded_pair, mid_a, mid_b, conv_other, out_other, gain_other = saved[
            block_index
        ]
        cotangent = (0.5 * grad.astype(jnp.float32)).astype(jnp.bfloat16)
        cotangent_b = relabel(cotangent, matrix)
        dm_a, dwo_a, dmg_a = grad_back(mid_a, cotangent, out_main, mid_scale)
        dm_b, dwo_b, dmg_b = grad_back(mid_b, cotangent_b, out_other, mid_scale)
        dm_padded = with_halo(jnp.stack([dm_a, dm_b]), (("ctx", 2),), DMAX)
        dh_a, dconv_a, dgain_a = grad_front(
            padded_pair[0], dm_padded[0], conv_main, dilate, length, hidden_in, gain_main
        )
        dh_b, dconv_b, dgain_b = grad_front(
            padded_pair[1], dm_padded[1], conv_other, dilate, length, other, gain_other
        )
        back_b = relabel_back(
            lax.optimization_barrier(dh_b.astype(jnp.bfloat16)), matrix
        ).astype(jnp.float32)
        conv_local = dconv_a + dconv_b[::-1]
        out_local = dwo_a + dwo_b
        gain_local = dgain_a + dgain_b
        mid_local = dmg_a + dmg_b
        grad = (grad.astype(jnp.float32) + settle(dh_a) + back_b).astype(jnp.bfloat16)
        conv_list[block_index] = conv_local
        out_list[block_index] = out_local
        gain_list[block_index] = gain_local
        mid_list[block_index] = mid_local
    table_local = table_term(one_hot, grad)
    conv_total, out_total, gain_total, mid_total, table_total = lax.psum(
        (
            jnp.stack(conv_list),
            jnp.stack(out_list),
            jnp.stack(gain_list),
            jnp.stack(mid_list),
            table_local,
        ),
        ("dp", "ctx"),
    )
    return (hidden, grad, table_total, conv_total, out_total, gain_total, mid_total)


def solution(mesh):
    placed = (
        P("dp", "ctx", None),
        P("dp", "ctx"),
        P(),
        P(),
        P(),
        P(),
        P(),
        P(),
        P(),
        P("dp", "ctx", None),
    )
    return jax.shard_map(
        shards,
        mesh=mesh,
        in_specs=placed,
        out_specs=(P("dp", "ctx", None), P("dp", "ctx", None), P(), P(), P(), P(), P()),
        check_vma=False,
    )
```

```python
import jax
import jax.numpy as jnp
from jax import lax
from jax.experimental import pallas as pl
from jax.experimental.pallas import tpu as pltpu
from jax.sharding import PartitionSpec as P

LAYERS = 2
DMAX = 64

MESH = pl.DeviceIdType.MESH
GROWS = 3072
HALF = 1536
QUARTER = 384
EIGHTH = 96
SMALL = 16
LANES = 384


def place(core, y, z, x):
    return (lax.div(y, 2) * 2 + core, (lax.rem(y, 2) * 4 + z) * 4 + x)


def coordinates():
    dp = lax.axis_index("dp")
    ctx = lax.axis_index("ctx")
    y = lax.div(dp, 2) * 2 + lax.div(ctx, 16)
    return (lax.rem(dp, 2), y, lax.rem(lax.div(ctx, 4), 4), lax.rem(ctx, 4))


def ring_peer(spot, axis, distance):
    moved = list(spot)
    moved[axis] = lax.rem(spot[axis] + distance, 4)
    return place(*moved)


def core_peer(spot):
    return place(1 - spot[0], *spot[1:])


ORDERS = ((3, 1, 2), (1, 2, 3), (2, 3, 1))


class Copies:
    def __init__(self, send, recv):
        self.send, self.recv, self.open = send, recv, []

    def start(self, index, source, target, device):
        copy = pltpu.make_async_remote_copy(
            src_ref=source, dst_ref=target, send_sem=self.send.at[index],
            recv_sem=self.recv.at[index], device_id=device, device_id_type=MESH)
        copy.start()
        return copy


class Total:
    def __init__(self, spot, grads, result, core_in, sums0, in_a, sums1, in_b, sums2, in_c, send, recv):
        self.spot, self.grads, self.result = spot, grads, result
        self.core_in, self.sums0, self.in_a, self.sums1 = core_in, sums0, in_a, sums1
        self.in_b, self.sums2, self.in_c = in_b, sums2, in_c
        self.copies = Copies(send, recv)
        self.base = spot[0] * HALF

    def lanes(self, third):
        return pl.ds(third * 128, 128)

    def core_start(self):
        other = (1 - self.spot[0]) * HALF
        self.core = self.copies.start(0, self.grads.at[pl.ds(other, HALF)], self.core_in, core_peer(self.spot))

    def core_finish(self):
        self.core.wait()

        def body(step, carry):
            rows = pl.ds(pl.multiple_of(step * QUARTER, 32), QUARTER)
            mine = pl.ds(pl.multiple_of(self.base + step * QUARTER, 32), QUARTER)
            self.sums0[rows] = (self.grads[mine].astype(jnp.float32) + self.core_in[rows].astype(jnp.float32)).astype(jnp.bfloat16)
            return carry

        lax.fori_loop(0, 4, body, 0)

    def a_start(self):
        self.a = []
        for third, order in enumerate(ORDERS):
            for distance in (2, 1, 3):
                chunk = lax.rem(self.spot[order[0]] + distance, 4)
                self.a.append(self.copies.start(
                    1 + third * 3 + distance - 1,
                    self.sums0.at[pl.ds(chunk * QUARTER, QUARTER), self.lanes(third)],
                    self.in_a.at[third, distance - 1], ring_peer(self.spot, order[0], distance)))

    def a_finish(self):
        for copy in self.a:
            copy.wait()
        for third, order in enumerate(ORDERS):
            mine = pl.ds(pl.multiple_of(self.spot[order[0]] * QUARTER, 32), QUARTER)
            total = self.sums0[mine, self.lanes(third)].astype(jnp.float32)
            for slot in range(3):
                total = total + self.in_a[third, slot].astype(jnp.float32)
            self.sums1[third] = total.astype(jnp.bfloat16)

    def b_start(self):
        self.b = []
        for third, order in enumerate(ORDERS):
            for distance in (2, 1, 3):
                chunk = lax.rem(self.spot[order[1]] + distance, 4)
                self.b.append(self.copies.start(
                    10 + third * 3 + distance - 1,
                    self.sums1.at[third, pl.ds(chunk * EIGHTH, EIGHTH)],
                    self.in_b.at[third, distance - 1], ring_peer(self.spot, order[1], distance)))

    def b_finish(self):
        for copy in self.b:
            copy.wait()
        for third, order in enumerate(ORDERS):
            mine = pl.ds(pl.multiple_of(self.spot[order[1]] * EIGHTH, 32), EIGHTH)
            total = self.sums1[third, mine].astype(jnp.float32)
            for slot in range(3):
                total = total + self.in_b[third, slot].astype(jnp.float32)
            self.sums2[third] = total.astype(jnp.bfloat16)

    def c_start(self):
        self.c = []
        for third, order in enumerate(ORDERS):
            for distance in (2, 1, 3):
                self.c.append(self.copies.start(
                    19 + third * 3 + distance - 1, self.sums2.at[third],
                    self.in_c.at[third, self.spot[order[2]]], ring_peer(self.spot, order[2], distance)))
            self.in_c[third, self.spot[order[2]]] = self.sums2[third]

    def rows_of(self, third):
        order = ORDERS[third]
        quarter = self.base + self.spot[order[0]] * QUARTER
        return quarter, quarter + self.spot[order[1]] * EIGHTH

    def c_finish(self):
        for copy in self.c:
            copy.wait()
        for third in range(3):
            total = self.in_c[third, 0].astype(jnp.float32)
            for slot in range(1, 4):
                total = total + self.in_c[third, slot].astype(jnp.float32)
            _, eighth = self.rows_of(third)
            self.result[pl.ds(pl.multiple_of(eighth, 32), EIGHTH), self.lanes(third)] = total.astype(jnp.bfloat16)

    def gather_start(self, which):
        copies = []
        for third, order in enumerate(ORDERS):
            quarter, eighth = self.rows_of(third)
            rows = pl.ds(eighth, EIGHTH) if which else pl.ds(quarter, QUARTER)
            piece = self.result.at[rows, self.lanes(third)]
            for distance in (2, 1, 3):
                copies.append(self.copies.start(
                    28 + which * 9 + third * 3 + distance - 1, piece, piece, ring_peer(self.spot, order[which], distance)))
        return copies

    def last_start(self):
        piece = self.result.at[pl.ds(self.base, HALF)]
        return self.copies.start(46, piece, piece, core_peer(self.spot))


TOTAL_COPIES = 47


def total_scratch():
    return [
        pltpu.VMEM((HALF, LANES), jnp.bfloat16),
        pltpu.VMEM((HALF, LANES), jnp.bfloat16),
        pltpu.VMEM((3, 3, QUARTER, 128), jnp.bfloat16),
        pltpu.VMEM((3, QUARTER, 128), jnp.bfloat16),
        pltpu.VMEM((3, 3, EIGHTH, 128), jnp.bfloat16),
        pltpu.VMEM((3, EIGHTH, 128), jnp.bfloat16),
        pltpu.VMEM((3, 4, EIGHTH, 128), jnp.bfloat16),
        pltpu.SemaphoreType.DMA((TOTAL_COPIES,)),
        pltpu.SemaphoreType.DMA((TOTAL_COPIES,)),
    ]


class Small:
    def __init__(self, spot, value, core_in, ring_in, send, recv):
        self.spot, self.value, self.core_in, self.ring_in = spot, value, core_in, ring_in
        self.copies = Copies(send, recv)

    def core_start(self):
        self.core = self.copies.start(0, self.value, self.core_in, core_peer(self.spot))

    def core_finish(self):
        self.core.wait()
        own = self.spot[3]
        self.ring_in[0, own] = self.value[...] + self.core_in[...]

    def ring_start(self, stage):
        axis = (3, 1, 2)[stage]
        own = self.spot[axis]
        self.ring = [
            self.copies.start(1 + stage * 3 + distance - 1, self.ring_in.at[stage, own], self.ring_in.at[stage, own],
                              ring_peer(self.spot, axis, distance)) for distance in (2, 1, 3)]

    def ring_finish(self, stage):
        for copy in self.ring:
            copy.wait()
        total = self.ring_in[stage, 0] + self.ring_in[stage, 1] + self.ring_in[stage, 2] + self.ring_in[stage, 3]
        if stage < 2:
            self.ring_in[stage + 1, self.spot[(3, 1, 2)[stage + 1]]] = total
        return total


def small_scratch():
    return [
        pltpu.VMEM((SMALL, LANES), jnp.float32),
        pltpu.VMEM((3, 4, SMALL, LANES), jnp.float32),
        pltpu.SemaphoreType.DMA((10,)),
        pltpu.SemaphoreType.DMA((10,)),
    ]


def greet(spot, extra=()):
    barrier = pltpu.get_barrier_semaphore()
    peers = [core_peer(spot)] + [ring_peer(spot, axis, distance) for axis in (1, 2, 3) for distance in (1, 2, 3)]
    peers += list(extra)
    for peer in peers:
        pl.semaphore_signal(barrier, inc=1, device_id=peer, device_id_type=MESH)
    pl.semaphore_wait(barrier, len(peers))


def run_totals(totals, small, small_out):
    for t in totals:
        t.core_start()
    small.core_start()
    for t in totals:
        t.core_finish()
        t.a_start()
    small.core_finish()
    small.ring_start(0)
    for t in totals:
        t.a_finish()
        t.b_start()
    small.ring_finish(0)
    small.ring_start(1)
    for t in totals:
        t.b_finish()
        t.c_start()
    small.ring_finish(1)
    small.ring_start(2)
    after = []
    for t in totals:
        t.c_finish()
        after.append(t.gather_start(1))
    small_out[...] = small.ring_finish(2)
    late = []
    for t, copies in zip(totals, after):
        for copy in copies:
            copy.wait()
        late.append(t.gather_start(0))
    last = []
    for t, copies in zip(totals, late):
        for copy in copies:
            copy.wait()
        last.append(t.last_start())
    for copy in last:
        copy.wait()


def total_kernel(grads, value, result, small_out, *scratch):
    spot = coordinates()
    greet(spot)
    each = len(total_scratch())
    totals = [Total(spot, grads.at[b], result.at[b], *scratch[b * each:(b + 1) * each]) for b in range(2)]
    small = Small(spot, value, *scratch[2 * each:])
    run_totals(totals, small, small_out)


def all_totals(grads, value):
    whole = pl.BlockSpec(memory_space=pltpu.VMEM)
    return pl.pallas_call(
        total_kernel,
        out_shape=(jax.ShapeDtypeStruct((2, GROWS, LANES), jnp.bfloat16), jax.ShapeDtypeStruct((SMALL, LANES), jnp.float32)),
        in_specs=[whole, whole],
        out_specs=(whole, whole),
        scratch_shapes=total_scratch() * 2 + small_scratch(),
        compiler_params=pltpu.CompilerParams(collective_id=0, has_side_effects=True, vmem_limit_bytes=40 * 1024 * 1024),
        cost_estimate=pl.CostEstimate(flops=10**7, bytes_accessed=2 * 10**7, transcendentals=0),
        name="totals",
    )(grads, value)


def pack_grads(conv, out):
    parts = jnp.concatenate([conv.reshape(2, 2304, 384), out[:, :, :384], out[:, :, 384:]], axis=1)
    return parts.astype(jnp.bfloat16)


def unpack_grads(result):
    result = result.astype(jnp.float32)
    conv = result[:, :2304].reshape(2, 3, 768, 384)
    out = jnp.concatenate([result[:, 2304:2688], result[:, 2688:]], axis=2)
    return conv, out


def pack_small(table, gain, mid):
    flat = jnp.concatenate([table.reshape(8, 384), gain.reshape(4, 384), mid.reshape(2, 384), jnp.zeros((2, 384), jnp.float32)])
    return flat


def unpack_small(value):
    return value[:8].reshape(4, 768), value[8:12].reshape(2, 768), value[12:14]


epsilon = 1e-05
precise = lax.Precision.HIGHEST


def with_halo(block, sides, width):
    for axis, dim in sides:
        count = lax.axis_size(axis)
        forward = [(i, i + 1) for i in range(count - 1)]
        backward = [(target, source) for source, target in forward]
        low = lax.ppermute(
            lax.slice_in_dim(block, block.shape[dim] - width, None, axis=dim), axis, forward
        )
        high = lax.ppermute(lax.slice_in_dim(block, 0, width, axis=dim), axis, backward)
        block = jnp.concatenate([low, block, high], axis=dim)
    return block


def normed_act(values, scaling):
    centre = jnp.mean(values, axis=-1, keepdims=True)
    shifted = values - centre
    spread = jnp.mean(shifted * shifted, axis=-1, keepdims=True)
    return jax.nn.gelu(shifted * lax.rsqrt(spread + epsilon) * scaling, approximate=False)


def matmul(left, right):
    flat = left.reshape(-1, left.shape[-1])
    product = jnp.dot(flat, right, preferred_element_type=jnp.float32)
    return product.reshape(left.shape[:-1] + (right.shape[-1],))


def matmul_t(left, right):
    flat = left.reshape(-1, left.shape[-1])
    product = lax.dot_general(
        flat, right, (((1,), (1,)), ((), ())), preferred_element_type=jnp.float32
    )
    return product.reshape(left.shape[:-1] + (right.shape[0],))


def outer_sum(left, right):
    flat_left = left.reshape(-1, left.shape[-1])
    flat_right = right.reshape(-1, right.shape[-1])
    return lax.dot_general(
        flat_left, flat_right, (((0,), (0,)), ((), ())), preferred_element_type=jnp.float32
    )


def settle(values):
    return lax.optimization_barrier(values.astype(jnp.bfloat16)).astype(jnp.float32)


def three_taps(padded, dilate, length):
    offset_low = DMAX - dilate
    offset_high = DMAX + dilate
    before = lax.dynamic_slice_in_dim(padded, offset_low, length, 1)
    centre = padded[:, DMAX : DMAX + length]
    behind = lax.dynamic_slice_in_dim(padded, offset_high, length, 1)
    return (before, centre, behind)


def front(hidden, scaling):
    return normed_act(hidden.astype(jnp.float32), scaling).astype(jnp.bfloat16)


def halo_pair(front_pair):
    return with_halo(front_pair, (("ctx", 2),), DMAX)


def middle(padded, conv_w, dilate, length):
    before, centre, behind = three_taps(padded, dilate, length)
    return matmul(before, conv_w[0]) + matmul(centre, conv_w[1]) + matmul(behind, conv_w[2])


def finish(mid_values, out_w, mid_scale):
    squashed = normed_act(mid_values, mid_scale).astype(jnp.bfloat16)
    return matmul(squashed, out_w)


def grad_back(mid_values, cotangent, out_w, mid_scale):
    squashed, act_vjp = jax.vjp(normed_act, mid_values, mid_scale)
    rounded = squashed.astype(jnp.bfloat16)
    d_out_w = outer_sum(rounded, cotangent)
    d_squashed = matmul_t(cotangent, out_w)
    d_mid, d_mid_scale = act_vjp(d_squashed)
    return (d_mid.astype(jnp.bfloat16), d_out_w, d_mid_scale)


def grad_front(padded_u, padded_dm, conv_w, dilate, length, hidden, scaling):
    u_before, u_centre, u_behind = three_taps(padded_u, dilate, length)
    d_before, d_centre, d_behind = three_taps(padded_dm, dilate, length)
    d_conv = jnp.stack(
        [
            outer_sum(u_before, d_centre),
            outer_sum(u_centre, d_centre),
            outer_sum(u_behind, d_centre),
        ]
    )
    d_front = (
        matmul_t(d_behind, conv_w[0])
        + matmul_t(d_centre, conv_w[1])
        + matmul_t(d_before, conv_w[2])
    )
    primal_out, front_vjp = jax.vjp(normed_act, hidden.astype(jnp.float32), scaling)
    d_hidden, d_scaling = front_vjp(d_front)
    return (d_hidden, d_conv, d_scaling)


def channel_matrix(strand_perm):
    rows = jnp.arange(strand_perm.shape[0], dtype=jnp.int32)[:, None]
    return (rows == strand_perm[None, :]).astype(jnp.bfloat16)


def relabel(values, matrix):
    return matmul(values, matrix).astype(jnp.bfloat16)


def relabel_back(values, matrix):
    return matmul_t(values, matrix).astype(jnp.bfloat16)


def embed(one_hot, token_table):
    flat = one_hot.reshape(-1, 4)
    product = jnp.dot(flat, token_table, precision=precise, preferred_element_type=jnp.float32)
    return product.reshape(one_hot.shape[:-1] + (token_table.shape[-1],))


def table_term(one_hot, grad):
    flat_hot = one_hot.reshape(-1, 4)
    flat_grad = grad.reshape(-1, grad.shape[-1]).astype(jnp.float32)
    return lax.dot_general(
        flat_hot,
        flat_grad,
        (((0,), (0,)), ((), ())),
        precision=precise,
        preferred_element_type=jnp.float32,
    )


def shards(
    trunk_input,
    tokens,
    token_table,
    conv_weight,
    out_weight,
    norm_gain,
    mid_gain,
    strand_perm,
    dilation,
    out_cotangent,
):
    length = trunk_input.shape[1]
    matrix = channel_matrix(strand_perm)
    one_hot = (tokens[..., None] == jnp.arange(4, dtype=jnp.int32)).astype(jnp.float32)
    hidden = (trunk_input.astype(jnp.float32) + embed(one_hot, token_table)).astype(jnp.bfloat16)
    saved = []
    for block_index in range(LAYERS):
        dilate = dilation[block_index]
        conv_main = conv_weight[block_index]
        out_main = out_weight[block_index]
        gain_main = norm_gain[block_index]
        mid_scale = mid_gain[block_index]
        other = relabel(hidden, matrix)
        conv_other = conv_main[::-1]
        out_other = out_main
        gain_other = gain_main
        padded_pair = halo_pair(jnp.stack([front(hidden, gain_main), front(other, gain_other)]))
        mid_a = middle(padded_pair[0], conv_main, dilate, length)
        mid_b = middle(padded_pair[1], conv_other, dilate, length)
        result_a = settle(finish(mid_a, out_main, mid_scale))
        rounded_b = lax.optimization_barrier(
            finish(mid_b, out_other, mid_scale).astype(jnp.bfloat16)
        )
        returned_b = relabel_back(rounded_b, matrix).astype(jnp.float32)
        saved.append((hidden, other, padded_pair, mid_a, mid_b, conv_other, out_other, gain_other))
        hidden = (hidden.astype(jnp.float32) + 0.5 * (result_a + returned_b)).astype(jnp.bfloat16)
    grad = out_cotangent
    conv_list = [None] * LAYERS
    out_list = [None] * LAYERS
    gain_list = [None] * LAYERS
    mid_list = [None] * LAYERS
    table_total = None
    for block_index in reversed(range(LAYERS)):
        dilate = dilation[block_index]
        conv_main = conv_weight[block_index]
        out_main = out_weight[block_index]
        gain_main = norm_gain[block_index]
        mid_scale = mid_gain[block_index]
        hidden_in, other, padded_pair, mid_a, mid_b, conv_other, out_other, gain_other = saved[
            block_index
        ]
        cotangent = (0.5 * grad.astype(jnp.float32)).astype(jnp.bfloat16)
        cotangent_b = relabel(cotangent, matrix)
        dm_a, dwo_a, dmg_a = grad_back(mid_a, cotangent, out_main, mid_scale)
        dm_b, dwo_b, dmg_b = grad_back(mid_b, cotangent_b, out_other, mid_scale)
        dm_padded = with_halo(jnp.stack([dm_a, dm_b]), (("ctx", 2),), DMAX)
        dh_a, dconv_a, dgain_a = grad_front(
            padded_pair[0], dm_padded[0], conv_main, dilate, length, hidden_in, gain_main
        )
        dh_b, dconv_b, dgain_b = grad_front(
            padded_pair[1], dm_padded[1], conv_other, dilate, length, other, gain_other
        )
        back_b = relabel_back(
            lax.optimization_barrier(dh_b.astype(jnp.bfloat16)), matrix
        ).astype(jnp.float32)
        conv_local = dconv_a + dconv_b[::-1]
        out_local = dwo_a + dwo_b
        gain_local = dgain_a + dgain_b
        mid_local = dmg_a + dmg_b
        grad = (grad.astype(jnp.float32) + settle(dh_a) + back_b).astype(jnp.bfloat16)
        conv_list[block_index] = conv_local
        out_list[block_index] = out_local
        gain_list[block_index] = gain_local
        mid_list[block_index] = mid_local
    table_local = table_term(one_hot, grad)
    result, small = all_totals(
        pack_grads(jnp.stack(conv_list), jnp.stack(out_list)),
        pack_small(table_local, jnp.stack(gain_list), jnp.stack(mid_list)),
    )
    conv_total, out_total = unpack_grads(result)
    table_total, gain_total, mid_total = unpack_small(small)
    return (hidden, grad, table_total, conv_total, out_total, gain_total, mid_total)


def solution(mesh):
    placed = (
        P("dp", "ctx", None),
        P("dp", "ctx"),
        P(),
        P(),
        P(),
        P(),
        P(),
        P(),
        P(),
        P("dp", "ctx", None),
    )
    return jax.shard_map(
        shards,
        mesh=mesh,
        in_specs=placed,
        out_specs=(P("dp", "ctx", None), P("dp", "ctx", None), P(), P(), P(), P(), P()),
        check_vma=False,
    )
```

```python
import jax
import jax.numpy as jnp
from jax import lax
from jax.experimental import pallas as pl
from jax.experimental.pallas import tpu as pltpu
from jax.sharding import PartitionSpec as P

LAYERS = 2
DMAX = 64

MESH = pl.DeviceIdType.MESH
GROWS = 3072
HALF = 1536
QUARTER = 384
EIGHTH = 96
SMALL = 16
LANES = 384


def place(core, y, z, x):
    return (lax.div(y, 2) * 2 + core, (lax.rem(y, 2) * 4 + z) * 4 + x)


def coordinates():
    dp = lax.axis_index("dp")
    ctx = lax.axis_index("ctx")
    y = lax.div(dp, 2) * 2 + lax.div(ctx, 16)
    return (lax.rem(dp, 2), y, lax.rem(lax.div(ctx, 4), 4), lax.rem(ctx, 4))


def ring_peer(spot, axis, distance):
    moved = list(spot)
    moved[axis] = lax.rem(spot[axis] + distance, 4)
    return place(*moved)


def core_peer(spot):
    return place(1 - spot[0], *spot[1:])


ORDERS = ((3, 1, 2), (1, 2, 3), (2, 3, 1))


class Copies:
    def __init__(self, send, recv):
        self.send, self.recv, self.open = send, recv, []

    def start(self, index, source, target, device):
        copy = pltpu.make_async_remote_copy(
            src_ref=source, dst_ref=target, send_sem=self.send.at[index],
            recv_sem=self.recv.at[index], device_id=device, device_id_type=MESH)
        copy.start()
        return copy


class Total:
    def __init__(self, spot, grads, result, core_in, sums0, in_a, sums1, in_b, sums2, in_c, send, recv):
        self.spot, self.grads, self.result = spot, grads, result
        self.core_in, self.sums0, self.in_a, self.sums1 = core_in, sums0, in_a, sums1
        self.in_b, self.sums2, self.in_c = in_b, sums2, in_c
        self.copies = Copies(send, recv)
        self.base = spot[0] * HALF

    def lanes(self, third):
        return pl.ds(third * 128, 128)

    def core_start(self):
        other = (1 - self.spot[0]) * HALF
        self.core = self.copies.start(0, self.grads.at[pl.ds(other, HALF)], self.core_in, core_peer(self.spot))

    def core_finish(self):
        self.core.wait()

        def body(step, carry):
            rows = pl.ds(pl.multiple_of(step * QUARTER, 32), QUARTER)
            mine = pl.ds(pl.multiple_of(self.base + step * QUARTER, 32), QUARTER)
            self.sums0[rows] = (self.grads[mine].astype(jnp.float32) + self.core_in[rows].astype(jnp.float32)).astype(jnp.bfloat16)
            return carry

        lax.fori_loop(0, 4, body, 0)

    def a_start(self):
        self.a = []
        for third, order in enumerate(ORDERS):
            for distance in (2, 1, 3):
                chunk = lax.rem(self.spot[order[0]] + distance, 4)
                self.a.append(self.copies.start(
                    1 + third * 3 + distance - 1,
                    self.sums0.at[pl.ds(chunk * QUARTER, QUARTER), self.lanes(third)],
                    self.in_a.at[third, distance - 1], ring_peer(self.spot, order[0], distance)))

    def a_finish(self):
        for copy in self.a:
            copy.wait()
        for third, order in enumerate(ORDERS):
            mine = pl.ds(pl.multiple_of(self.spot[order[0]] * QUARTER, 32), QUARTER)
            total = self.sums0[mine, self.lanes(third)].astype(jnp.float32)
            for slot in range(3):
                total = total + self.in_a[third, slot].astype(jnp.float32)
            self.sums1[third] = total.astype(jnp.bfloat16)

    def b_start(self):
        self.b = []
        for third, order in enumerate(ORDERS):
            for distance in (2, 1, 3):
                chunk = lax.rem(self.spot[order[1]] + distance, 4)
                self.b.append(self.copies.start(
                    10 + third * 3 + distance - 1,
                    self.sums1.at[third, pl.ds(chunk * EIGHTH, EIGHTH)],
                    self.in_b.at[third, distance - 1], ring_peer(self.spot, order[1], distance)))

    def b_finish(self):
        for copy in self.b:
            copy.wait()
        for third, order in enumerate(ORDERS):
            mine = pl.ds(pl.multiple_of(self.spot[order[1]] * EIGHTH, 32), EIGHTH)
            total = self.sums1[third, mine].astype(jnp.float32)
            for slot in range(3):
                total = total + self.in_b[third, slot].astype(jnp.float32)
            self.sums2[third] = total.astype(jnp.bfloat16)

    def c_start(self):
        self.c = []
        for third, order in enumerate(ORDERS):
            for distance in (2, 1, 3):
                self.c.append(self.copies.start(
                    19 + third * 3 + distance - 1, self.sums2.at[third],
                    self.in_c.at[third, self.spot[order[2]]], ring_peer(self.spot, order[2], distance)))
            self.in_c[third, self.spot[order[2]]] = self.sums2[third]

    def rows_of(self, third):
        order = ORDERS[third]
        quarter = self.base + self.spot[order[0]] * QUARTER
        return quarter, quarter + self.spot[order[1]] * EIGHTH

    def c_finish(self):
        for copy in self.c:
            copy.wait()
        for third in range(3):
            total = self.in_c[third, 0].astype(jnp.float32)
            for slot in range(1, 4):
                total = total + self.in_c[third, slot].astype(jnp.float32)
            _, eighth = self.rows_of(third)
            self.result[pl.ds(pl.multiple_of(eighth, 32), EIGHTH), self.lanes(third)] = total.astype(jnp.bfloat16)

    def gather_start(self, which):
        copies = []
        for third, order in enumerate(ORDERS):
            quarter, eighth = self.rows_of(third)
            rows = pl.ds(eighth, EIGHTH) if which else pl.ds(quarter, QUARTER)
            piece = self.result.at[rows, self.lanes(third)]
            for distance in (2, 1, 3):
                copies.append(self.copies.start(
                    28 + which * 9 + third * 3 + distance - 1, piece, piece, ring_peer(self.spot, order[which], distance)))
        return copies

    def last_start(self):
        piece = self.result.at[pl.ds(self.base, HALF)]
        return self.copies.start(46, piece, piece, core_peer(self.spot))


TOTAL_COPIES = 47


def total_scratch():
    return [
        pltpu.VMEM((HALF, LANES), jnp.bfloat16),
        pltpu.VMEM((HALF, LANES), jnp.bfloat16),
        pltpu.VMEM((3, 3, QUARTER, 128), jnp.bfloat16),
        pltpu.VMEM((3, QUARTER, 128), jnp.bfloat16),
        pltpu.VMEM((3, 3, EIGHTH, 128), jnp.bfloat16),
        pltpu.VMEM((3, EIGHTH, 128), jnp.bfloat16),
        pltpu.VMEM((3, 4, EIGHTH, 128), jnp.bfloat16),
        pltpu.SemaphoreType.DMA((TOTAL_COPIES,)),
        pltpu.SemaphoreType.DMA((TOTAL_COPIES,)),
    ]


class Small:
    def __init__(self, spot, value, core_in, ring_in, send, recv):
        self.spot, self.value, self.core_in, self.ring_in = spot, value, core_in, ring_in
        self.copies = Copies(send, recv)

    def core_start(self):
        self.core = self.copies.start(0, self.value, self.core_in, core_peer(self.spot))

    def core_finish(self):
        self.core.wait()
        own = self.spot[3]
        self.ring_in[0, own] = self.value[...] + self.core_in[...]

    def ring_start(self, stage):
        axis = (3, 1, 2)[stage]
        own = self.spot[axis]
        self.ring = [
            self.copies.start(1 + stage * 3 + distance - 1, self.ring_in.at[stage, own], self.ring_in.at[stage, own],
                              ring_peer(self.spot, axis, distance)) for distance in (2, 1, 3)]

    def ring_finish(self, stage):
        for copy in self.ring:
            copy.wait()
        total = self.ring_in[stage, 0] + self.ring_in[stage, 1] + self.ring_in[stage, 2] + self.ring_in[stage, 3]
        if stage < 2:
            self.ring_in[stage + 1, self.spot[(3, 1, 2)[stage + 1]]] = total
        return total


def small_scratch():
    return [
        pltpu.VMEM((SMALL, LANES), jnp.float32),
        pltpu.VMEM((3, 4, SMALL, LANES), jnp.float32),
        pltpu.SemaphoreType.DMA((10,)),
        pltpu.SemaphoreType.DMA((10,)),
    ]


def greet(spot, extra=()):
    barrier = pltpu.get_barrier_semaphore()
    peers = [core_peer(spot)] + [ring_peer(spot, axis, distance) for axis in (1, 2, 3) for distance in (1, 2, 3)]
    peers += list(extra)
    for peer in peers:
        pl.semaphore_signal(barrier, inc=1, device_id=peer, device_id_type=MESH)
    pl.semaphore_wait(barrier, len(peers))


epsilon = 1e-05
OWN = 256
WIDE = OWN + 2 * DMAX
CH = 768
MID = 384
TILE = 32
BF = jnp.bfloat16
F32 = jnp.float32


def dot(left, right):
    return jnp.dot(left, right, preferred_element_type=F32)


def dot_t(left, right):
    return lax.dot_general(left, right, (((1,), (1,)), ((), ())), preferred_element_type=F32)


def dot_rows(left, right):
    return lax.dot_general(left, right, (((0,), (0,)), ((), ())), preferred_element_type=F32)


def strand(s, width=CH):
    return pl.ds(s * width, width)


def loop(count, body):
    def step(index, carry):
        body(index)
        return carry

    lax.fori_loop(0, count, step, 0)


def tile_at(index, base=0, size=TILE):
    return pl.ds(pl.multiple_of(base + index * size, size), size)


def standard(values):
    centre = jnp.mean(values, axis=-1, keepdims=True)
    shifted = values - centre
    scale = lax.rsqrt(jnp.mean(shifted * shifted, axis=-1, keepdims=True) + epsilon)
    return shifted * scale, centre, scale


def gelu_pair(z):
    below = 0.5 + 0.5 * lax.erf(z * 0.7071067811865476)
    return z * below, below + z * (0.3989422804014327 * jnp.exp(-0.5 * z * z))


def norm_back(dz, hat, scale, gain):
    dhat = dz * gain
    return scale * (
        dhat - jnp.mean(dhat, axis=-1, keepdims=True) - hat * jnp.mean(dhat * hat, axis=-1, keepdims=True)
    )


def fold(values):
    return values.reshape(TILE // 8, 8, values.shape[-1]).sum(axis=0)


def step_kernel(
    dilation, trunk, tokens, table, norm_gain, mid_gain, perm, cotangent, conv_hbm, out_hbm,
    block_out, trunk_grad, result, small_out,
    conv_w, out_w, matrix, move, hidden, relabelled, u_pad, u_low, u_high, hat, slope, scale, mid,
    mid_hat, mid_slope, mid_scale, q, wide, back, rounded, e, dm_pad, dm_low, dm_high, grad, gain_acc, mid_acc,
    weight_sem, halo_send, halo_recv, grads, *scratch,
):
    spot = coordinates()
    dp = lax.axis_index("dp")
    ctx = lax.axis_index("ctx")
    left = (dp, lax.rem(ctx + 31, 32))
    right = (dp, lax.rem(ctx + 1, 32))
    first_bin = jnp.where(ctx == 0, DMAX, 0)
    end_bin = jnp.where(ctx == 31, DMAX + OWN, WIDE)
    weights = [
        pltpu.make_async_copy(conv_hbm, conv_w, weight_sem.at[0]),
        pltpu.make_async_copy(out_hbm, out_w, weight_sem.at[1]),
    ]
    for copy in weights:
        copy.start()
    each = len(total_scratch())
    totals = [Total(spot, grads.at[b], result.at[b], *scratch[b * each:(b + 1) * each]) for b in range(LAYERS)]
    small = Small(spot, *scratch[2 * each:])
    halos = Copies(halo_send, halo_recv)

    def trade(index, mine):
        return [
            halos.start(2 * index, mine.at[pl.ds(DMAX, DMAX)], mine.at[pl.ds(DMAX + OWN, DMAX)], left),
            halos.start(2 * index + 1, mine.at[pl.ds(OWN, DMAX)], mine.at[pl.ds(0, DMAX)], right),
        ]

    one_hot = (tokens[...] == lax.broadcasted_iota(jnp.int32, (8, OWN), 0)).astype(F32)
    added = lax.dot_general(one_hot, table[...], (((0,), (0,)), ((), ())), precision=lax.Precision.HIGHEST, preferred_element_type=F32)
    hidden[0, pl.ds(DMAX, OWN)] = (trunk[...].astype(F32) + added).astype(BF)
    greet(spot, (left, right))
    pending = trade(0, hidden.at[0])

    def fill_matrix(index):
        rows = tile_at(index)
        channel = lax.broadcasted_iota(jnp.int32, (TILE, CH), 0) + index * TILE
        matrix[rows] = jnp.where(channel == perm[...], 1.0, 0.0).astype(BF)

    loop(CH // TILE, fill_matrix)
    bin_from = lax.broadcasted_iota(jnp.int32, (OWN, WIDE), 1)
    bin_to = lax.broadcasted_iota(jnp.int32, (OWN, WIDE), 0) + DMAX
    inside = (bin_from >= first_bin) & (bin_from < end_bin)
    for b in range(LAYERS):
        for way in range(2):
            at = bin_to + (2 * way - 1) * dilation[b]
            move[b, way] = jnp.where(inside & (bin_from == at), 1.0, 0.0).astype(BF)
    e[pl.ds(0, OWN)] = (0.5 * cotangent[...].astype(F32)).astype(BF)

    for b in range(LAYERS):
        gain = norm_gain[pl.ds(b, 1)]
        mid_s = mid_gain[pl.ds(b, 1)]

        def front(rows, own):
            x = hidden[b, rows].astype(F32)
            hat_f, centre, inv = standard(x)
            hat_r = (relabelled[rows] - centre) * inv
            for s, normed in enumerate((hat_f, hat_r)):
                u, du = gelu_pair(normed * gain)
                u_pad[b, rows, strand(s)] = u.astype(BF)
                if own is not None:
                    hat[b, s, own] = normed
                    slope[b, s, own] = du
            if own is not None:
                scale[b, own] = jnp.broadcast_to(inv, (TILE, 128))

        relabelled[pl.ds(DMAX, OWN)] = dot(hidden[b, pl.ds(DMAX, OWN)], matrix[...])
        loop(OWN // TILE, lambda i: front(tile_at(i, DMAX), tile_at(i)))
        if b == 0:
            for copy in weights:
                copy.wait()
        for s in range(2):
            mid[s] = dot(u_pad[b, pl.ds(DMAX, OWN), strand(s)], conv_w[b, 1])
        for copy in pending:
            copy.wait()
        for base in (0, DMAX + OWN):
            relabelled[pl.ds(base, DMAX)] = dot(hidden[b, pl.ds(base, DMAX)], matrix[...])
            loop(DMAX // TILE, lambda i: front(tile_at(i, base), None))

        for s in range(2):
            u_low[s] = dot(move[b, s], u_pad[b, :, strand(s)]).astype(BF)
            u_high[s] = dot(move[b, 1 - s], u_pad[b, :, strand(s)]).astype(BF)
        for s in range(2):
            mid[s] += dot(u_low[s], conv_w[b, 0]) + dot(u_high[s], conv_w[b, 2])

        def middle(i):
            rows = tile_at(i)
            for s in range(2):
                normed, _, inv = standard(mid[s, rows])
                value, derivative = gelu_pair(normed * mid_s)
                q[b, s, rows] = value.astype(BF)
                mid_hat[b, s, rows] = normed
                mid_slope[b, s, rows] = derivative
                mid_scale[b, s, rows] = jnp.broadcast_to(inv, (TILE, 128))

        loop(OWN // TILE, middle)
        rounded[...] = dot(q[b, 1], out_w[b]).astype(BF)
        wide[0] = dot(q[b, 0], out_w[b])
        back[...] = dot_t(rounded[...], matrix[...])

        def join(i):
            rows = tile_at(i)
            total = wide[0, rows].astype(BF).astype(F32) + back[rows]
            following = (hidden[b, tile_at(i, DMAX)].astype(F32) + 0.5 * total).astype(BF)
            if b + 1 < LAYERS:
                hidden[b + 1, tile_at(i, DMAX)] = following
            else:
                block_out[rows] = following

        loop(OWN // TILE, join)
        if b + 1 < LAYERS:
            pending = trade(b + 1, hidden.at[b + 1])

    grad[...] = cotangent[...]
    gain_acc[...] = jnp.zeros_like(gain_acc)
    mid_acc[...] = jnp.zeros_like(mid_acc)
    for b in (1, 0):
        gain = norm_gain[pl.ds(b, 1)]
        mid_s = mid_gain[pl.ds(b, 1)]
        sums = grads.at[b]
        if b == 0:
            e[pl.ds(0, OWN)] = (0.5 * grad[...].astype(F32)).astype(BF)
        e[pl.ds(OWN, OWN)] = dot(e[pl.ds(0, OWN)], matrix[...]).astype(BF)
        for s in range(2):
            mid[s] = dot_t(e[pl.ds(s * OWN, OWN)], out_w[b])

        def middle_back(i):
            rows = tile_at(i)
            total = jnp.zeros((8, MID), F32)
            for s in range(2):
                dz = mid[s, rows] * mid_slope[b, s, rows]
                normed = mid_hat[b, s, rows]
                total = total + fold(dz * normed)
                dm = norm_back(dz, normed, mid_scale[b, s, rows, 0:1], mid_s)
                dm_pad[b, tile_at(i, DMAX), strand(s, MID)] = dm.astype(BF)
            mid_acc[b] += total

        loop(OWN // TILE, middle_back)
        pending = trade(LAYERS + b, dm_pad.at[b])
        if b == 0:
            totals[1].a_finish()
            totals[1].b_start()
        q_all = q[b].reshape(2 * OWN, MID)
        out_grad = dot_rows(q_all, e[...])
        sums[pl.ds(2304, MID)] = out_grad[:, :MID].astype(BF)
        sums[pl.ds(2688, MID)] = out_grad[:, MID:].astype(BF)
        own = pl.ds(DMAX, OWN)
        u_all = jnp.concatenate([u_pad[b, own, strand(s)] for s in range(2)], axis=0)
        dm_all = jnp.concatenate([dm_pad[b, own, strand(s, MID)] for s in range(2)], axis=0)
        sums[pl.ds(CH, CH)] = dot_rows(u_all, dm_all).astype(BF)
        for s in range(2):
            wide[s] = dot_t(dm_pad[b, own, strand(s, MID)], conv_w[b, 1])
        for copy in pending:
            copy.wait()
        for s in range(2):
            dm_low[s] = dot(move[b, 1 - s], dm_pad[b, :, strand(s, MID)]).astype(BF)
            dm_high[s] = dot(move[b, s], dm_pad[b, :, strand(s, MID)]).astype(BF)
        sums[pl.ds(0, CH)] = dot_rows(u_all, dm_low[...].reshape(2 * OWN, MID)).astype(BF)
        sums[pl.ds(2 * CH, CH)] = dot_rows(u_all, dm_high[...].reshape(2 * OWN, MID)).astype(BF)
        totals[b].core_start()
        if b == 0:
            totals[1].b_finish()
            totals[1].c_start()
        for s in range(2):
            wide[s] += dot_t(dm_low[s], conv_w[b, 0]) + dot_t(dm_high[s], conv_w[b, 2])

        def front_back(i):
            rows = tile_at(i)
            total = jnp.zeros((8, CH), F32)
            for s in range(2):
                dz = wide[s, rows] * slope[b, s, rows]
                normed = hat[b, s, rows]
                total = total + fold(dz * normed)
                dx = norm_back(dz, normed, scale[b, rows, 0:1], gain)
                if s == 0:
                    wide[0, rows] = dx
                else:
                    rounded[rows] = dx.astype(BF)
            gain_acc[b] += total

        loop(OWN // TILE, front_back)
        back[...] = dot_t(rounded[...], matrix[...])

        def join_back(i):
            rows = tile_at(i)
            total = grad[rows].astype(F32) + wide[0, rows].astype(BF).astype(F32) + back[rows]
            grad[rows] = total.astype(BF)

        loop(OWN // TILE, join_back)
        totals[b].core_finish()
        totals[b].a_start()

    trunk_grad[...] = grad[...]
    table_term = dot(one_hot.astype(BF), grad[...])
    small.value[pl.ds(0, 4)] = table_term[0:4, :MID]
    small.value[pl.ds(4, 4)] = table_term[0:4, MID:]
    for b in range(LAYERS):
        term = jnp.sum(gain_acc[b], axis=0, keepdims=True)
        small.value[pl.ds(8 + 2 * b, 1)] = term[:, :MID]
        small.value[pl.ds(9 + 2 * b, 1)] = term[:, MID:]
        small.value[pl.ds(12 + b, 1)] = jnp.sum(mid_acc[b], axis=0, keepdims=True)
    small.value[pl.ds(14, 2)] = jnp.zeros((2, MID), F32)
    small.core_start()
    totals[1].c_finish()
    first = totals[1].gather_start(1)
    small.core_finish()
    small.ring_start(0)
    totals[0].a_finish()
    totals[0].b_start()
    for copy in first:
        copy.wait()
    first = totals[1].gather_start(0)
    small.ring_finish(0)
    small.ring_start(1)
    totals[0].b_finish()
    totals[0].c_start()
    small.ring_finish(1)
    small.ring_start(2)
    totals[0].c_finish()
    second = totals[0].gather_start(1)
    for copy in first:
        copy.wait()
    first = totals[1].last_start()
    small_out[...] = small.ring_finish(2)
    for copy in second:
        copy.wait()
    second = totals[0].gather_start(0)
    first.wait()
    for copy in second:
        copy.wait()
    totals[0].last_start().wait()


def whole_step(trunk, tokens, table, conv_w, out_w, norm_gain, mid_gain, perm, dilation, cotangent):
    vmem = pl.BlockSpec(memory_space=pltpu.VMEM)
    stay = pl.BlockSpec(memory_space=pl.ANY)
    smem = pl.BlockSpec(memory_space=pltpu.SMEM)
    scratch = [
        pltpu.VMEM((LAYERS, 3, CH, MID), BF),
        pltpu.VMEM((LAYERS, MID, CH), BF),
        pltpu.VMEM((CH, CH), BF),
        pltpu.VMEM((LAYERS, 2, OWN, WIDE), BF),
        pltpu.VMEM((LAYERS, WIDE, CH), BF),
        pltpu.VMEM((WIDE, CH), F32),
        pltpu.VMEM((LAYERS, WIDE, 2 * CH), BF),
        pltpu.VMEM((2, OWN, CH), BF),
        pltpu.VMEM((2, OWN, CH), BF),
        pltpu.VMEM((LAYERS, 2, OWN, CH), F32),
        pltpu.VMEM((LAYERS, 2, OWN, CH), F32),
        pltpu.VMEM((LAYERS, OWN, 128), F32),
        pltpu.VMEM((2, OWN, MID), F32),
        pltpu.VMEM((LAYERS, 2, OWN, MID), F32),
        pltpu.VMEM((LAYERS, 2, OWN, MID), F32),
        pltpu.VMEM((LAYERS, 2, OWN, 128), F32),
        pltpu.VMEM((LAYERS, 2, OWN, MID), BF),
        pltpu.VMEM((2, OWN, CH), F32),
        pltpu.VMEM((OWN, CH), F32),
        pltpu.VMEM((OWN, CH), BF),
        pltpu.VMEM((2 * OWN, CH), BF),
        pltpu.VMEM((LAYERS, WIDE, 2 * MID), BF),
        pltpu.VMEM((2, OWN, MID), BF),
        pltpu.VMEM((2, OWN, MID), BF),
        pltpu.VMEM((OWN, CH), BF),
        pltpu.VMEM((LAYERS, 8, CH), F32),
        pltpu.VMEM((LAYERS, 8, MID), F32),
        pltpu.SemaphoreType.DMA((2,)),
        pltpu.SemaphoreType.DMA((8,)),
        pltpu.SemaphoreType.DMA((8,)),
        pltpu.VMEM((LAYERS, GROWS, LANES), BF),
    ]
    small = [pltpu.VMEM((SMALL, LANES), F32)] + small_scratch()
    return pl.pallas_call(
        step_kernel,
        out_shape=(
            jax.ShapeDtypeStruct((OWN, CH), BF),
            jax.ShapeDtypeStruct((OWN, CH), BF),
            jax.ShapeDtypeStruct((LAYERS, GROWS, LANES), BF),
            jax.ShapeDtypeStruct((SMALL, LANES), F32),
        ),
        in_specs=[smem] + [vmem] * 7 + [stay] * 2,
        out_specs=(vmem,) * 4,
        scratch_shapes=scratch + total_scratch() * 2 + small,
        compiler_params=pltpu.CompilerParams(collective_id=0, has_side_effects=True, vmem_limit_bytes=56 * 1024 * 1024),
        cost_estimate=pl.CostEstimate(flops=10**10, bytes_accessed=2 * 10**7, transcendentals=0),
        name="step",
    )(dilation, trunk, tokens, table, norm_gain, mid_gain, perm, cotangent, conv_w, out_w)


def unpack_grads(result):
    result = result.astype(F32)
    conv = result[:, :2304].reshape(LAYERS, 3, CH, MID)
    out = jnp.concatenate([result[:, 2304:2688], result[:, 2688:]], axis=2)
    return conv, out


def shards(trunk_input, tokens, token_table, conv_weight, out_weight, norm_gain, mid_gain, strand_perm, dilation, out_cotangent):
    table = jnp.pad(token_table, ((0, 4), (0, 0)))
    block_out, trunk_grad, result, small = whole_step(
        trunk_input[0], tokens, table, conv_weight, out_weight, norm_gain, mid_gain, strand_perm[None], dilation, out_cotangent[0])
    conv_total, out_total = unpack_grads(result)
    table_total = jnp.concatenate([small[:4], small[4:8]], axis=1)
    gain_total = small[8:12].reshape(LAYERS, CH)
    return (block_out[None], trunk_grad[None], table_total, conv_total, out_total, gain_total, small[12:14])


def solution(mesh):
    placed = (P("dp", "ctx", None), P("dp", "ctx"), P(), P(), P(), P(), P(), P(), P(), P("dp", "ctx", None))
    return jax.shard_map(
        shards,
        mesh=mesh,
        in_specs=placed,
        out_specs=(P("dp", "ctx", None), P("dp", "ctx", None), P(), P(), P(), P(), P()),
        check_vma=False,
    )
```

```python
import jax
import jax.numpy as jnp
from jax import lax
from jax.experimental import pallas as pl
from jax.experimental.pallas import tpu as pltpu
from jax.sharding import PartitionSpec as P

LAYERS = 2
DMAX = 64

MESH = pl.DeviceIdType.MESH
GROWS = 3072
HALF = 1536
QUARTER = 384
EIGHTH = 96
SMALL = 16
LANES = 384


def place(core, y, z, x):
    return (lax.div(y, 2) * 2 + core, (lax.rem(y, 2) * 4 + z) * 4 + x)


def coordinates():
    dp = lax.axis_index("dp")
    ctx = lax.axis_index("ctx")
    y = lax.div(dp, 2) * 2 + lax.div(ctx, 16)
    return (lax.rem(dp, 2), y, lax.rem(lax.div(ctx, 4), 4), lax.rem(ctx, 4))


def ring_peer(spot, axis, distance):
    moved = list(spot)
    moved[axis] = lax.rem(spot[axis] + distance, 4)
    return place(*moved)


def core_peer(spot):
    return place(1 - spot[0], *spot[1:])


ORDERS = ((3, 1, 2), (1, 2, 3), (2, 3, 1))


class Copies:
    def __init__(self, send, recv):
        self.send, self.recv, self.open = send, recv, []

    def start(self, index, source, target, device):
        copy = pltpu.make_async_remote_copy(
            src_ref=source, dst_ref=target, send_sem=self.send.at[index],
            recv_sem=self.recv.at[index], device_id=device, device_id_type=MESH)
        copy.start()
        return copy


class Total:
    def __init__(self, spot, grads, result, core_in, sums0, in_a, sums1, in_b, sums2, in_c, send, recv):
        self.spot, self.grads, self.result = spot, grads, result
        self.core_in, self.sums0, self.in_a, self.sums1 = core_in, sums0, in_a, sums1
        self.in_b, self.sums2, self.in_c = in_b, sums2, in_c
        self.copies = Copies(send, recv)
        self.base = spot[0] * HALF

    def lanes(self, third):
        return pl.ds(third * 128, 128)

    def core_start(self):
        other = (1 - self.spot[0]) * HALF
        self.core = self.copies.start(0, self.grads.at[pl.ds(other, HALF)], self.core_in, core_peer(self.spot))

    def core_finish(self):
        self.core.wait()

        def body(step, carry):
            rows = pl.ds(pl.multiple_of(step * QUARTER, 32), QUARTER)
            mine = pl.ds(pl.multiple_of(self.base + step * QUARTER, 32), QUARTER)
            self.sums0[rows] = (self.grads[mine].astype(jnp.float32) + self.core_in[rows].astype(jnp.float32)).astype(jnp.bfloat16)
            return carry

        lax.fori_loop(0, 4, body, 0)

    def a_start(self):
        self.a = []
        for third, order in enumerate(ORDERS):
            for distance in (2, 1, 3):
                chunk = lax.rem(self.spot[order[0]] + distance, 4)
                self.a.append(self.copies.start(
                    1 + third * 3 + distance - 1,
                    self.sums0.at[pl.ds(chunk * QUARTER, QUARTER), self.lanes(third)],
                    self.in_a.at[third, distance - 1], ring_peer(self.spot, order[0], distance)))

    def a_finish(self):
        for copy in self.a:
            copy.wait()
        for third, order in enumerate(ORDERS):
            mine = pl.ds(pl.multiple_of(self.spot[order[0]] * QUARTER, 32), QUARTER)
            total = self.sums0[mine, self.lanes(third)].astype(jnp.float32)
            for slot in range(3):
                total = total + self.in_a[third, slot].astype(jnp.float32)
            self.sums1[third] = total.astype(jnp.bfloat16)

    def b_start(self):
        self.b = []
        for third, order in enumerate(ORDERS):
            for distance in (2, 1, 3):
                chunk = lax.rem(self.spot[order[1]] + distance, 4)
                self.b.append(self.copies.start(
                    10 + third * 3 + distance - 1,
                    self.sums1.at[third, pl.ds(chunk * EIGHTH, EIGHTH)],
                    self.in_b.at[third, distance - 1], ring_peer(self.spot, order[1], distance)))

    def b_finish(self):
        for copy in self.b:
            copy.wait()
        for third, order in enumerate(ORDERS):
            mine = pl.ds(pl.multiple_of(self.spot[order[1]] * EIGHTH, 32), EIGHTH)
            total = self.sums1[third, mine].astype(jnp.float32)
            for slot in range(3):
                total = total + self.in_b[third, slot].astype(jnp.float32)
            self.sums2[third] = total.astype(jnp.bfloat16)

    def c_start(self):
        self.c = []
        for third, order in enumerate(ORDERS):
            for distance in (2, 1, 3):
                self.c.append(self.copies.start(
                    19 + third * 3 + distance - 1, self.sums2.at[third],
                    self.in_c.at[third, self.spot[order[2]]], ring_peer(self.spot, order[2], distance)))
            self.in_c[third, self.spot[order[2]]] = self.sums2[third]

    def rows_of(self, third):
        order = ORDERS[third]
        quarter = self.base + self.spot[order[0]] * QUARTER
        return quarter, quarter + self.spot[order[1]] * EIGHTH

    def c_finish(self):
        for copy in self.c:
            copy.wait()
        for third in range(3):
            total = self.in_c[third, 0].astype(jnp.float32)
            for slot in range(1, 4):
                total = total + self.in_c[third, slot].astype(jnp.float32)
            _, eighth = self.rows_of(third)
            self.result[pl.ds(pl.multiple_of(eighth, 32), EIGHTH), self.lanes(third)] = total.astype(jnp.bfloat16)

    def gather_start(self, which):
        copies = []
        for third, order in enumerate(ORDERS):
            quarter, eighth = self.rows_of(third)
            rows = pl.ds(eighth, EIGHTH) if which else pl.ds(quarter, QUARTER)
            piece = self.result.at[rows, self.lanes(third)]
            for distance in (2, 1, 3):
                copies.append(self.copies.start(
                    28 + which * 9 + third * 3 + distance - 1, piece, piece, ring_peer(self.spot, order[which], distance)))
        return copies

    def last_start(self):
        piece = self.result.at[pl.ds(self.base, HALF)]
        return self.copies.start(46, piece, piece, core_peer(self.spot))


TOTAL_COPIES = 47


def total_scratch():
    return [
        pltpu.VMEM((HALF, LANES), jnp.bfloat16),
        pltpu.VMEM((HALF, LANES), jnp.bfloat16),
        pltpu.VMEM((3, 3, QUARTER, 128), jnp.bfloat16),
        pltpu.VMEM((3, QUARTER, 128), jnp.bfloat16),
        pltpu.VMEM((3, 3, EIGHTH, 128), jnp.bfloat16),
        pltpu.VMEM((3, EIGHTH, 128), jnp.bfloat16),
        pltpu.VMEM((3, 4, EIGHTH, 128), jnp.bfloat16),
        pltpu.SemaphoreType.DMA((TOTAL_COPIES,)),
        pltpu.SemaphoreType.DMA((TOTAL_COPIES,)),
    ]


class Small:
    def __init__(self, spot, value, core_in, ring_in, send, recv):
        self.spot, self.value, self.core_in, self.ring_in = spot, value, core_in, ring_in
        self.copies = Copies(send, recv)

    def core_start(self):
        self.core = self.copies.start(0, self.value, self.core_in, core_peer(self.spot))

    def core_finish(self):
        self.core.wait()
        own = self.spot[3]
        self.ring_in[0, own] = self.value[...] + self.core_in[...]

    def ring_start(self, stage):
        axis = (3, 1, 2)[stage]
        own = self.spot[axis]
        self.ring = [
            self.copies.start(1 + stage * 3 + distance - 1, self.ring_in.at[stage, own], self.ring_in.at[stage, own],
                              ring_peer(self.spot, axis, distance)) for distance in (2, 1, 3)]

    def ring_finish(self, stage):
        for copy in self.ring:
            copy.wait()
        total = self.ring_in[stage, 0] + self.ring_in[stage, 1] + self.ring_in[stage, 2] + self.ring_in[stage, 3]
        if stage < 2:
            self.ring_in[stage + 1, self.spot[(3, 1, 2)[stage + 1]]] = total
        return total


def small_scratch():
    return [
        pltpu.VMEM((SMALL, LANES), jnp.float32),
        pltpu.VMEM((3, 4, SMALL, LANES), jnp.float32),
        pltpu.SemaphoreType.DMA((10,)),
        pltpu.SemaphoreType.DMA((10,)),
    ]


def greet(spot, extra=()):
    barrier = pltpu.get_barrier_semaphore()
    peers = [core_peer(spot)] + [ring_peer(spot, axis, distance) for axis in (1, 2, 3) for distance in (1, 2, 3)]
    peers += list(extra)
    for peer in peers:
        pl.semaphore_signal(barrier, inc=1, device_id=peer, device_id_type=MESH)
    pl.semaphore_wait(barrier, len(peers))


epsilon = 1e-05
OWN = 256
WIDE = OWN + 2 * DMAX
CH = 768
MID = 384
TILE = 32
BF = jnp.bfloat16
F32 = jnp.float32


def dot(left, right):
    return jnp.dot(left, right, preferred_element_type=F32)


def dot_t(left, right):
    return lax.dot_general(left, right, (((1,), (1,)), ((), ())), preferred_element_type=F32)


def dot_rows(left, right):
    return lax.dot_general(left, right, (((0,), (0,)), ((), ())), preferred_element_type=F32)


def strand(s, width=CH):
    return pl.ds(s * width, width)


def loop(count, body):
    def step(index, carry):
        body(index)
        return carry

    lax.fori_loop(0, count, step, 0)


def tile_at(index, base=0, size=TILE):
    return pl.ds(pl.multiple_of(base + index * size, size), size)


def standard(values):
    centre = jnp.mean(values, axis=-1, keepdims=True)
    shifted = values - centre
    scale = lax.rsqrt(jnp.mean(shifted * shifted, axis=-1, keepdims=True) + epsilon)
    return shifted * scale, centre, scale


def gelu_pair(z):
    size = 1.0 + 0.23164189 * jnp.abs(z)
    t = pl.reciprocal(size, approx=True)
    t = t * (2.0 - size * t)
    bell = jnp.exp(-0.5 * z * z)
    tail = t * (0.127414796 + t * (-0.142248368 + t * (0.7107068705 + t * (-0.7265760135 + t * 0.5307027145))))
    tail = tail * bell
    below = jnp.where(z >= 0.0, 1.0 - tail, tail)
    return z * below, below + z * (0.3989422804014327 * bell)


def norm_back(dz, hat, scale, gain):
    dhat = dz * gain
    return scale * (
        dhat - jnp.mean(dhat, axis=-1, keepdims=True) - hat * jnp.mean(dhat * hat, axis=-1, keepdims=True)
    )


def fold(values):
    return values.reshape(TILE // 8, 8, values.shape[-1]).sum(axis=0)


def step_kernel(
    dilation, trunk, tokens, table, norm_gain, mid_gain, perm, cotangent, conv_hbm, out_hbm,
    block_hbm, trunk_hbm, conv_grads, out_grads, table_grad, gain_grad, mid_grad,
    block_out, table_pad, result, result_sem,
    conv_w, out_w, matrix, move, hidden, relabelled, u_pad, u_low, u_high, hat, slope, scale, mid,
    mid_hat, mid_slope, mid_scale, q, wide, back, rounded, e, dm_pad, dm_low, dm_high, grad, gain_acc, mid_acc,
    weight_sem, halo_send, halo_recv, grads, *scratch,
):
    spot = coordinates()
    dp = lax.axis_index("dp")
    ctx = lax.axis_index("ctx")
    left = (dp, lax.rem(ctx + 31, 32))
    right = (dp, lax.rem(ctx + 1, 32))
    first_bin = jnp.where(ctx == 0, DMAX, 0)
    end_bin = jnp.where(ctx == 31, DMAX + OWN, WIDE)
    weights = [
        pltpu.make_async_copy(conv_hbm, conv_w, weight_sem.at[0]),
        pltpu.make_async_copy(out_hbm, out_w, weight_sem.at[1]),
    ]
    for copy in weights:
        copy.start()
    each = len(total_scratch())
    totals = [Total(spot, grads.at[b], result.at[b], *scratch[b * each:(b + 1) * each]) for b in range(LAYERS)]
    small = Small(spot, *scratch[2 * each:])
    halos = Copies(halo_send, halo_recv)

    def trade(index, mine):
        return [
            halos.start(2 * index, mine.at[pl.ds(DMAX, DMAX)], mine.at[pl.ds(DMAX + OWN, DMAX)], left),
            halos.start(2 * index + 1, mine.at[pl.ds(OWN, DMAX)], mine.at[pl.ds(0, DMAX)], right),
        ]

    leaving = []

    def leave(source, target):
        copy = pltpu.make_async_copy(source, target, result_sem.at[len(leaving)])
        copy.start()
        leaving.append(copy)

    def leave_sums(b):
        leave(result.at[b, pl.ds(0, 2304)], conv_grads.at[b])
        for s in range(2):
            leave(result.at[b, pl.ds(2304 + s * MID, MID)], out_grads.at[b, :, strand(s, MID)])

    table_pad[...] = jnp.zeros_like(table_pad)
    table_pad[pl.ds(0, 4)] = table[...]
    one_hot = (tokens[...] == lax.broadcasted_iota(jnp.int32, (8, OWN), 0)).astype(F32)
    added = lax.dot_general(one_hot, table_pad[...], (((0,), (0,)), ((), ())), precision=lax.Precision.HIGHEST, preferred_element_type=F32)
    hidden[0, pl.ds(DMAX, OWN)] = (trunk[...].astype(F32) + added).astype(BF)
    greet(spot, (left, right))
    pending = trade(0, hidden.at[0])

    def fill_matrix(index):
        rows = tile_at(index)
        channel = lax.broadcasted_iota(jnp.int32, (TILE, CH), 0) + index * TILE
        matrix[rows] = jnp.where(channel == perm[...][None, :], 1.0, 0.0).astype(BF)

    loop(CH // TILE, fill_matrix)
    bin_from = lax.broadcasted_iota(jnp.int32, (OWN, WIDE), 1)
    bin_to = lax.broadcasted_iota(jnp.int32, (OWN, WIDE), 0) + DMAX
    inside = (bin_from >= first_bin) & (bin_from < end_bin)
    for b in range(LAYERS):
        for way in range(2):
            at = bin_to + (2 * way - 1) * dilation[b]
            move[b, way] = jnp.where(inside & (bin_from == at), 1.0, 0.0).astype(BF)
    e[pl.ds(0, OWN)] = (0.5 * cotangent[...].astype(F32)).astype(BF)

    for b in range(LAYERS):
        gain = norm_gain[pl.ds(b, 1)]
        mid_s = mid_gain[pl.ds(b, 1)]

        def front(rows, own):
            x = hidden[b, rows].astype(F32)
            hat_f, centre, inv = standard(x)
            hat_r = (relabelled[rows] - centre) * inv
            for s, normed in enumerate((hat_f, hat_r)):
                u, du = gelu_pair(normed * gain)
                u_pad[b, rows, strand(s)] = u.astype(BF)
                if own is not None:
                    hat[b, s, own] = normed
                    slope[b, s, own] = du
            if own is not None:
                scale[b, own] = jnp.broadcast_to(inv, (TILE, 128))

        relabelled[pl.ds(DMAX, OWN)] = dot(hidden[b, pl.ds(DMAX, OWN)], matrix[...])
        loop(OWN // TILE, lambda i: front(tile_at(i, DMAX), tile_at(i)))
        if b == 0:
            for copy in weights:
                copy.wait()
        for s in range(2):
            mid[s] = dot(u_pad[b, pl.ds(DMAX, OWN), strand(s)], conv_w[b, 1])
        for copy in pending:
            copy.wait()
        for base in (0, DMAX + OWN):
            relabelled[pl.ds(base, DMAX)] = dot(hidden[b, pl.ds(base, DMAX)], matrix[...])
            loop(DMAX // TILE, lambda i: front(tile_at(i, base), None))

        for s in range(2):
            u_low[s] = dot(move[b, s], u_pad[b, :, strand(s)]).astype(BF)
            u_high[s] = dot(move[b, 1 - s], u_pad[b, :, strand(s)]).astype(BF)
        for s in range(2):
            mid[s] += dot(u_low[s], conv_w[b, 0]) + dot(u_high[s], conv_w[b, 2])

        def middle(i):
            rows = tile_at(i)
            for s in range(2):
                normed, _, inv = standard(mid[s, rows])
                value, derivative = gelu_pair(normed * mid_s)
                q[b, s, rows] = value.astype(BF)
                mid_hat[b, s, rows] = normed
                mid_slope[b, s, rows] = derivative
                mid_scale[b, s, rows] = jnp.broadcast_to(inv, (TILE, 128))

        loop(OWN // TILE, middle)
        rounded[...] = dot(q[b, 1], out_w[b]).astype(BF)
        wide[0] = dot(q[b, 0], out_w[b])
        back[...] = dot_t(rounded[...], matrix[...])

        def join(i):
            rows = tile_at(i)
            total = wide[0, rows].astype(BF).astype(F32) + back[rows]
            following = (hidden[b, tile_at(i, DMAX)].astype(F32) + 0.5 * total).astype(BF)
            if b + 1 < LAYERS:
                hidden[b + 1, tile_at(i, DMAX)] = following
            else:
                block_out[rows] = following

        loop(OWN // TILE, join)
        if b + 1 < LAYERS:
            pending = trade(b + 1, hidden.at[b + 1])

    leave(block_out, block_hbm)
    grad[...] = cotangent[...]
    gain_acc[...] = jnp.zeros_like(gain_acc)
    mid_acc[...] = jnp.zeros_like(mid_acc)
    for b in (1, 0):
        gain = norm_gain[pl.ds(b, 1)]
        mid_s = mid_gain[pl.ds(b, 1)]
        sums = grads.at[b]
        if b == 0:
            e[pl.ds(0, OWN)] = (0.5 * grad[...].astype(F32)).astype(BF)
        e[pl.ds(OWN, OWN)] = dot(e[pl.ds(0, OWN)], matrix[...]).astype(BF)
        for s in range(2):
            mid[s] = dot_t(e[pl.ds(s * OWN, OWN)], out_w[b])

        def middle_back(i):
            rows = tile_at(i)
            total = jnp.zeros((8, MID), F32)
            for s in range(2):
                dz = mid[s, rows] * mid_slope[b, s, rows]
                normed = mid_hat[b, s, rows]
                total = total + fold(dz * normed)
                dm = norm_back(dz, normed, mid_scale[b, s, rows, 0:1], mid_s)
                dm_pad[b, tile_at(i, DMAX), strand(s, MID)] = dm.astype(BF)
            mid_acc[b] += total

        loop(OWN // TILE, middle_back)
        pending = trade(LAYERS + b, dm_pad.at[b])
        if b == 0:
            totals[1].a_finish()
            totals[1].b_start()
        q_all = q[b].reshape(2 * OWN, MID)
        out_grad = dot_rows(q_all, e[...])
        sums[pl.ds(2304, MID)] = out_grad[:, :MID].astype(BF)
        sums[pl.ds(2688, MID)] = out_grad[:, MID:].astype(BF)
        own = pl.ds(DMAX, OWN)
        u_all = jnp.concatenate([u_pad[b, own, strand(s)] for s in range(2)], axis=0)
        dm_all = jnp.concatenate([dm_pad[b, own, strand(s, MID)] for s in range(2)], axis=0)
        sums[pl.ds(CH, CH)] = dot_rows(u_all, dm_all).astype(BF)
        for s in range(2):
            wide[s] = dot_t(dm_pad[b, own, strand(s, MID)], conv_w[b, 1])
        for copy in pending:
            copy.wait()
        for s in range(2):
            dm_low[s] = dot(move[b, 1 - s], dm_pad[b, :, strand(s, MID)]).astype(BF)
            dm_high[s] = dot(move[b, s], dm_pad[b, :, strand(s, MID)]).astype(BF)
        sums[pl.ds(0, CH)] = dot_rows(u_all, dm_low[...].reshape(2 * OWN, MID)).astype(BF)
        sums[pl.ds(2 * CH, CH)] = dot_rows(u_all, dm_high[...].reshape(2 * OWN, MID)).astype(BF)
        totals[b].core_start()
        if b == 0:
            totals[1].b_finish()
            totals[1].c_start()
        for s in range(2):
            wide[s] += dot_t(dm_low[s], conv_w[b, 0]) + dot_t(dm_high[s], conv_w[b, 2])

        def front_back(i):
            rows = tile_at(i)
            total = jnp.zeros((8, CH), F32)
            for s in range(2):
                dz = wide[s, rows] * slope[b, s, rows]
                normed = hat[b, s, rows]
                total = total + fold(dz * normed)
                dx = norm_back(dz, normed, scale[b, rows, 0:1], gain)
                if s == 0:
                    wide[0, rows] = dx
                else:
                    rounded[rows] = dx.astype(BF)
            gain_acc[b] += total

        loop(OWN // TILE, front_back)
        back[...] = dot_t(rounded[...], matrix[...])

        def join_back(i):
            rows = tile_at(i)
            total = grad[rows].astype(F32) + wide[0, rows].astype(BF).astype(F32) + back[rows]
            grad[rows] = total.astype(BF)

        loop(OWN // TILE, join_back)
        totals[b].core_finish()
        totals[b].a_start()

    leave(grad, trunk_hbm)
    table_term = dot(one_hot.astype(BF), grad[...])
    small.value[pl.ds(0, 4)] = table_term[0:4, :MID]
    small.value[pl.ds(4, 4)] = table_term[0:4, MID:]
    for b in range(LAYERS):
        term = jnp.sum(gain_acc[b], axis=0, keepdims=True)
        small.value[pl.ds(8 + 2 * b, 1)] = term[:, :MID]
        small.value[pl.ds(9 + 2 * b, 1)] = term[:, MID:]
        small.value[pl.ds(12 + b, 1)] = jnp.sum(mid_acc[b], axis=0, keepdims=True)
    small.value[pl.ds(14, 2)] = jnp.zeros((2, MID), F32)
    small.core_start()
    totals[1].c_finish()
    first = totals[1].gather_start(1)
    small.core_finish()
    small.ring_start(0)
    totals[0].a_finish()
    totals[0].b_start()
    for copy in first:
        copy.wait()
    first = totals[1].gather_start(0)
    small.ring_finish(0)
    small.ring_start(1)
    totals[0].b_finish()
    totals[0].c_start()
    small.ring_finish(1)
    small.ring_start(2)
    totals[0].c_finish()
    second = totals[0].gather_start(1)
    for copy in first:
        copy.wait()
    first = totals[1].last_start()
    sums = small.ring_finish(2)
    table_grad[:, pl.ds(0, MID)] = sums[0:4]
    table_grad[:, pl.ds(MID, MID)] = sums[4:8]
    for b in range(LAYERS):
        gain_grad[pl.ds(b, 1), pl.ds(0, MID)] = sums[8 + 2 * b:9 + 2 * b]
        gain_grad[pl.ds(b, 1), pl.ds(MID, MID)] = sums[9 + 2 * b:10 + 2 * b]
    mid_grad[...] = sums[12:14]
    for copy in second:
        copy.wait()
    second = totals[0].gather_start(0)
    first.wait()
    leave_sums(1)
    for copy in second:
        copy.wait()
    totals[0].last_start().wait()
    leave_sums(0)
    for copy in leaving:
        copy.wait()


def whole_step(trunk, tokens, table, conv_w, out_w, norm_gain, mid_gain, perm, dilation, cotangent):
    vmem = pl.BlockSpec(memory_space=pltpu.VMEM)
    stay = pl.BlockSpec(memory_space=pl.ANY)
    smem = pl.BlockSpec(memory_space=pltpu.SMEM)
    scratch = [
        pltpu.VMEM((OWN, CH), BF),
        pltpu.VMEM((8, CH), F32),
        pltpu.VMEM((LAYERS, GROWS, LANES), BF),
        pltpu.SemaphoreType.DMA((8,)),
        pltpu.VMEM((LAYERS, 3, CH, MID), BF),
        pltpu.VMEM((LAYERS, MID, CH), BF),
        pltpu.VMEM((CH, CH), BF),
        pltpu.VMEM((LAYERS, 2, OWN, WIDE), BF),
        pltpu.VMEM((LAYERS, WIDE, CH), BF),
        pltpu.VMEM((WIDE, CH), F32),
        pltpu.VMEM((LAYERS, WIDE, 2 * CH), BF),
        pltpu.VMEM((2, OWN, CH), BF),
        pltpu.VMEM((2, OWN, CH), BF),
        pltpu.VMEM((LAYERS, 2, OWN, CH), F32),
        pltpu.VMEM((LAYERS, 2, OWN, CH), F32),
        pltpu.VMEM((LAYERS, OWN, 128), F32),
        pltpu.VMEM((2, OWN, MID), F32),
        pltpu.VMEM((LAYERS, 2, OWN, MID), F32),
        pltpu.VMEM((LAYERS, 2, OWN, MID), F32),
        pltpu.VMEM((LAYERS, 2, OWN, 128), F32),
        pltpu.VMEM((LAYERS, 2, OWN, MID), BF),
        pltpu.VMEM((2, OWN, CH), F32),
        pltpu.VMEM((OWN, CH), F32),
        pltpu.VMEM((OWN, CH), BF),
        pltpu.VMEM((2 * OWN, CH), BF),
        pltpu.VMEM((LAYERS, WIDE, 2 * MID), BF),
        pltpu.VMEM((2, OWN, MID), BF),
        pltpu.VMEM((2, OWN, MID), BF),
        pltpu.VMEM((OWN, CH), BF),
        pltpu.VMEM((LAYERS, 8, CH), F32),
        pltpu.VMEM((LAYERS, 8, MID), F32),
        pltpu.SemaphoreType.DMA((2,)),
        pltpu.SemaphoreType.DMA((8,)),
        pltpu.SemaphoreType.DMA((8,)),
        pltpu.VMEM((LAYERS, GROWS, LANES), BF),
    ]
    small = [pltpu.VMEM((SMALL, LANES), F32)] + small_scratch()
    return pl.pallas_call(
        step_kernel,
        out_shape=(
            jax.ShapeDtypeStruct((OWN, CH), BF),
            jax.ShapeDtypeStruct((OWN, CH), BF),
            jax.ShapeDtypeStruct((LAYERS, 3 * CH, MID), BF),
            jax.ShapeDtypeStruct((LAYERS, MID, CH), BF),
            jax.ShapeDtypeStruct((4, CH), F32),
            jax.ShapeDtypeStruct((LAYERS, CH), F32),
            jax.ShapeDtypeStruct((LAYERS, MID), F32),
        ),
        in_specs=[smem] + [vmem] * 7 + [stay] * 2,
        out_specs=(stay,) * 4 + (vmem,) * 3,
        scratch_shapes=scratch + total_scratch() * 2 + small,
        compiler_params=pltpu.CompilerParams(collective_id=0, has_side_effects=True, vmem_limit_bytes=56 * 1024 * 1024),
        cost_estimate=pl.CostEstimate(flops=10**10, bytes_accessed=2 * 10**7, transcendentals=0),
        name="step",
    )(dilation, trunk, tokens, table, norm_gain, mid_gain, perm, cotangent, conv_w, out_w)


def shards(trunk_input, tokens, token_table, conv_weight, out_weight, norm_gain, mid_gain, strand_perm, dilation, out_cotangent):
    block_out, trunk_grad, conv_total, out_total, table_total, gain_total, mid_total = whole_step(
        trunk_input[0], tokens, token_table, conv_weight, out_weight, norm_gain, mid_gain, strand_perm, dilation, out_cotangent[0])
    conv_total = conv_total.astype(F32).reshape(LAYERS, 3, CH, MID)
    return (block_out[None], trunk_grad[None], table_total, conv_total, out_total.astype(F32), gain_total, mid_total)


def solution(mesh):
    placed = (P("dp", "ctx", None), P("dp", "ctx"), P(), P(), P(), P(), P(), P(), P(), P("dp", "ctx", None))
    return jax.shard_map(
        shards,
        mesh=mesh,
        in_specs=placed,
        out_specs=(P("dp", "ctx", None), P("dp", "ctx", None), P(), P(), P(), P(), P()),
        check_vma=False,
    )
```

```python
import jax
import jax.numpy as jnp
from jax import lax
from jax.experimental import pallas as pl
from jax.experimental.pallas import tpu as pltpu
from jax.sharding import PartitionSpec as P

LAYERS = 2
DMAX = 64

MESH = pl.DeviceIdType.MESH
GROWS = 3072
HALF = 1536
QUARTER = 384
EIGHTH = 96
SMALL = 16
LANES = 384


def place(core, y, z, x):
    return (lax.div(y, 2) * 2 + core, (lax.rem(y, 2) * 4 + z) * 4 + x)


def coordinates():
    dp = lax.axis_index("dp")
    ctx = lax.axis_index("ctx")
    y = lax.div(dp, 2) * 2 + lax.div(ctx, 16)
    return (lax.rem(dp, 2), y, lax.rem(lax.div(ctx, 4), 4), lax.rem(ctx, 4))


def ring_peer(spot, axis, distance):
    moved = list(spot)
    moved[axis] = lax.rem(spot[axis] + distance, 4)
    return place(*moved)


def core_peer(spot):
    return place(1 - spot[0], *spot[1:])


ORDERS = ((3, 1, 2), (1, 2, 3), (2, 3, 1))


class Copies:
    def __init__(self, send, recv):
        self.send, self.recv, self.open = send, recv, []

    def start(self, index, source, target, device):
        copy = pltpu.make_async_remote_copy(
            src_ref=source, dst_ref=target, send_sem=self.send.at[index],
            recv_sem=self.recv.at[index], device_id=device, device_id_type=MESH)
        copy.start()
        return copy


class Total:
    def __init__(self, spot, grads, result, core_in, sums0, in_a, sums1, in_b, sums2, in_c, send, recv):
        self.spot, self.grads, self.result = spot, grads, result
        self.core_in, self.sums0, self.in_a, self.sums1 = core_in, sums0, in_a, sums1
        self.in_b, self.sums2, self.in_c = in_b, sums2, in_c
        self.copies = Copies(send, recv)
        self.base = spot[0] * HALF

    def lanes(self, third):
        return pl.ds(third * 128, 128)

    def core_start(self):
        other = (1 - self.spot[0]) * HALF
        self.core = self.copies.start(0, self.grads.at[pl.ds(other, HALF)], self.core_in, core_peer(self.spot))

    def core_finish(self):
        self.core.wait()

        def body(step, carry):
            rows = pl.ds(pl.multiple_of(step * QUARTER, 32), QUARTER)
            mine = pl.ds(pl.multiple_of(self.base + step * QUARTER, 32), QUARTER)
            self.sums0[rows] = (self.grads[mine].astype(jnp.float32) + self.core_in[rows].astype(jnp.float32)).astype(jnp.bfloat16)
            return carry

        lax.fori_loop(0, 4, body, 0)

    def a_start(self):
        self.a = []
        for third, order in enumerate(ORDERS):
            for distance in (2, 1, 3):
                chunk = lax.rem(self.spot[order[0]] + distance, 4)
                self.a.append(self.copies.start(
                    1 + third * 3 + distance - 1,
                    self.sums0.at[pl.ds(chunk * QUARTER, QUARTER), self.lanes(third)],
                    self.in_a.at[third, distance - 1], ring_peer(self.spot, order[0], distance)))

    def a_finish(self):
        for copy in self.a:
            copy.wait()
        for third, order in enumerate(ORDERS):
            mine = pl.ds(pl.multiple_of(self.spot[order[0]] * QUARTER, 32), QUARTER)
            total = self.sums0[mine, self.lanes(third)].astype(jnp.float32)
            for slot in range(3):
                total = total + self.in_a[third, slot].astype(jnp.float32)
            self.sums1[third] = total.astype(jnp.bfloat16)

    def b_start(self):
        self.b = []
        for third, order in enumerate(ORDERS):
            for distance in (2, 1, 3):
                chunk = lax.rem(self.spot[order[1]] + distance, 4)
                self.b.append(self.copies.start(
                    10 + third * 3 + distance - 1,
                    self.sums1.at[third, pl.ds(chunk * EIGHTH, EIGHTH)],
                    self.in_b.at[third, distance - 1], ring_peer(self.spot, order[1], distance)))

    def b_finish(self):
        for copy in self.b:
            copy.wait()
        for third, order in enumerate(ORDERS):
            mine = pl.ds(pl.multiple_of(self.spot[order[1]] * EIGHTH, 32), EIGHTH)
            total = self.sums1[third, mine].astype(jnp.float32)
            for slot in range(3):
                total = total + self.in_b[third, slot].astype(jnp.float32)
            self.sums2[third] = total.astype(jnp.bfloat16)

    def c_start(self):
        self.c = []
        for third, order in enumerate(ORDERS):
            for distance in (2, 1, 3):
                self.c.append(self.copies.start(
                    19 + third * 3 + distance - 1, self.sums2.at[third],
                    self.in_c.at[third, self.spot[order[2]]], ring_peer(self.spot, order[2], distance)))
            self.in_c[third, self.spot[order[2]]] = self.sums2[third]

    def rows_of(self, third):
        order = ORDERS[third]
        quarter = self.base + self.spot[order[0]] * QUARTER
        return quarter, quarter + self.spot[order[1]] * EIGHTH

    def c_finish(self):
        for copy in self.c:
            copy.wait()
        for third in range(3):
            total = self.in_c[third, 0].astype(jnp.float32)
            for slot in range(1, 4):
                total = total + self.in_c[third, slot].astype(jnp.float32)
            _, eighth = self.rows_of(third)
            self.result[pl.ds(pl.multiple_of(eighth, 32), EIGHTH), self.lanes(third)] = total.astype(jnp.bfloat16)

    def gather(self, which):
        copies = []
        for third, order in enumerate(ORDERS):
            quarter, eighth = self.rows_of(third)
            rows = pl.ds(eighth, EIGHTH) if which else pl.ds(quarter, QUARTER)
            piece = self.result.at[rows, self.lanes(third)]
            for distance in (1, 3, 2):
                copies.append(self.copies.start(
                    28 + which * 9 + third * 3 + distance - 1, piece, piece, ring_peer(self.spot, order[which], distance)))
        return copies

    def b_gather(self):
        self.late = self.gather(1)

    def pass_on(self, third, distance):
        quarter = lax.rem(self.spot[ORDERS[third][0]] + 4 - distance, 4)
        piece = self.result.at[pl.ds(self.base + quarter * QUARTER, QUARTER), self.lanes(third)]
        self.last.append(self.copies.start(46 + third * 4 + distance, piece, piece, core_peer(self.spot)))

    def a_gather(self):
        for copy in self.late:
            copy.wait()
        self.late = self.gather(0)
        self.last = []
        for third in range(3):
            self.pass_on(third, 0)

    def forward(self):
        for slot, distance in enumerate((1, 3, 2)):
            for third in range(3):
                self.late[third * 3 + slot].wait()
                self.pass_on(third, distance)

    def finish(self):
        for copy in self.last:
            copy.wait()


TOTAL_COPIES = 58


def total_scratch():
    return [
        pltpu.VMEM((HALF, LANES), jnp.bfloat16),
        pltpu.VMEM((HALF, LANES), jnp.bfloat16),
        pltpu.VMEM((3, 3, QUARTER, 128), jnp.bfloat16),
        pltpu.VMEM((3, QUARTER, 128), jnp.bfloat16),
        pltpu.VMEM((3, 3, EIGHTH, 128), jnp.bfloat16),
        pltpu.VMEM((3, EIGHTH, 128), jnp.bfloat16),
        pltpu.VMEM((3, 4, EIGHTH, 128), jnp.bfloat16),
        pltpu.SemaphoreType.DMA((TOTAL_COPIES,)),
        pltpu.SemaphoreType.DMA((TOTAL_COPIES,)),
    ]


class Small:
    def __init__(self, spot, value, core_in, ring_in, send, recv):
        self.spot, self.value, self.core_in, self.ring_in = spot, value, core_in, ring_in
        self.copies = Copies(send, recv)

    def core_start(self):
        self.core = self.copies.start(0, self.value, self.core_in, core_peer(self.spot))

    def core_finish(self):
        self.core.wait()
        own = self.spot[3]
        self.ring_in[0, own] = self.value[...] + self.core_in[...]

    def ring_start(self, stage):
        axis = (3, 1, 2)[stage]
        own = self.spot[axis]
        self.ring = [
            self.copies.start(1 + stage * 3 + distance - 1, self.ring_in.at[stage, own], self.ring_in.at[stage, own],
                              ring_peer(self.spot, axis, distance)) for distance in (2, 1, 3)]

    def ring_finish(self, stage):
        for copy in self.ring:
            copy.wait()
        total = self.ring_in[stage, 0] + self.ring_in[stage, 1] + self.ring_in[stage, 2] + self.ring_in[stage, 3]
        if stage < 2:
            self.ring_in[stage + 1, self.spot[(3, 1, 2)[stage + 1]]] = total
        return total


def small_scratch():
    return [
        pltpu.VMEM((SMALL, LANES), jnp.float32),
        pltpu.VMEM((3, 4, SMALL, LANES), jnp.float32),
        pltpu.SemaphoreType.DMA((10,)),
        pltpu.SemaphoreType.DMA((10,)),
    ]


def greet(spot, extra=()):
    barrier = pltpu.get_barrier_semaphore()
    peers = [core_peer(spot)] + [ring_peer(spot, axis, distance) for axis in (1, 2, 3) for distance in (1, 2, 3)]
    peers += list(extra)
    for peer in peers:
        pl.semaphore_signal(barrier, inc=1, device_id=peer, device_id_type=MESH)
    pl.semaphore_wait(barrier, len(peers))


epsilon = 1e-05
OWN = 256
WIDE = OWN + 2 * DMAX
CH = 768
MID = 384
TILE = 64
BF = jnp.bfloat16
F32 = jnp.float32


def dot(left, right):
    return jnp.dot(left, right, preferred_element_type=F32)


def dot_t(left, right):
    return lax.dot_general(left, right, (((1,), (1,)), ((), ())), preferred_element_type=F32)


def dot_rows(left, right):
    return lax.dot_general(left, right, (((0,), (0,)), ((), ())), preferred_element_type=F32)


def strand(s, width=CH):
    return pl.ds(s * width, width)


def loop(count, body):
    def step(index, carry):
        body(index)
        return carry

    lax.fori_loop(0, count, step, 0, unroll=2 if count % 2 == 0 else 1)


def tile_at(index, base=0, size=TILE):
    return pl.ds(pl.multiple_of(base + index * size, size), size)


def standard(values):
    centre = jnp.mean(values, axis=-1, keepdims=True)
    shifted = values - centre
    scale = lax.rsqrt(jnp.mean(shifted * shifted, axis=-1, keepdims=True) + epsilon)
    return shifted * scale, centre, scale


def gelu_pair(z):
    size = 1.0 + 0.23164189 * jnp.abs(z)
    t = pl.reciprocal(size, approx=True)
    t = t * (2.0 - size * t)
    bell = jnp.exp(-0.5 * z * z)
    tail = t * (0.127414796 + t * (-0.142248368 + t * (0.7107068705 + t * (-0.7265760135 + t * 0.5307027145))))
    tail = tail * bell
    below = jnp.where(z >= 0.0, 1.0 - tail, tail)
    return z * below, below + z * (0.3989422804014327 * bell)


def norm_back(dz, hat, scale, gain):
    dhat = dz * gain
    return scale * (
        dhat - jnp.mean(dhat, axis=-1, keepdims=True) - hat * jnp.mean(dhat * hat, axis=-1, keepdims=True)
    )


def fold(values):
    return values.reshape(TILE // 8, 8, values.shape[-1]).sum(axis=0)


def step_kernel(
    dilation, trunk, tokens, table, norm_gain, mid_gain, perm, cotangent, conv_hbm, out_hbm,
    block_hbm, trunk_hbm, conv_grads, out_grads, table_grad, gain_grad, mid_grad,
    block_out, table_pad, result, result_sem,
    conv_w, out_w, matrix, move, hidden, relabelled, u_pad, u_low, u_high, hat, slope, scale, mid,
    mid_hat, mid_slope, mid_scale, q, wide, back, rounded, e, dm_pad, dm_low, dm_high, grad, gain_acc, mid_acc,
    weight_sem, halo_send, halo_recv, grads, *scratch,
):
    spot = coordinates()
    dp = lax.axis_index("dp")
    ctx = lax.axis_index("ctx")
    left = (dp, lax.rem(ctx + 31, 32))
    right = (dp, lax.rem(ctx + 1, 32))
    first_bin = jnp.where(ctx == 0, DMAX, 0)
    end_bin = jnp.where(ctx == 31, DMAX + OWN, WIDE)
    weights = [
        pltpu.make_async_copy(conv_hbm, conv_w, weight_sem.at[0]),
        pltpu.make_async_copy(out_hbm, out_w, weight_sem.at[1]),
    ]
    for copy in weights:
        copy.start()
    each = len(total_scratch())
    totals = [Total(spot, grads.at[b], result.at[b], *scratch[b * each:(b + 1) * each]) for b in range(LAYERS)]
    small = Small(spot, *scratch[2 * each:])
    halos = Copies(halo_send, halo_recv)

    def trade(index, mine):
        return [
            halos.start(2 * index, mine.at[pl.ds(DMAX, DMAX)], mine.at[pl.ds(DMAX + OWN, DMAX)], left),
            halos.start(2 * index + 1, mine.at[pl.ds(OWN, DMAX)], mine.at[pl.ds(0, DMAX)], right),
        ]

    leaving = []

    def leave(source, target):
        copy = pltpu.make_async_copy(source, target, result_sem.at[len(leaving)])
        copy.start()
        leaving.append(copy)

    def leave_sums(b):
        leave(result.at[b, pl.ds(0, 2304)], conv_grads.at[b])
        for s in range(2):
            leave(result.at[b, pl.ds(2304 + s * MID, MID)], out_grads.at[b, :, strand(s, MID)])

    table_pad[...] = jnp.zeros_like(table_pad)
    table_pad[pl.ds(0, 4)] = table[...]
    one_hot = (tokens[...] == lax.broadcasted_iota(jnp.int32, (8, OWN), 0)).astype(F32)
    added = lax.dot_general(one_hot, table_pad[...], (((0,), (0,)), ((), ())), precision=lax.Precision.HIGHEST, preferred_element_type=F32)
    hidden[0, pl.ds(DMAX, OWN)] = (trunk[...].astype(F32) + added).astype(BF)
    greet(spot, (left, right))
    pending = trade(0, hidden.at[0])

    def fill_matrix(index):
        rows = tile_at(index)
        channel = lax.broadcasted_iota(jnp.int32, (TILE, CH), 0) + index * TILE
        matrix[rows] = jnp.where(channel == perm[...][None, :], 1.0, 0.0).astype(BF)

    loop(CH // TILE, fill_matrix)
    bin_from = lax.broadcasted_iota(jnp.int32, (OWN, WIDE), 1)
    bin_to = lax.broadcasted_iota(jnp.int32, (OWN, WIDE), 0) + DMAX
    inside = (bin_from >= first_bin) & (bin_from < end_bin)
    for b in range(LAYERS):
        for way in range(2):
            at = bin_to + (2 * way - 1) * dilation[b]
            move[b, way] = jnp.where(inside & (bin_from == at), 1.0, 0.0).astype(BF)
    e[pl.ds(0, OWN)] = (0.5 * cotangent[...].astype(F32)).astype(BF)

    for b in range(LAYERS):
        gain = norm_gain[pl.ds(b, 1)]
        mid_s = mid_gain[pl.ds(b, 1)]

        def front(rows, own):
            x = hidden[b, rows].astype(F32)
            hat_f, centre, inv = standard(x)
            hat_r = (relabelled[rows] - centre) * inv
            for s, normed in enumerate((hat_f, hat_r)):
                u, du = gelu_pair(normed * gain)
                u_pad[b, rows, strand(s)] = u.astype(BF)
                if own is not None:
                    hat[b, s, own] = normed
                    slope[b, s, own] = du
            if own is not None:
                scale[b, own] = jnp.broadcast_to(inv, (TILE, 128))

        relabelled[pl.ds(DMAX, OWN)] = dot(hidden[b, pl.ds(DMAX, OWN)], matrix[...])
        loop(OWN // TILE, lambda i: front(tile_at(i, DMAX), tile_at(i)))
        if b == 0:
            for copy in weights:
                copy.wait()
        for s in range(2):
            mid[s] = dot(u_pad[b, pl.ds(DMAX, OWN), strand(s)], conv_w[b, 1])
        for copy in pending:
            copy.wait()
        for base in (0, DMAX + OWN):
            relabelled[pl.ds(base, DMAX)] = dot(hidden[b, pl.ds(base, DMAX)], matrix[...])
            loop(DMAX // TILE, lambda i: front(tile_at(i, base), None))

        for s in range(2):
            u_low[b, s] = dot(move[b, s], u_pad[b, :, strand(s)]).astype(BF)
            u_high[b, s] = dot(move[b, 1 - s], u_pad[b, :, strand(s)]).astype(BF)
        for s in range(2):
            mid[s] += dot(u_low[b, s], conv_w[b, 0]) + dot(u_high[b, s], conv_w[b, 2])

        def middle(i):
            rows = tile_at(i)
            for s in range(2):
                normed, _, inv = standard(mid[s, rows])
                value, derivative = gelu_pair(normed * mid_s)
                q[b, s, rows] = value.astype(BF)
                mid_hat[b, s, rows] = normed
                mid_slope[b, s, rows] = derivative
                mid_scale[b, s, rows] = jnp.broadcast_to(inv, (TILE, 128))

        loop(OWN // TILE, middle)
        rounded[...] = dot(q[b, 1], out_w[b]).astype(BF)
        wide[0] = dot(q[b, 0], out_w[b])
        back[...] = dot_t(rounded[...], matrix[...])

        def join(i):
            rows = tile_at(i)
            total = wide[0, rows].astype(BF).astype(F32) + back[rows]
            following = (hidden[b, tile_at(i, DMAX)].astype(F32) + 0.5 * total).astype(BF)
            if b + 1 < LAYERS:
                hidden[b + 1, tile_at(i, DMAX)] = following
            else:
                block_out[rows] = following

        loop(OWN // TILE, join)
        if b + 1 < LAYERS:
            pending = trade(b + 1, hidden.at[b + 1])

    leave(block_out, block_hbm)
    grad[...] = cotangent[...]
    gain_acc[...] = jnp.zeros_like(gain_acc)
    mid_acc[...] = jnp.zeros_like(mid_acc)
    for b in (1, 0):
        gain = norm_gain[pl.ds(b, 1)]
        mid_s = mid_gain[pl.ds(b, 1)]
        sums = grads.at[b]
        if b == 0:
            e[pl.ds(0, OWN)] = (0.5 * grad[...].astype(F32)).astype(BF)
        e[pl.ds(OWN, OWN)] = dot(e[pl.ds(0, OWN)], matrix[...]).astype(BF)
        for s in range(2):
            mid[s] = dot_t(e[pl.ds(s * OWN, OWN)], out_w[b])

        def middle_back(i):
            rows = tile_at(i)
            total = jnp.zeros((8, MID), F32)
            for s in range(2):
                dz = mid[s, rows] * mid_slope[b, s, rows]
                normed = mid_hat[b, s, rows]
                total = total + fold(dz * normed)
                dm = norm_back(dz, normed, mid_scale[b, s, rows, 0:1], mid_s)
                dm_pad[b, tile_at(i, DMAX), strand(s, MID)] = dm.astype(BF)
            mid_acc[b] += total

        loop(OWN // TILE, middle_back)
        pending = trade(LAYERS + b, dm_pad.at[b])
        q_all = q[b].reshape(2 * OWN, MID)
        out_grad = dot_rows(q_all, e[...])
        sums[pl.ds(2304, MID)] = out_grad[:, :MID].astype(BF)
        sums[pl.ds(2688, MID)] = out_grad[:, MID:].astype(BF)
        own = pl.ds(DMAX, OWN)
        u_all = jnp.concatenate([u_pad[b, own, strand(s)] for s in range(2)], axis=0)
        dm_all = jnp.concatenate([dm_pad[b, own, strand(s, MID)] for s in range(2)], axis=0)
        for tap, left_side in enumerate((u_low[b].reshape(2 * OWN, CH), u_all, u_high[b].reshape(2 * OWN, CH))):
            sums[pl.ds(tap * CH, CH)] = dot_rows(left_side, dm_all).astype(BF)
        totals[b].core_start()
        for s in range(2):
            wide[s] = dot_t(dm_pad[b, own, strand(s, MID)], conv_w[b, 1])
        if b == 0:
            totals[1].a_finish()
            totals[1].b_start()
        for copy in pending:
            copy.wait()
        for s in range(2):
            dm_low[s] = dot(move[b, 1 - s], dm_pad[b, :, strand(s, MID)]).astype(BF)
            dm_high[s] = dot(move[b, s], dm_pad[b, :, strand(s, MID)]).astype(BF)
        for s in range(2):
            wide[s] += dot_t(dm_low[s], conv_w[b, 0]) + dot_t(dm_high[s], conv_w[b, 2])
        totals[b].core_finish()
        totals[b].a_start()
        if b == 0:
            totals[1].b_finish()
            totals[1].c_start()

        def front_back(i):
            rows = tile_at(i)
            total = jnp.zeros((8, CH), F32)
            for s in range(2):
                dz = wide[s, rows] * slope[b, s, rows]
                normed = hat[b, s, rows]
                total = total + fold(dz * normed)
                dx = norm_back(dz, normed, scale[b, rows, 0:1], gain)
                if s == 0:
                    wide[0, rows] = dx
                else:
                    rounded[rows] = dx.astype(BF)
            gain_acc[b] += total

        loop(OWN // TILE, front_back)
        back[...] = dot_t(rounded[...], matrix[...])

        def join_back(i):
            rows = tile_at(i)
            total = grad[rows].astype(F32) + wide[0, rows].astype(BF).astype(F32) + back[rows]
            grad[rows] = total.astype(BF)

        loop(OWN // TILE, join_back)

    leave(grad, trunk_hbm)
    table_term = dot(one_hot.astype(BF), grad[...])
    small.value[pl.ds(0, 4)] = table_term[0:4, :MID]
    small.value[pl.ds(4, 4)] = table_term[0:4, MID:]
    for b in range(LAYERS):
        term = jnp.sum(gain_acc[b], axis=0, keepdims=True)
        small.value[pl.ds(8 + 2 * b, 1)] = term[:, :MID]
        small.value[pl.ds(9 + 2 * b, 1)] = term[:, MID:]
        small.value[pl.ds(12 + b, 1)] = jnp.sum(mid_acc[b], axis=0, keepdims=True)
    small.value[pl.ds(14, 2)] = jnp.zeros((2, MID), F32)
    small.core_start()
    totals[1].c_finish()
    totals[1].b_gather()
    totals[0].a_finish()
    totals[0].b_start()
    small.core_finish()
    small.ring_start(0)
    totals[1].a_gather()
    totals[0].b_finish()
    totals[0].c_start()
    small.ring_finish(0)
    small.ring_start(1)
    totals[0].c_finish()
    totals[0].b_gather()
    totals[1].forward()
    small.ring_finish(1)
    small.ring_start(2)
    totals[0].a_gather()
    totals[1].finish()
    leave_sums(1)
    sums = small.ring_finish(2)
    table_grad[:, pl.ds(0, MID)] = sums[0:4]
    table_grad[:, pl.ds(MID, MID)] = sums[4:8]
    for b in range(LAYERS):
        gain_grad[pl.ds(b, 1), pl.ds(0, MID)] = sums[8 + 2 * b:9 + 2 * b]
        gain_grad[pl.ds(b, 1), pl.ds(MID, MID)] = sums[9 + 2 * b:10 + 2 * b]
    mid_grad[...] = sums[12:14]
    totals[0].forward()
    totals[0].finish()
    leave_sums(0)
    for copy in leaving:
        copy.wait()


def whole_step(trunk, tokens, table, conv_w, out_w, norm_gain, mid_gain, perm, dilation, cotangent):
    vmem = pl.BlockSpec(memory_space=pltpu.VMEM)
    stay = pl.BlockSpec(memory_space=pl.ANY)
    smem = pl.BlockSpec(memory_space=pltpu.SMEM)
    scratch = [
        pltpu.VMEM((OWN, CH), BF),
        pltpu.VMEM((8, CH), F32),
        pltpu.VMEM((LAYERS, GROWS, LANES), BF),
        pltpu.SemaphoreType.DMA((8,)),
        pltpu.VMEM((LAYERS, 3, CH, MID), BF),
        pltpu.VMEM((LAYERS, MID, CH), BF),
        pltpu.VMEM((CH, CH), BF),
        pltpu.VMEM((LAYERS, 2, OWN, WIDE), BF),
        pltpu.VMEM((LAYERS, WIDE, CH), BF),
        pltpu.VMEM((WIDE, CH), F32),
        pltpu.VMEM((LAYERS, WIDE, 2 * CH), BF),
        pltpu.VMEM((LAYERS, 2, OWN, CH), BF),
        pltpu.VMEM((LAYERS, 2, OWN, CH), BF),
        pltpu.VMEM((LAYERS, 2, OWN, CH), F32),
        pltpu.VMEM((LAYERS, 2, OWN, CH), F32),
        pltpu.VMEM((LAYERS, OWN, 128), F32),
        pltpu.VMEM((2, OWN, MID), F32),
        pltpu.VMEM((LAYERS, 2, OWN, MID), F32),
        pltpu.VMEM((LAYERS, 2, OWN, MID), F32),
        pltpu.VMEM((LAYERS, 2, OWN, 128), F32),
        pltpu.VMEM((LAYERS, 2, OWN, MID), BF),
        pltpu.VMEM((2, OWN, CH), F32),
        pltpu.VMEM((OWN, CH), F32),
        pltpu.VMEM((OWN, CH), BF),
        pltpu.VMEM((2 * OWN, CH), BF),
        pltpu.VMEM((LAYERS, WIDE, 2 * MID), BF),
        pltpu.VMEM((2, OWN, MID), BF),
        pltpu.VMEM((2, OWN, MID), BF),
        pltpu.VMEM((OWN, CH), BF),
        pltpu.VMEM((LAYERS, 8, CH), F32),
        pltpu.VMEM((LAYERS, 8, MID), F32),
        pltpu.SemaphoreType.DMA((2,)),
        pltpu.SemaphoreType.DMA((8,)),
        pltpu.SemaphoreType.DMA((8,)),
        pltpu.VMEM((LAYERS, GROWS, LANES), BF),
    ]
    small = [pltpu.VMEM((SMALL, LANES), F32)] + small_scratch()
    return pl.pallas_call(
        step_kernel,
        out_shape=(
            jax.ShapeDtypeStruct((OWN, CH), BF),
            jax.ShapeDtypeStruct((OWN, CH), BF),
            jax.ShapeDtypeStruct((LAYERS, 3 * CH, MID), BF),
            jax.ShapeDtypeStruct((LAYERS, MID, CH), BF),
            jax.ShapeDtypeStruct((4, CH), F32),
            jax.ShapeDtypeStruct((LAYERS, CH), F32),
            jax.ShapeDtypeStruct((LAYERS, MID), F32),
        ),
        in_specs=[smem] + [vmem] * 7 + [stay] * 2,
        out_specs=(stay,) * 4 + (vmem,) * 3,
        scratch_shapes=scratch + total_scratch() * 2 + small,
        compiler_params=pltpu.CompilerParams(collective_id=0, has_side_effects=True, vmem_limit_bytes=56 * 1024 * 1024),
        cost_estimate=pl.CostEstimate(flops=10**10, bytes_accessed=2 * 10**7, transcendentals=0),
        name="step",
    )(dilation, trunk, tokens, table, norm_gain, mid_gain, perm, cotangent, conv_w, out_w)


def widen_kernel(conv_in, out_in, block_in, trunk_in, table_in, gain_in, mid_in,
                 conv_out, out_out, block_out, trunk_out, table_out, gain_out, mid_out):
    conv_out[...] = conv_in[...].astype(F32)
    out_out[...] = out_in[...].astype(F32)
    block_out[...] = block_in[...]
    trunk_out[...] = trunk_in[...]
    table_out[...] = table_in[...]
    gain_out[...] = gain_in[...]
    mid_out[...] = mid_in[...]


def widen(*arrays):
    steps = 4

    def piece(array):
        if array.shape[0] % (steps * 16) == 0:
            return pl.BlockSpec((array.shape[0] // steps, array.shape[1]), lambda i: (i, 0))
        return pl.BlockSpec(array.shape, lambda i: (0, 0))

    specs = [piece(array) for array in arrays]
    return pl.pallas_call(
        widen_kernel,
        grid=(steps,),
        out_shape=[jax.ShapeDtypeStruct(array.shape, F32 if i < 2 else array.dtype) for i, array in enumerate(arrays)],
        in_specs=specs,
        out_specs=specs,
        compiler_params=pltpu.CompilerParams(vmem_limit_bytes=60 * 1024 * 1024),
        cost_estimate=pl.CostEstimate(flops=10**6, bytes_accessed=15 * 10**6, transcendentals=0),
        name="widen",
    )(*arrays)


def shards(trunk_input, tokens, token_table, conv_weight, out_weight, norm_gain, mid_gain, strand_perm, dilation, out_cotangent):
    block_out, trunk_grad, conv_total, out_total, table_total, gain_total, mid_total = whole_step(
        trunk_input[0], tokens, token_table, conv_weight, out_weight, norm_gain, mid_gain, strand_perm, dilation, out_cotangent[0])
    conv_total, out_total, block_out, trunk_grad, table_total, gain_total, mid_total = widen(
        conv_total.reshape(LAYERS * 3 * CH, MID), out_total.reshape(LAYERS * MID, CH), block_out, trunk_grad, table_total, gain_total, mid_total)
    return (block_out[None], trunk_grad[None], table_total, conv_total.reshape(LAYERS, 3, CH, MID),
            out_total.reshape(LAYERS, MID, CH), gain_total, mid_total)


def solution(mesh):
    placed = (P("dp", "ctx", None), P("dp", "ctx"), P(), P(), P(), P(), P(), P(), P(), P("dp", "ctx", None))
    return jax.shard_map(
        shards,
        mesh=mesh,
        in_specs=placed,
        out_specs=(P("dp", "ctx", None), P("dp", "ctx", None), P(), P(), P(), P(), P()),
        check_vma=False,
    )
```

```python
import jax
import jax.numpy as jnp
from jax import lax
from jax.experimental import pallas as pl
from jax.experimental.pallas import tpu as pltpu
from jax.sharding import PartitionSpec as P

LAYERS = 2
DMAX = 64

MESH = pl.DeviceIdType.MESH
GROWS = 3072
HALF = 1536
QUARTER = 384
EIGHTH = 96
SMALL = 16
LANES = 384


def place(core, y, z, x):
    return (lax.div(y, 2) * 2 + core, (lax.rem(y, 2) * 4 + z) * 4 + x)


def coordinates():
    dp = lax.axis_index("dp")
    ctx = lax.axis_index("ctx")
    y = lax.div(dp, 2) * 2 + lax.div(ctx, 16)
    return (lax.rem(dp, 2), y, lax.rem(lax.div(ctx, 4), 4), lax.rem(ctx, 4))


def ring_peer(spot, axis, distance):
    moved = list(spot)
    moved[axis] = lax.rem(spot[axis] + distance, 4)
    return place(*moved)


def core_peer(spot):
    return place(1 - spot[0], *spot[1:])


ORDERS = ((3, 1, 2), (1, 2, 3), (2, 3, 1))


class Copies:
    def __init__(self, send, recv):
        self.send, self.recv, self.open = send, recv, []

    def start(self, index, source, target, device):
        copy = pltpu.make_async_remote_copy(
            src_ref=source, dst_ref=target, send_sem=self.send.at[index],
            recv_sem=self.recv.at[index], device_id=device, device_id_type=MESH)
        copy.start()
        return copy


class Total:
    def __init__(self, spot, grads, result, core_in, sums0, in_a, sums1, in_b, sums2, in_c, send, recv):
        self.spot, self.grads, self.result = spot, grads, result
        self.core_in, self.sums0, self.in_a, self.sums1 = core_in, sums0, in_a, sums1
        self.in_b, self.sums2, self.in_c = in_b, sums2, in_c
        self.copies = Copies(send, recv)
        self.base = spot[0] * HALF

    def lanes(self, third):
        return pl.ds(third * 128, 128)

    def core_start(self):
        other = (1 - self.spot[0]) * HALF
        self.core = self.copies.start(0, self.grads.at[pl.ds(other, HALF)], self.core_in, core_peer(self.spot))

    def core_finish(self):
        self.core.wait()

        def body(step, carry):
            rows = pl.ds(pl.multiple_of(step * QUARTER, 32), QUARTER)
            mine = pl.ds(pl.multiple_of(self.base + step * QUARTER, 32), QUARTER)
            self.sums0[rows] = (self.grads[mine].astype(jnp.float32) + self.core_in[rows].astype(jnp.float32)).astype(jnp.bfloat16)
            return carry

        lax.fori_loop(0, 4, body, 0)

    def a_start(self):
        self.a = []
        for third, order in enumerate(ORDERS):
            for distance in (2, 1, 3):
                chunk = lax.rem(self.spot[order[0]] + distance, 4)
                self.a.append(self.copies.start(
                    1 + third * 3 + distance - 1,
                    self.sums0.at[pl.ds(chunk * QUARTER, QUARTER), self.lanes(third)],
                    self.in_a.at[third, distance - 1], ring_peer(self.spot, order[0], distance)))

    def a_to_b(self):
        self.b = []
        for third, order in enumerate(ORDERS):
            mine = pl.ds(pl.multiple_of(self.spot[order[0]] * QUARTER, 32), QUARTER)
            for copy in self.a[third * 3:third * 3 + 3]:
                copy.wait()
            total = self.sums0[mine, self.lanes(third)].astype(jnp.float32)
            for slot in range(3):
                total = total + self.in_a[third, slot].astype(jnp.float32)
            self.sums1[third] = total.astype(jnp.bfloat16)
            for distance in (2, 1, 3):
                chunk = lax.rem(self.spot[order[1]] + distance, 4)
                self.b.append(self.copies.start(
                    10 + third * 3 + distance - 1,
                    self.sums1.at[third, pl.ds(chunk * EIGHTH, EIGHTH)],
                    self.in_b.at[third, distance - 1], ring_peer(self.spot, order[1], distance)))

    def b_to_c(self):
        self.c = []
        for third, order in enumerate(ORDERS):
            mine = pl.ds(pl.multiple_of(self.spot[order[1]] * EIGHTH, 32), EIGHTH)
            for copy in self.b[third * 3:third * 3 + 3]:
                copy.wait()
            total = self.sums1[third, mine].astype(jnp.float32)
            for slot in range(3):
                total = total + self.in_b[third, slot].astype(jnp.float32)
            self.sums2[third] = total.astype(jnp.bfloat16)
            for distance in (2, 1, 3):
                self.c.append(self.copies.start(
                    19 + third * 3 + distance - 1, self.sums2.at[third],
                    self.in_c.at[third, self.spot[order[2]]], ring_peer(self.spot, order[2], distance)))
            self.in_c[third, self.spot[order[2]]] = self.sums2[third]

    def rows_of(self, third):
        order = ORDERS[third]
        quarter = self.base + self.spot[order[0]] * QUARTER
        return quarter, quarter + self.spot[order[1]] * EIGHTH

    def spread(self, third, which):
        order = ORDERS[third]
        quarter, eighth = self.rows_of(third)
        rows = pl.ds(eighth, EIGHTH) if which else pl.ds(quarter, QUARTER)
        piece = self.result.at[rows, self.lanes(third)]
        return [
            self.copies.start(28 + which * 9 + third * 3 + distance - 1, piece, piece, ring_peer(self.spot, order[which], distance))
            for distance in (1, 3, 2)]

    def c_to_gather(self):
        self.early = []
        for third in range(3):
            for copy in self.c[third * 3:third * 3 + 3]:
                copy.wait()
            total = self.in_c[third, 0].astype(jnp.float32)
            for slot in range(1, 4):
                total = total + self.in_c[third, slot].astype(jnp.float32)
            _, eighth = self.rows_of(third)
            self.result[pl.ds(pl.multiple_of(eighth, 32), EIGHTH), self.lanes(third)] = total.astype(jnp.bfloat16)
            self.early += self.spread(third, 1)

    def pass_on(self, third, distance):
        quarter = lax.rem(self.spot[ORDERS[third][0]] + 4 - distance, 4)
        piece = self.result.at[pl.ds(self.base + quarter * QUARTER, QUARTER), self.lanes(third)]
        self.last.append(self.copies.start(46 + third * 4 + distance, piece, piece, core_peer(self.spot)))

    def a_gather(self):
        self.late, self.last = [], []
        for third in range(3):
            for copy in self.early[third * 3:third * 3 + 3]:
                copy.wait()
            self.late += self.spread(third, 0)
        for third in range(3):
            self.pass_on(third, 0)

    def forward(self):
        for slot, distance in enumerate((1, 3, 2)):
            for third in range(3):
                self.late[third * 3 + slot].wait()
                self.pass_on(third, distance)

    def finish(self):
        for copy in self.last:
            copy.wait()


TOTAL_COPIES = 58


def total_scratch():
    return [
        pltpu.VMEM((HALF, LANES), jnp.bfloat16),
        pltpu.VMEM((HALF, LANES), jnp.bfloat16),
        pltpu.VMEM((3, 3, QUARTER, 128), jnp.bfloat16),
        pltpu.VMEM((3, QUARTER, 128), jnp.bfloat16),
        pltpu.VMEM((3, 3, EIGHTH, 128), jnp.bfloat16),
        pltpu.VMEM((3, EIGHTH, 128), jnp.bfloat16),
        pltpu.VMEM((3, 4, EIGHTH, 128), jnp.bfloat16),
        pltpu.SemaphoreType.DMA((TOTAL_COPIES,)),
        pltpu.SemaphoreType.DMA((TOTAL_COPIES,)),
    ]


class Small:
    def __init__(self, spot, value, core_in, ring_in, send, recv):
        self.spot, self.value, self.core_in, self.ring_in = spot, value, core_in, ring_in
        self.copies = Copies(send, recv)

    def core_start(self):
        self.core = self.copies.start(0, self.value, self.core_in, core_peer(self.spot))

    def core_finish(self):
        self.core.wait()
        own = self.spot[3]
        self.ring_in[0, own] = self.value[...] + self.core_in[...]

    def ring_start(self, stage):
        axis = (3, 1, 2)[stage]
        own = self.spot[axis]
        self.ring = [
            self.copies.start(1 + stage * 3 + distance - 1, self.ring_in.at[stage, own], self.ring_in.at[stage, own],
                              ring_peer(self.spot, axis, distance)) for distance in (2, 1, 3)]

    def ring_finish(self, stage):
        for copy in self.ring:
            copy.wait()
        total = self.ring_in[stage, 0] + self.ring_in[stage, 1] + self.ring_in[stage, 2] + self.ring_in[stage, 3]
        if stage < 2:
            self.ring_in[stage + 1, self.spot[(3, 1, 2)[stage + 1]]] = total
        return total


def small_scratch():
    return [
        pltpu.VMEM((SMALL, LANES), jnp.float32),
        pltpu.VMEM((3, 4, SMALL, LANES), jnp.float32),
        pltpu.SemaphoreType.DMA((10,)),
        pltpu.SemaphoreType.DMA((10,)),
    ]


def greet(spot, extra=()):
    barrier = pltpu.get_barrier_semaphore()
    peers = [core_peer(spot)] + [ring_peer(spot, axis, distance) for axis in (1, 2, 3) for distance in (1, 2, 3)]
    peers += list(extra)
    for peer in peers:
        pl.semaphore_signal(barrier, inc=1, device_id=peer, device_id_type=MESH)
    return lambda: pl.semaphore_wait(barrier, len(peers))


epsilon = 1e-05
OWN = 256
WIDE = OWN + 2 * DMAX
CH = 768
MID = 384
TILE = 64
BF = jnp.bfloat16
F32 = jnp.float32


def dot(left, right):
    return jnp.dot(left, right, preferred_element_type=F32)


def dot_t(left, right):
    return lax.dot_general(left, right, (((1,), (1,)), ((), ())), preferred_element_type=F32)


def dot_rows(left, right):
    return lax.dot_general(left, right, (((0,), (0,)), ((), ())), preferred_element_type=F32)


def strand(s, width=CH):
    return pl.ds(s * width, width)


def loop(count, body):
    def step(index, carry):
        body(index)
        return carry

    lax.fori_loop(0, count, step, 0, unroll=2 if count % 2 == 0 else 1)


def tile_at(index, base=0, size=TILE):
    return pl.ds(pl.multiple_of(base + index * size, size), size)


def standard(values):
    centre = jnp.mean(values, axis=-1, keepdims=True)
    shifted = values - centre
    scale = lax.rsqrt(jnp.mean(shifted * shifted, axis=-1, keepdims=True) + epsilon)
    return shifted * scale, centre, scale


def gelu_pair(z):
    size = 1.0 + 0.23164189 * jnp.abs(z)
    t = pl.reciprocal(size, approx=True)
    t = t * (2.0 - size * t)
    bell = jnp.exp(-0.5 * z * z)
    tail = t * (0.127414796 + t * (-0.142248368 + t * (0.7107068705 + t * (-0.7265760135 + t * 0.5307027145))))
    tail = tail * bell
    below = jnp.where(z >= 0.0, 1.0 - tail, tail)
    return z * below, below + z * (0.3989422804014327 * bell)


def norm_back(dz, hat, scale, gain):
    dhat = dz * gain
    return scale * (
        dhat - jnp.mean(dhat, axis=-1, keepdims=True) - hat * jnp.mean(dhat * hat, axis=-1, keepdims=True)
    )


def fold(values):
    return values.reshape(TILE // 8, 8, values.shape[-1]).sum(axis=0)


def step_kernel(
    dilation, trunk, tokens, table, norm_gain, mid_gain, perm, cotangent, conv_hbm, out_hbm,
    block_hbm, trunk_hbm, conv_grads, out_grads, table_grad, gain_grad, mid_grad,
    block_out, table_pad, result, result_sem,
    conv_w, out_w, matrix, move, hidden, relabelled, u_pad, u_low, u_high, hat, slope, scale, mid,
    mid_hat, mid_slope, mid_scale, q, wide, back, rounded, e, dm_pad, dm_low, dm_high, grad, gain_acc, mid_acc,
    weight_sem, halo_send, halo_recv, grads, *scratch,
):
    spot = coordinates()
    dp = lax.axis_index("dp")
    ctx = lax.axis_index("ctx")
    left = (dp, lax.rem(ctx + 31, 32))
    right = (dp, lax.rem(ctx + 1, 32))
    first_bin = jnp.where(ctx == 0, DMAX, 0)
    end_bin = jnp.where(ctx == 31, DMAX + OWN, WIDE)
    met = greet(spot, (left, right))
    weights = [
        pltpu.make_async_copy(conv_hbm, conv_w, weight_sem.at[0]),
        pltpu.make_async_copy(out_hbm, out_w, weight_sem.at[1]),
    ]
    for copy in weights:
        copy.start()
    each = len(total_scratch())
    totals = [Total(spot, grads.at[b], result.at[b], *scratch[b * each:(b + 1) * each]) for b in range(LAYERS)]
    small = Small(spot, *scratch[2 * each:])
    halos = Copies(halo_send, halo_recv)

    def trade(index, mine):
        return [
            halos.start(2 * index, mine.at[pl.ds(DMAX, DMAX)], mine.at[pl.ds(DMAX + OWN, DMAX)], left),
            halos.start(2 * index + 1, mine.at[pl.ds(OWN, DMAX)], mine.at[pl.ds(0, DMAX)], right),
        ]

    leaving = []

    def leave(source, target):
        copy = pltpu.make_async_copy(source, target, result_sem.at[len(leaving)])
        copy.start()
        leaving.append(copy)

    def leave_sums(b):
        leave(result.at[b, pl.ds(0, 2304)], conv_grads.at[b])
        for s in range(2):
            leave(result.at[b, pl.ds(2304 + s * MID, MID)], out_grads.at[b, :, strand(s, MID)])

    table_pad[...] = jnp.zeros_like(table_pad)
    rest = table[...]
    for part in range(3):
        piece = rest.astype(BF).astype(F32)
        table_pad[pl.ds(8 * part, 4)] = piece
        rest = rest - piece
    one_hot = (tokens[...] == lax.broadcasted_iota(jnp.int32, (8, OWN), 0)).astype(F32)
    three_hot = jnp.concatenate([one_hot] * 4, axis=0).astype(BF)
    added = dot_rows(three_hot, table_pad[...].astype(BF))
    hidden[0, pl.ds(DMAX, OWN)] = (trunk[...].astype(F32) + added).astype(BF)
    met()
    pending = trade(0, hidden.at[0])

    def fill_matrix(index):
        rows = tile_at(index)
        channel = lax.broadcasted_iota(jnp.int32, (TILE, CH), 0) + index * TILE
        matrix[rows] = jnp.where(channel == perm[...][None, :], 1.0, 0.0).astype(BF)

    loop(CH // TILE, fill_matrix)
    bin_from = lax.broadcasted_iota(jnp.int32, (OWN, WIDE), 1)
    bin_to = lax.broadcasted_iota(jnp.int32, (OWN, WIDE), 0) + DMAX
    inside = (bin_from >= first_bin) & (bin_from < end_bin)
    for b in range(LAYERS):
        for way in range(2):
            at = bin_to + (2 * way - 1) * dilation[b]
            move[b, way] = jnp.where(inside & (bin_from == at), 1.0, 0.0).astype(BF)
    e[pl.ds(0, OWN)] = (0.5 * cotangent[...].astype(F32)).astype(BF)

    for b in range(LAYERS):
        gain = norm_gain[pl.ds(b, 1)]
        mid_s = mid_gain[pl.ds(b, 1)]

        def front(rows, own):
            x = hidden[b, rows].astype(F32)
            hat_f, centre, inv = standard(x)
            hat_r = (relabelled[rows] - centre) * inv
            for s, normed in enumerate((hat_f, hat_r)):
                u, du = gelu_pair(normed * gain)
                u_pad[b, rows, strand(s)] = u.astype(BF)
                if own is not None:
                    hat[b, s, own] = normed
                    slope[b, s, own] = du
            if own is not None:
                scale[b, own] = jnp.broadcast_to(inv, (TILE, 128))

        relabelled[pl.ds(DMAX, OWN)] = dot(hidden[b, pl.ds(DMAX, OWN)], matrix[...])
        loop(OWN // TILE, lambda i: front(tile_at(i, DMAX), tile_at(i)))
        if b == 0:
            for copy in weights:
                copy.wait()
        for s in range(2):
            mid[s] = dot(u_pad[b, pl.ds(DMAX, OWN), strand(s)], conv_w[b, 1])
        for copy in pending:
            copy.wait()
        for base in (0, DMAX + OWN):
            relabelled[pl.ds(base, DMAX)] = dot(hidden[b, pl.ds(base, DMAX)], matrix[...])
            loop(DMAX // TILE, lambda i: front(tile_at(i, base), None))

        for s in range(2):
            u_low[b, s] = dot(move[b, s], u_pad[b, :, strand(s)]).astype(BF)
            u_high[b, s] = dot(move[b, 1 - s], u_pad[b, :, strand(s)]).astype(BF)
        for s in range(2):
            mid[s] += dot(u_low[b, s], conv_w[b, 0]) + dot(u_high[b, s], conv_w[b, 2])

        def middle(i):
            rows = tile_at(i)
            for s in range(2):
                normed, _, inv = standard(mid[s, rows])
                value, derivative = gelu_pair(normed * mid_s)
                q[b, s, rows] = value.astype(BF)
                mid_hat[b, s, rows] = normed
                mid_slope[b, s, rows] = derivative
                mid_scale[b, s, rows] = jnp.broadcast_to(inv, (TILE, 128))

        loop(OWN // TILE, middle)
        rounded[...] = dot(q[b, 1], out_w[b]).astype(BF)
        wide[0] = dot(q[b, 0], out_w[b])
        back[...] = dot_t(rounded[...], matrix[...])

        def join(i):
            rows = tile_at(i)
            total = wide[0, rows].astype(BF).astype(F32) + back[rows]
            following = (hidden[b, tile_at(i, DMAX)].astype(F32) + 0.5 * total).astype(BF)
            if b + 1 < LAYERS:
                hidden[b + 1, tile_at(i, DMAX)] = following
            else:
                block_out[rows] = following

        loop(OWN // TILE, join)
        if b + 1 < LAYERS:
            pending = trade(b + 1, hidden.at[b + 1])

    leave(block_out, block_hbm)
    grad[...] = cotangent[...]
    gain_acc[...] = jnp.zeros_like(gain_acc)
    mid_acc[...] = jnp.zeros_like(mid_acc)
    for b in (1, 0):
        gain = norm_gain[pl.ds(b, 1)]
        mid_s = mid_gain[pl.ds(b, 1)]
        sums = grads.at[b]
        if b == 0:
            e[pl.ds(0, OWN)] = (0.5 * grad[...].astype(F32)).astype(BF)
        e[pl.ds(OWN, OWN)] = dot(e[pl.ds(0, OWN)], matrix[...]).astype(BF)
        for s in range(2):
            mid[s] = dot_t(e[pl.ds(s * OWN, OWN)], out_w[b])

        def middle_back(i):
            rows = tile_at(i)
            total = jnp.zeros((8, MID), F32)
            for s in range(2):
                dz = mid[s, rows] * mid_slope[b, s, rows]
                normed = mid_hat[b, s, rows]
                total = total + fold(dz * normed)
                dm = norm_back(dz, normed, mid_scale[b, s, rows, 0:1], mid_s)
                dm_pad[b, tile_at(i, DMAX), strand(s, MID)] = dm.astype(BF)
            mid_acc[b] += total

        loop(OWN // TILE, middle_back)
        pending = trade(LAYERS + b, dm_pad.at[b])
        q_all = q[b].reshape(2 * OWN, MID)
        out_grad = dot_rows(q_all, e[...])
        sums[pl.ds(2304, MID)] = out_grad[:, :MID].astype(BF)
        sums[pl.ds(2688, MID)] = out_grad[:, MID:].astype(BF)
        own = pl.ds(DMAX, OWN)
        u_all = jnp.concatenate([u_pad[b, own, strand(s)] for s in range(2)], axis=0)
        dm_all = jnp.concatenate([dm_pad[b, own, strand(s, MID)] for s in range(2)], axis=0)
        for tap, left_side in enumerate((u_low[b].reshape(2 * OWN, CH), u_all, u_high[b].reshape(2 * OWN, CH))):
            sums[pl.ds(tap * CH, CH)] = dot_rows(left_side, dm_all).astype(BF)
        totals[b].core_start()
        for s in range(2):
            wide[s] = dot_t(dm_pad[b, own, strand(s, MID)], conv_w[b, 1])
        if b == 0:
            totals[1].a_to_b()
        for copy in pending:
            copy.wait()
        for s in range(2):
            dm_low[s] = dot(move[b, 1 - s], dm_pad[b, :, strand(s, MID)]).astype(BF)
            dm_high[s] = dot(move[b, s], dm_pad[b, :, strand(s, MID)]).astype(BF)
        for s in range(2):
            wide[s] += dot_t(dm_low[s], conv_w[b, 0]) + dot_t(dm_high[s], conv_w[b, 2])
        totals[b].core_finish()
        totals[b].a_start()
        if b == 0:
            totals[1].b_to_c()

        def front_back(i):
            rows = tile_at(i)
            total = jnp.zeros((8, CH), F32)
            for s in range(2):
                dz = wide[s, rows] * slope[b, s, rows]
                normed = hat[b, s, rows]
                total = total + fold(dz * normed)
                dx = norm_back(dz, normed, scale[b, rows, 0:1], gain)
                if s == 0:
                    wide[0, rows] = dx
                else:
                    rounded[rows] = dx.astype(BF)
            gain_acc[b] += total

        loop(OWN // TILE, front_back)
        back[...] = dot_t(rounded[...], matrix[...])

        def join_back(i):
            rows = tile_at(i)
            total = grad[rows].astype(F32) + wide[0, rows].astype(BF).astype(F32) + back[rows]
            grad[rows] = total.astype(BF)

        loop(OWN // TILE, join_back)

    leave(grad, trunk_hbm)
    table_term = dot(one_hot.astype(BF), grad[...])
    small.value[pl.ds(0, 4)] = table_term[0:4, :MID]
    small.value[pl.ds(4, 4)] = table_term[0:4, MID:]
    for b in range(LAYERS):
        term = jnp.sum(gain_acc[b], axis=0, keepdims=True)
        small.value[pl.ds(8 + 2 * b, 1)] = term[:, :MID]
        small.value[pl.ds(9 + 2 * b, 1)] = term[:, MID:]
        small.value[pl.ds(12 + b, 1)] = jnp.sum(mid_acc[b], axis=0, keepdims=True)
    small.value[pl.ds(14, 2)] = jnp.zeros((2, MID), F32)
    small.core_start()
    totals[1].c_to_gather()
    totals[0].a_to_b()
    small.core_finish()
    small.ring_start(0)
    totals[1].a_gather()
    totals[0].b_to_c()
    small.ring_finish(0)
    small.ring_start(1)
    totals[0].c_to_gather()
    totals[1].forward()
    small.ring_finish(1)
    small.ring_start(2)
    totals[0].a_gather()
    totals[1].finish()
    leave_sums(1)
    sums = small.ring_finish(2)
    table_grad[:, pl.ds(0, MID)] = sums[0:4]
    table_grad[:, pl.ds(MID, MID)] = sums[4:8]
    for b in range(LAYERS):
        gain_grad[pl.ds(b, 1), pl.ds(0, MID)] = sums[8 + 2 * b:9 + 2 * b]
        gain_grad[pl.ds(b, 1), pl.ds(MID, MID)] = sums[9 + 2 * b:10 + 2 * b]
    mid_grad[...] = sums[12:14]
    totals[0].forward()
    totals[0].finish()
    leave_sums(0)
    for copy in leaving:
        copy.wait()


def whole_step(trunk, tokens, table, conv_w, out_w, norm_gain, mid_gain, perm, dilation, cotangent):
    vmem = pl.BlockSpec(memory_space=pltpu.VMEM)
    stay = pl.BlockSpec(memory_space=pl.ANY)
    smem = pl.BlockSpec(memory_space=pltpu.SMEM)
    scratch = [
        pltpu.VMEM((OWN, CH), BF),
        pltpu.VMEM((32, CH), F32),
        pltpu.VMEM((LAYERS, GROWS, LANES), BF),
        pltpu.SemaphoreType.DMA((8,)),
        pltpu.VMEM((LAYERS, 3, CH, MID), BF),
        pltpu.VMEM((LAYERS, MID, CH), BF),
        pltpu.VMEM((CH, CH), BF),
        pltpu.VMEM((LAYERS, 2, OWN, WIDE), BF),
        pltpu.VMEM((LAYERS, WIDE, CH), BF),
        pltpu.VMEM((WIDE, CH), F32),
        pltpu.VMEM((LAYERS, WIDE, 2 * CH), BF),
        pltpu.VMEM((LAYERS, 2, OWN, CH), BF),
        pltpu.VMEM((LAYERS, 2, OWN, CH), BF),
        pltpu.VMEM((LAYERS, 2, OWN, CH), F32),
        pltpu.VMEM((LAYERS, 2, OWN, CH), F32),
        pltpu.VMEM((LAYERS, OWN, 128), F32),
        pltpu.VMEM((2, OWN, MID), F32),
        pltpu.VMEM((LAYERS, 2, OWN, MID), F32),
        pltpu.VMEM((LAYERS, 2, OWN, MID), F32),
        pltpu.VMEM((LAYERS, 2, OWN, 128), F32),
        pltpu.VMEM((LAYERS, 2, OWN, MID), BF),
        pltpu.VMEM((2, OWN, CH), F32),
        pltpu.VMEM((OWN, CH), F32),
        pltpu.VMEM((OWN, CH), BF),
        pltpu.VMEM((2 * OWN, CH), BF),
        pltpu.VMEM((LAYERS, WIDE, 2 * MID), BF),
        pltpu.VMEM((2, OWN, MID), BF),
        pltpu.VMEM((2, OWN, MID), BF),
        pltpu.VMEM((OWN, CH), BF),
        pltpu.VMEM((LAYERS, 8, CH), F32),
        pltpu.VMEM((LAYERS, 8, MID), F32),
        pltpu.SemaphoreType.DMA((2,)),
        pltpu.SemaphoreType.DMA((8,)),
        pltpu.SemaphoreType.DMA((8,)),
        pltpu.VMEM((LAYERS, GROWS, LANES), BF),
    ]
    small = [pltpu.VMEM((SMALL, LANES), F32)] + small_scratch()
    return pl.pallas_call(
        step_kernel,
        out_shape=(
            jax.ShapeDtypeStruct((OWN, CH), BF),
            jax.ShapeDtypeStruct((OWN, CH), BF),
            jax.ShapeDtypeStruct((LAYERS, 3 * CH, MID), BF),
            jax.ShapeDtypeStruct((LAYERS, MID, CH), BF),
            jax.ShapeDtypeStruct((4, CH), F32),
            jax.ShapeDtypeStruct((LAYERS, CH), F32),
            jax.ShapeDtypeStruct((LAYERS, MID), F32),
        ),
        in_specs=[smem] + [vmem] * 7 + [stay] * 2,
        out_specs=(stay,) * 4 + (vmem,) * 3,
        scratch_shapes=scratch + total_scratch() * 2 + small,
        compiler_params=pltpu.CompilerParams(collective_id=0, has_side_effects=True, vmem_limit_bytes=56 * 1024 * 1024),
        cost_estimate=pl.CostEstimate(flops=10**10, bytes_accessed=2 * 10**7, transcendentals=0),
        name="step",
    )(dilation, trunk, tokens, table, norm_gain, mid_gain, perm, cotangent, conv_w, out_w)


CONV_PIECES = 9
OUT_PIECES = 3


def widen_kernel(conv_in, out_in, block_in, trunk_in, table_in, gain_in, mid_in,
                 conv_out, out_out, block_out, trunk_out, table_out, gain_out, mid_out,
                 conv_narrow, out_narrow, conv_wide, out_wide, block_held, trunk_held, table_held, gain_held, mid_held,
                 in_sem, back_sem):
    work = []
    for source, target, narrow, broad, pieces in (
            (conv_in, conv_out, conv_narrow, conv_wide, CONV_PIECES), (out_in, out_out, out_narrow, out_wide, OUT_PIECES)):
        size = source.shape[0] // pieces
        for i in range(pieces):
            rows = pl.ds(i * size, size)
            index = len(work)
            work.append((
                pltpu.make_async_copy(source.at[rows], narrow.at[rows], in_sem.at[index]),
                pltpu.make_async_copy(broad.at[rows], target.at[rows], back_sem.at[index]),
                narrow, broad, rows))
    for source, target, held in (
            (block_in, block_out, block_held), (trunk_in, trunk_out, trunk_held), (table_in, table_out, table_held),
            (gain_in, gain_out, gain_held), (mid_in, mid_out, mid_held)):
        index = len(work)
        work.append((
            pltpu.make_async_copy(source, held, in_sem.at[index]),
            pltpu.make_async_copy(held, target, back_sem.at[index]), None, None, None))
    for fetch, *_ in work:
        fetch.start()
    for fetch, store, narrow, broad, rows in work:
        fetch.wait()
        if narrow is not None:
            broad[rows] = narrow[rows].astype(F32)
        store.start()
    for _, store, *_ in work:
        store.wait()


def widen(*arrays):
    stay = pl.BlockSpec(memory_space=pl.ANY)
    conv, out = arrays[:2]
    return pl.pallas_call(
        widen_kernel,
        out_shape=[jax.ShapeDtypeStruct(array.shape, F32 if i < 2 else array.dtype) for i, array in enumerate(arrays)],
        in_specs=[stay] * len(arrays),
        out_specs=[stay] * len(arrays),
        scratch_shapes=[
            pltpu.VMEM(conv.shape, BF), pltpu.VMEM(out.shape, BF), pltpu.VMEM(conv.shape, F32), pltpu.VMEM(out.shape, F32),
            *[pltpu.VMEM(array.shape, array.dtype) for array in arrays[2:]],
            pltpu.SemaphoreType.DMA((CONV_PIECES + OUT_PIECES + 5,)), pltpu.SemaphoreType.DMA((CONV_PIECES + OUT_PIECES + 5,)),
        ],
        compiler_params=pltpu.CompilerParams(vmem_limit_bytes=60 * 1024 * 1024),
        cost_estimate=pl.CostEstimate(flops=10**6, bytes_accessed=15 * 10**6, transcendentals=0),
        name="widen",
    )(*arrays)


def shards(trunk_input, tokens, token_table, conv_weight, out_weight, norm_gain, mid_gain, strand_perm, dilation, out_cotangent):
    block_out, trunk_grad, conv_total, out_total, table_total, gain_total, mid_total = whole_step(
        trunk_input[0], tokens, token_table, conv_weight, out_weight, norm_gain, mid_gain, strand_perm, dilation, out_cotangent[0])
    conv_total, out_total, block_out, trunk_grad, table_total, gain_total, mid_total = widen(
        conv_total.reshape(LAYERS * 3 * CH, MID), out_total.reshape(LAYERS * MID, CH), block_out, trunk_grad, table_total, gain_total, mid_total)
    return (block_out[None], trunk_grad[None], table_total, conv_total.reshape(LAYERS, 3, CH, MID),
            out_total.reshape(LAYERS, MID, CH), gain_total, mid_total)


def solution(mesh):
    placed = (P("dp", "ctx", None), P("dp", "ctx"), P(), P(), P(), P(), P(), P(), P(), P("dp", "ctx", None))
    return jax.shard_map(
        shards,
        mesh=mesh,
        in_specs=placed,
        out_specs=(P("dp", "ctx", None), P("dp", "ctx", None), P(), P(), P(), P(), P()),
        check_vma=False,
    )
```

```python
import jax
import jax.numpy as jnp
from jax import lax
from jax.experimental import pallas as pl
from jax.experimental.pallas import tpu as pltpu
from jax.sharding import PartitionSpec as P

LAYERS = 2
DMAX = 64

MESH = pl.DeviceIdType.MESH
GROWS = 3072
HALF = 1536
QUARTER = 384
EIGHTH = 96
SMALL = 16
LANES = 384


def place(core, y, z, x):
    return (lax.div(y, 2) * 2 + core, (lax.rem(y, 2) * 4 + z) * 4 + x)


def coordinates():
    dp = lax.axis_index("dp")
    ctx = lax.axis_index("ctx")
    y = lax.div(dp, 2) * 2 + lax.div(ctx, 16)
    return (lax.rem(dp, 2), y, lax.rem(lax.div(ctx, 4), 4), lax.rem(ctx, 4))


def ring_peer(spot, axis, distance):
    moved = list(spot)
    moved[axis] = lax.rem(spot[axis] + distance, 4)
    return place(*moved)


def core_peer(spot):
    return place(1 - spot[0], *spot[1:])


ORDERS = ((3, 1, 2), (1, 2, 3), (2, 3, 1))


class Copies:
    def __init__(self, send, recv):
        self.send, self.recv, self.open = send, recv, []

    def start(self, index, source, target, device):
        copy = pltpu.make_async_remote_copy(
            src_ref=source, dst_ref=target, send_sem=self.send.at[index],
            recv_sem=self.recv.at[index], device_id=device, device_id_type=MESH)
        copy.start()
        return copy


class Total:
    def __init__(self, spot, grads, result, core_in, sums0, in_a, sums1, in_b, sums2, in_c, send, recv):
        self.spot, self.grads, self.result = spot, grads, result
        self.core_in, self.sums0, self.in_a, self.sums1 = core_in, sums0, in_a, sums1
        self.in_b, self.sums2, self.in_c = in_b, sums2, in_c
        self.copies = Copies(send, recv)
        self.base = spot[0] * HALF

    def lanes(self, third):
        return pl.ds(third * 128, 128)

    def core_start(self):
        other = (1 - self.spot[0]) * HALF
        self.core = self.copies.start(0, self.grads.at[pl.ds(other, HALF)], self.core_in, core_peer(self.spot))

    def core_finish(self):
        self.core.wait()

        def body(step, carry):
            rows = pl.ds(pl.multiple_of(step * QUARTER, 32), QUARTER)
            mine = pl.ds(pl.multiple_of(self.base + step * QUARTER, 32), QUARTER)
            self.sums0[rows] = (self.grads[mine].astype(jnp.float32) + self.core_in[rows].astype(jnp.float32)).astype(jnp.bfloat16)
            return carry

        lax.fori_loop(0, 4, body, 0)

    def a_start(self):
        self.a = []
        for third, order in enumerate(ORDERS):
            for distance in (2, 1, 3):
                chunk = lax.rem(self.spot[order[0]] + distance, 4)
                self.a.append(self.copies.start(
                    1 + third * 3 + distance - 1,
                    self.sums0.at[pl.ds(chunk * QUARTER, QUARTER), self.lanes(third)],
                    self.in_a.at[third, distance - 1], ring_peer(self.spot, order[0], distance)))

    def a_to_b(self):
        self.b = []
        for third, order in enumerate(ORDERS):
            mine = pl.ds(pl.multiple_of(self.spot[order[0]] * QUARTER, 32), QUARTER)
            for copy in self.a[third * 3:third * 3 + 3]:
                copy.wait()
            total = self.sums0[mine, self.lanes(third)].astype(jnp.float32)
            for slot in range(3):
                total = total + self.in_a[third, slot].astype(jnp.float32)
            self.sums1[third] = total.astype(jnp.bfloat16)
            for distance in (2, 1, 3):
                chunk = lax.rem(self.spot[order[1]] + distance, 4)
                self.b.append(self.copies.start(
                    10 + third * 3 + distance - 1,
                    self.sums1.at[third, pl.ds(chunk * EIGHTH, EIGHTH)],
                    self.in_b.at[third, distance - 1], ring_peer(self.spot, order[1], distance)))

    def b_to_c(self):
        self.c = []
        for third, order in enumerate(ORDERS):
            mine = pl.ds(pl.multiple_of(self.spot[order[1]] * EIGHTH, 32), EIGHTH)
            for copy in self.b[third * 3:third * 3 + 3]:
                copy.wait()
            total = self.sums1[third, mine].astype(jnp.float32)
            for slot in range(3):
                total = total + self.in_b[third, slot].astype(jnp.float32)
            self.sums2[third] = total.astype(jnp.bfloat16)
            for distance in (2, 1, 3):
                self.c.append(self.copies.start(
                    19 + third * 3 + distance - 1, self.sums2.at[third],
                    self.in_c.at[third, self.spot[order[2]]], ring_peer(self.spot, order[2], distance)))
            self.in_c[third, self.spot[order[2]]] = self.sums2[third]

    def rows_of(self, third):
        order = ORDERS[third]
        quarter = self.base + self.spot[order[0]] * QUARTER
        return quarter, quarter + self.spot[order[1]] * EIGHTH

    def spread(self, third, which):
        order = ORDERS[third]
        quarter, eighth = self.rows_of(third)
        rows = pl.ds(eighth, EIGHTH) if which else pl.ds(quarter, QUARTER)
        piece = self.result.at[rows, self.lanes(third)]
        return [
            self.copies.start(28 + which * 9 + third * 3 + distance - 1, piece, piece, ring_peer(self.spot, order[which], distance))
            for distance in (1, 3, 2)]

    def c_to_gather(self):
        self.early = []
        for third in range(3):
            for copy in self.c[third * 3:third * 3 + 3]:
                copy.wait()
            total = self.in_c[third, 0].astype(jnp.float32)
            for slot in range(1, 4):
                total = total + self.in_c[third, slot].astype(jnp.float32)
            _, eighth = self.rows_of(third)
            self.result[pl.ds(pl.multiple_of(eighth, 32), EIGHTH), self.lanes(third)] = total.astype(jnp.bfloat16)
            self.early += self.spread(third, 1)

    def pass_on(self, third, distance):
        quarter = lax.rem(self.spot[ORDERS[third][0]] + 4 - distance, 4)
        piece = self.result.at[pl.ds(self.base + quarter * QUARTER, QUARTER), self.lanes(third)]
        self.last.append(self.copies.start(46 + third * 4 + distance, piece, piece, core_peer(self.spot)))

    def a_gather(self):
        self.late, self.last = [], []
        for third in range(3):
            for copy in self.early[third * 3:third * 3 + 3]:
                copy.wait()
            self.late += self.spread(third, 0)
        for third in range(3):
            self.pass_on(third, 0)

    def forward(self):
        for slot, distance in enumerate((1, 3, 2)):
            for third in range(3):
                self.late[third * 3 + slot].wait()
                self.pass_on(third, distance)

    def finish(self):
        for copy in self.last:
            copy.wait()


TOTAL_COPIES = 58


def total_scratch():
    return [
        pltpu.VMEM((HALF, LANES), jnp.bfloat16),
        pltpu.VMEM((HALF, LANES), jnp.bfloat16),
        pltpu.VMEM((3, 3, QUARTER, 128), jnp.bfloat16),
        pltpu.VMEM((3, QUARTER, 128), jnp.bfloat16),
        pltpu.VMEM((3, 3, EIGHTH, 128), jnp.bfloat16),
        pltpu.VMEM((3, EIGHTH, 128), jnp.bfloat16),
        pltpu.VMEM((3, 4, EIGHTH, 128), jnp.bfloat16),
        pltpu.SemaphoreType.DMA((TOTAL_COPIES,)),
        pltpu.SemaphoreType.DMA((TOTAL_COPIES,)),
    ]


class Small:
    def __init__(self, spot, value, core_in, ring_in, send, recv):
        self.spot, self.value, self.core_in, self.ring_in = spot, value, core_in, ring_in
        self.copies = Copies(send, recv)

    def core_start(self):
        self.core = self.copies.start(0, self.value, self.core_in, core_peer(self.spot))

    def core_finish(self):
        self.core.wait()
        own = self.spot[3]
        self.ring_in[0, own] = self.value[...] + self.core_in[...]

    def ring_start(self, stage):
        axis = (3, 1, 2)[stage]
        own = self.spot[axis]
        self.ring = [
            self.copies.start(1 + stage * 3 + distance - 1, self.ring_in.at[stage, own], self.ring_in.at[stage, own],
                              ring_peer(self.spot, axis, distance)) for distance in (2, 1, 3)]

    def ring_finish(self, stage):
        for copy in self.ring:
            copy.wait()
        total = self.ring_in[stage, 0] + self.ring_in[stage, 1] + self.ring_in[stage, 2] + self.ring_in[stage, 3]
        if stage < 2:
            self.ring_in[stage + 1, self.spot[(3, 1, 2)[stage + 1]]] = total
        return total


def small_scratch():
    return [
        pltpu.VMEM((SMALL, LANES), jnp.float32),
        pltpu.VMEM((3, 4, SMALL, LANES), jnp.float32),
        pltpu.SemaphoreType.DMA((10,)),
        pltpu.SemaphoreType.DMA((10,)),
    ]


def greet(spot, extra=()):
    barrier = pltpu.get_barrier_semaphore()
    peers = [core_peer(spot)] + [ring_peer(spot, axis, distance) for axis in (1, 2, 3) for distance in (1, 2, 3)]
    peers += list(extra)
    for peer in peers:
        pl.semaphore_signal(barrier, inc=1, device_id=peer, device_id_type=MESH)
    return lambda: pl.semaphore_wait(barrier, len(peers))


epsilon = 1e-05
OWN = 256
WIDE = OWN + 2 * DMAX
CH = 768
MID = 384
TILE = 64
BF = jnp.bfloat16
F32 = jnp.float32


def dot(left, right):
    return jnp.dot(left, right, preferred_element_type=F32)


def dot_t(left, right):
    return lax.dot_general(left, right, (((1,), (1,)), ((), ())), preferred_element_type=F32)


def dot_rows(left, right):
    return lax.dot_general(left, right, (((0,), (0,)), ((), ())), preferred_element_type=F32)


def strand(s, width=CH):
    return pl.ds(s * width, width)


def loop(count, body):
    def step(index, carry):
        body(index)
        return carry

    lax.fori_loop(0, count, step, 0, unroll=2 if count % 2 == 0 else 1)


def tile_at(index, base=0, size=TILE):
    return pl.ds(pl.multiple_of(base + index * size, size), size)


def standard(values):
    centre = jnp.mean(values, axis=-1, keepdims=True)
    shifted = values - centre
    scale = lax.rsqrt(jnp.mean(shifted * shifted, axis=-1, keepdims=True) + epsilon)
    return shifted * scale, centre, scale


def gelu_pair(z):
    size = 1.0 + 0.23164189 * jnp.abs(z)
    t = pl.reciprocal(size, approx=True)
    t = t * (2.0 - size * t)
    bell = jnp.exp(-0.5 * z * z)
    tail = t * (0.127414796 + t * (-0.142248368 + t * (0.7107068705 + t * (-0.7265760135 + t * 0.5307027145))))
    tail = tail * bell
    below = jnp.where(z >= 0.0, 1.0 - tail, tail)
    return z * below, below + z * (0.3989422804014327 * bell)


def norm_back(dz, hat, scale, gain):
    dhat = dz * gain
    return scale * (
        dhat - jnp.mean(dhat, axis=-1, keepdims=True) - hat * jnp.mean(dhat * hat, axis=-1, keepdims=True)
    )


def fold(values):
    return values.reshape(TILE // 8, 8, values.shape[-1]).sum(axis=0)


def step_kernel(
    dilation, trunk, tokens, table, norm_gain, mid_gain, perm, cotangent, conv_hbm, out_hbm,
    block_hbm, trunk_hbm, conv_grads, out_grads, table_hbm, gain_hbm, mid_hbm,
    block_out, table_grad, gain_grad, mid_grad, table_pad, result, result_sem,
    conv_w, out_w, matrix, move, hidden, relabelled, u_pad, u_low, u_high, hat, slope, scale, mid,
    mid_hat, mid_slope, mid_scale, q, wide, back, rounded, e, dm_pad, dm_low, dm_high, grad, gain_acc, mid_acc,
    weight_sem, halo_send, halo_recv, grads, *scratch,
):
    spot = coordinates()
    dp = lax.axis_index("dp")
    ctx = lax.axis_index("ctx")
    left = (dp, lax.rem(ctx + 31, 32))
    right = (dp, lax.rem(ctx + 1, 32))
    first_bin = jnp.where(ctx == 0, DMAX, 0)
    end_bin = jnp.where(ctx == 31, DMAX + OWN, WIDE)
    met = greet(spot, (left, right))
    weights = [
        pltpu.make_async_copy(conv_hbm, conv_w, weight_sem.at[0]),
        pltpu.make_async_copy(out_hbm, out_w, weight_sem.at[1]),
    ]
    for copy in weights:
        copy.start()
    each = len(total_scratch())
    totals = [Total(spot, grads.at[b], result.at[b], *scratch[b * each:(b + 1) * each]) for b in range(LAYERS)]
    small = Small(spot, *scratch[2 * each:])
    halos = Copies(halo_send, halo_recv)

    def trade(index, mine):
        return [
            halos.start(2 * index, mine.at[pl.ds(DMAX, DMAX)], mine.at[pl.ds(DMAX + OWN, DMAX)], left),
            halos.start(2 * index + 1, mine.at[pl.ds(OWN, DMAX)], mine.at[pl.ds(0, DMAX)], right),
        ]

    leaving = []

    def leave(source, target):
        copy = pltpu.make_async_copy(source, target, result_sem.at[len(leaving)])
        copy.start()
        leaving.append(copy)

    def leave_sums(b):
        leave(result.at[b, pl.ds(0, 2304)], conv_grads.at[b])
        for s in range(2):
            leave(result.at[b, pl.ds(2304 + s * MID, MID)], out_grads.at[b, :, strand(s, MID)])

    table_pad[...] = jnp.zeros_like(table_pad)
    rest = table[...]
    for part in range(3):
        piece = rest.astype(BF).astype(F32)
        table_pad[pl.ds(8 * part, 4)] = piece
        rest = rest - piece
    one_hot = (tokens[...] == lax.broadcasted_iota(jnp.int32, (8, OWN), 0)).astype(F32)
    three_hot = jnp.concatenate([one_hot] * 4, axis=0).astype(BF)
    added = dot_rows(three_hot, table_pad[...].astype(BF))
    hidden[0, pl.ds(DMAX, OWN)] = (trunk[...].astype(F32) + added).astype(BF)
    met()
    pending = trade(0, hidden.at[0])

    def fill_matrix(index):
        rows = tile_at(index)
        channel = lax.broadcasted_iota(jnp.int32, (TILE, CH), 0) + index * TILE
        matrix[rows] = jnp.where(channel == perm[...][None, :], 1.0, 0.0).astype(BF)

    loop(CH // TILE, fill_matrix)
    bin_from = lax.broadcasted_iota(jnp.int32, (OWN, WIDE), 1)
    bin_to = lax.broadcasted_iota(jnp.int32, (OWN, WIDE), 0) + DMAX
    inside = (bin_from >= first_bin) & (bin_from < end_bin)
    for b in range(LAYERS):
        for way in range(2):
            at = bin_to + (2 * way - 1) * dilation[b]
            move[b, way] = jnp.where(inside & (bin_from == at), 1.0, 0.0).astype(BF)
    e[pl.ds(0, OWN)] = (0.5 * cotangent[...].astype(F32)).astype(BF)

    for b in range(LAYERS):
        gain = norm_gain[pl.ds(b, 1)]
        mid_s = mid_gain[pl.ds(b, 1)]

        def front(rows, own):
            x = hidden[b, rows].astype(F32)
            hat_f, centre, inv = standard(x)
            hat_r = (relabelled[rows] - centre) * inv
            for s, normed in enumerate((hat_f, hat_r)):
                u, du = gelu_pair(normed * gain)
                u_pad[b, rows, strand(s)] = u.astype(BF)
                if own is not None:
                    hat[b, s, own] = normed
                    slope[b, s, own] = du
            if own is not None:
                scale[b, own] = jnp.broadcast_to(inv, (TILE, 128))

        relabelled[pl.ds(DMAX, OWN)] = dot(hidden[b, pl.ds(DMAX, OWN)], matrix[...])
        loop(OWN // TILE, lambda i: front(tile_at(i, DMAX), tile_at(i)))
        if b == 0:
            for copy in weights:
                copy.wait()
        for s in range(2):
            mid[s] = dot(u_pad[b, pl.ds(DMAX, OWN), strand(s)], conv_w[b, 1])
        for copy in pending:
            copy.wait()
        for base in (0, DMAX + OWN):
            relabelled[pl.ds(base, DMAX)] = dot(hidden[b, pl.ds(base, DMAX)], matrix[...])
            loop(DMAX // TILE, lambda i: front(tile_at(i, base), None))

        for s in range(2):
            u_low[b, s] = dot(move[b, s], u_pad[b, :, strand(s)]).astype(BF)
            u_high[b, s] = dot(move[b, 1 - s], u_pad[b, :, strand(s)]).astype(BF)
        for s in range(2):
            mid[s] += dot(u_low[b, s], conv_w[b, 0]) + dot(u_high[b, s], conv_w[b, 2])

        def middle(i):
            rows = tile_at(i)
            for s in range(2):
                normed, _, inv = standard(mid[s, rows])
                value, derivative = gelu_pair(normed * mid_s)
                q[b, s, rows] = value.astype(BF)
                mid_hat[b, s, rows] = normed
                mid_slope[b, s, rows] = derivative
                mid_scale[b, s, rows] = jnp.broadcast_to(inv, (TILE, 128))

        loop(OWN // TILE, middle)
        rounded[...] = dot(q[b, 1], out_w[b]).astype(BF)
        wide[0] = dot(q[b, 0], out_w[b])
        back[...] = dot_t(rounded[...], matrix[...])

        def join(i):
            rows = tile_at(i)
            total = wide[0, rows].astype(BF).astype(F32) + back[rows]
            following = (hidden[b, tile_at(i, DMAX)].astype(F32) + 0.5 * total).astype(BF)
            if b + 1 < LAYERS:
                hidden[b + 1, tile_at(i, DMAX)] = following
            else:
                block_out[rows] = following

        join(0)
        join(OWN // TILE - 1)
        if b + 1 < LAYERS:
            pending = trade(b + 1, hidden.at[b + 1])
        for i in range(1, OWN // TILE - 1):
            join(i)

    leave(block_out, block_hbm)
    grad[...] = cotangent[...]
    gain_acc[...] = jnp.zeros_like(gain_acc)
    mid_acc[...] = jnp.zeros_like(mid_acc)
    for b in (1, 0):
        gain = norm_gain[pl.ds(b, 1)]
        mid_s = mid_gain[pl.ds(b, 1)]
        sums = grads.at[b]
        if b == 0:
            e[pl.ds(0, OWN)] = (0.5 * grad[...].astype(F32)).astype(BF)
        e[pl.ds(OWN, OWN)] = dot(e[pl.ds(0, OWN)], matrix[...]).astype(BF)
        for s in range(2):
            mid[s] = dot_t(e[pl.ds(s * OWN, OWN)], out_w[b])

        def middle_back(i):
            rows = tile_at(i)
            total = jnp.zeros((8, MID), F32)
            for s in range(2):
                dz = mid[s, rows] * mid_slope[b, s, rows]
                normed = mid_hat[b, s, rows]
                total = total + fold(dz * normed)
                dm = norm_back(dz, normed, mid_scale[b, s, rows, 0:1], mid_s)
                dm_pad[b, tile_at(i, DMAX), strand(s, MID)] = dm.astype(BF)
            mid_acc[b] += total

        middle_back(0)
        middle_back(OWN // TILE - 1)
        pending = trade(LAYERS + b, dm_pad.at[b])
        for i in range(1, OWN // TILE - 1):
            middle_back(i)
        q_all = q[b].reshape(2 * OWN, MID)
        out_grad = dot_rows(q_all, e[...])
        sums[pl.ds(2304, MID)] = out_grad[:, :MID].astype(BF)
        sums[pl.ds(2688, MID)] = out_grad[:, MID:].astype(BF)
        own = pl.ds(DMAX, OWN)
        u_all = jnp.concatenate([u_pad[b, own, strand(s)] for s in range(2)], axis=0)
        dm_all = jnp.concatenate([dm_pad[b, own, strand(s, MID)] for s in range(2)], axis=0)
        for tap, left_side in enumerate((u_low[b].reshape(2 * OWN, CH), u_all, u_high[b].reshape(2 * OWN, CH))):
            sums[pl.ds(tap * CH, CH)] = dot_rows(left_side, dm_all).astype(BF)
        totals[b].core_start()
        for s in range(2):
            wide[s] = dot_t(dm_pad[b, own, strand(s, MID)], conv_w[b, 1])
        if b == 0:
            totals[1].a_to_b()
            totals[0].core_finish()
            totals[0].a_start()
        for copy in pending:
            copy.wait()
        for s in range(2):
            dm_low[s] = dot(move[b, 1 - s], dm_pad[b, :, strand(s, MID)]).astype(BF)
            dm_high[s] = dot(move[b, s], dm_pad[b, :, strand(s, MID)]).astype(BF)
        if b == 1:
            totals[1].core_finish()
            totals[1].a_start()
        for s in range(2):
            wide[s] += dot_t(dm_low[s], conv_w[b, 0]) + dot_t(dm_high[s], conv_w[b, 2])
        if b == 0:
            totals[1].b_to_c()

        def front_back(i):
            rows = tile_at(i)
            total = jnp.zeros((8, CH), F32)
            for s in range(2):
                dz = wide[s, rows] * slope[b, s, rows]
                normed = hat[b, s, rows]
                total = total + fold(dz * normed)
                dx = norm_back(dz, normed, scale[b, rows, 0:1], gain)
                if s == 0:
                    wide[0, rows] = dx
                else:
                    rounded[rows] = dx.astype(BF)
            gain_acc[b] += total

        loop(OWN // TILE, front_back)
        back[...] = dot_t(rounded[...], matrix[...])

        def join_back(i):
            rows = tile_at(i)
            total = grad[rows].astype(F32) + wide[0, rows].astype(BF).astype(F32) + back[rows]
            grad[rows] = total.astype(BF)

        loop(OWN // TILE, join_back)

    leave(grad, trunk_hbm)
    table_term = dot(one_hot.astype(BF), grad[...])
    small.value[pl.ds(0, 4)] = table_term[0:4, :MID]
    small.value[pl.ds(4, 4)] = table_term[0:4, MID:]
    for b in range(LAYERS):
        term = jnp.sum(gain_acc[b], axis=0, keepdims=True)
        small.value[pl.ds(8 + 2 * b, 1)] = term[:, :MID]
        small.value[pl.ds(9 + 2 * b, 1)] = term[:, MID:]
        small.value[pl.ds(12 + b, 1)] = jnp.sum(mid_acc[b], axis=0, keepdims=True)
    small.value[pl.ds(14, 2)] = jnp.zeros((2, MID), F32)
    small.core_start()
    totals[1].c_to_gather()
    totals[0].a_to_b()
    small.core_finish()
    small.ring_start(0)
    totals[1].a_gather()
    totals[0].b_to_c()
    small.ring_finish(0)
    small.ring_start(1)
    totals[0].c_to_gather()
    totals[1].forward()
    small.ring_finish(1)
    small.ring_start(2)
    totals[0].a_gather()
    totals[1].finish()
    leave_sums(1)
    sums = small.ring_finish(2)
    table_grad[:, pl.ds(0, MID)] = sums[0:4]
    table_grad[:, pl.ds(MID, MID)] = sums[4:8]
    for b in range(LAYERS):
        gain_grad[pl.ds(b, 1), pl.ds(0, MID)] = sums[8 + 2 * b:9 + 2 * b]
        gain_grad[pl.ds(b, 1), pl.ds(MID, MID)] = sums[9 + 2 * b:10 + 2 * b]
    mid_grad[...] = sums[12:14]
    leave(table_grad, table_hbm)
    leave(gain_grad, gain_hbm)
    leave(mid_grad, mid_hbm)
    totals[0].forward()
    totals[0].finish()
    leave_sums(0)
    for copy in leaving:
        copy.wait()


def whole_step(trunk, tokens, table, conv_w, out_w, norm_gain, mid_gain, perm, dilation, cotangent):
    vmem = pl.BlockSpec(memory_space=pltpu.VMEM)
    stay = pl.BlockSpec(memory_space=pl.ANY)
    smem = pl.BlockSpec(memory_space=pltpu.SMEM)
    scratch = [
        pltpu.VMEM((OWN, CH), BF),
        pltpu.VMEM((4, CH), F32),
        pltpu.VMEM((LAYERS, CH), F32),
        pltpu.VMEM((LAYERS, MID), F32),
        pltpu.VMEM((32, CH), F32),
        pltpu.VMEM((LAYERS, GROWS, LANES), BF),
        pltpu.SemaphoreType.DMA((11,)),
        pltpu.VMEM((LAYERS, 3, CH, MID), BF),
        pltpu.VMEM((LAYERS, MID, CH), BF),
        pltpu.VMEM((CH, CH), BF),
        pltpu.VMEM((LAYERS, 2, OWN, WIDE), BF),
        pltpu.VMEM((LAYERS, WIDE, CH), BF),
        pltpu.VMEM((WIDE, CH), F32),
        pltpu.VMEM((LAYERS, WIDE, 2 * CH), BF),
        pltpu.VMEM((LAYERS, 2, OWN, CH), BF),
        pltpu.VMEM((LAYERS, 2, OWN, CH), BF),
        pltpu.VMEM((LAYERS, 2, OWN, CH), F32),
        pltpu.VMEM((LAYERS, 2, OWN, CH), F32),
        pltpu.VMEM((LAYERS, OWN, 128), F32),
        pltpu.VMEM((2, OWN, MID), F32),
        pltpu.VMEM((LAYERS, 2, OWN, MID), F32),
        pltpu.VMEM((LAYERS, 2, OWN, MID), F32),
        pltpu.VMEM((LAYERS, 2, OWN, 128), F32),
        pltpu.VMEM((LAYERS, 2, OWN, MID), BF),
        pltpu.VMEM((2, OWN, CH), F32),
        pltpu.VMEM((OWN, CH), F32),
        pltpu.VMEM((OWN, CH), BF),
        pltpu.VMEM((2 * OWN, CH), BF),
        pltpu.VMEM((LAYERS, WIDE, 2 * MID), BF),
        pltpu.VMEM((2, OWN, MID), BF),
        pltpu.VMEM((2, OWN, MID), BF),
        pltpu.VMEM((OWN, CH), BF),
        pltpu.VMEM((LAYERS, 8, CH), F32),
        pltpu.VMEM((LAYERS, 8, MID), F32),
        pltpu.SemaphoreType.DMA((2,)),
        pltpu.SemaphoreType.DMA((8,)),
        pltpu.SemaphoreType.DMA((8,)),
        pltpu.VMEM((LAYERS, GROWS, LANES), BF),
    ]
    small = [pltpu.VMEM((SMALL, LANES), F32)] + small_scratch()
    return pl.pallas_call(
        step_kernel,
        out_shape=(
            jax.ShapeDtypeStruct((OWN, CH), BF),
            jax.ShapeDtypeStruct((OWN, CH), BF),
            jax.ShapeDtypeStruct((LAYERS, 3 * CH, MID), BF),
            jax.ShapeDtypeStruct((LAYERS, MID, CH), BF),
            jax.ShapeDtypeStruct((4, CH), F32),
            jax.ShapeDtypeStruct((LAYERS, CH), F32),
            jax.ShapeDtypeStruct((LAYERS, MID), F32),
        ),
        in_specs=[smem] + [vmem] * 7 + [stay] * 2,
        out_specs=(stay,) * 7,
        scratch_shapes=scratch + total_scratch() * 2 + small,
        compiler_params=pltpu.CompilerParams(collective_id=0, has_side_effects=True, vmem_limit_bytes=56 * 1024 * 1024),
        cost_estimate=pl.CostEstimate(flops=10**10, bytes_accessed=2 * 10**7, transcendentals=0),
        name="step",
    )(dilation, trunk, tokens, table, norm_gain, mid_gain, perm, cotangent, conv_w, out_w)


CONV_PIECES = 9
OUT_PIECES = 3


def widen_kernel(conv_in, out_in, block_in, trunk_in, table_in, gain_in, mid_in,
                 conv_out, out_out, block_out, trunk_out, table_out, gain_out, mid_out,
                 conv_narrow, out_narrow, conv_wide, out_wide, block_held, trunk_held, table_held, gain_held, mid_held,
                 in_sem, back_sem):
    work = []
    for source, target, narrow, broad, pieces in (
            (conv_in, conv_out, conv_narrow, conv_wide, CONV_PIECES), (out_in, out_out, out_narrow, out_wide, OUT_PIECES)):
        size = source.shape[0] // pieces
        for i in range(pieces):
            rows = pl.ds(i * size, size)
            index = len(work)
            work.append((
                pltpu.make_async_copy(source.at[rows], narrow.at[rows], in_sem.at[index]),
                pltpu.make_async_copy(broad.at[rows], target.at[rows], back_sem.at[index]),
                narrow, broad, rows))
    for source, target, held in (
            (block_in, block_out, block_held), (trunk_in, trunk_out, trunk_held), (table_in, table_out, table_held),
            (gain_in, gain_out, gain_held), (mid_in, mid_out, mid_held)):
        index = len(work)
        work.append((
            pltpu.make_async_copy(source, held, in_sem.at[index]),
            pltpu.make_async_copy(held, target, back_sem.at[index]), None, None, None))
    for fetch, *_ in work:
        fetch.start()
    for fetch, store, narrow, broad, rows in work:
        fetch.wait()
        if narrow is not None:
            broad[rows] = narrow[rows].astype(F32)
        store.start()
    for _, store, *_ in work:
        store.wait()


def widen(*arrays):
    stay = pl.BlockSpec(memory_space=pl.ANY)
    conv, out = arrays[:2]
    return pl.pallas_call(
        widen_kernel,
        out_shape=[jax.ShapeDtypeStruct(array.shape, F32 if i < 2 else array.dtype) for i, array in enumerate(arrays)],
        in_specs=[stay] * len(arrays),
        out_specs=[stay] * len(arrays),
        scratch_shapes=[
            pltpu.VMEM(conv.shape, BF), pltpu.VMEM(out.shape, BF), pltpu.VMEM(conv.shape, F32), pltpu.VMEM(out.shape, F32),
            *[pltpu.VMEM(array.shape, array.dtype) for array in arrays[2:]],
            pltpu.SemaphoreType.DMA((CONV_PIECES + OUT_PIECES + 5,)), pltpu.SemaphoreType.DMA((CONV_PIECES + OUT_PIECES + 5,)),
        ],
        compiler_params=pltpu.CompilerParams(vmem_limit_bytes=60 * 1024 * 1024),
        cost_estimate=pl.CostEstimate(flops=10**6, bytes_accessed=15 * 10**6, transcendentals=0),
        name="widen",
    )(*arrays)


def shards(trunk_input, tokens, token_table, conv_weight, out_weight, norm_gain, mid_gain, strand_perm, dilation, out_cotangent):
    block_out, trunk_grad, conv_total, out_total, table_total, gain_total, mid_total = whole_step(
        trunk_input[0], tokens, token_table, conv_weight, out_weight, norm_gain, mid_gain, strand_perm, dilation, out_cotangent[0])
    conv_total, out_total, block_out, trunk_grad, table_total, gain_total, mid_total = widen(
        conv_total.reshape(LAYERS * 3 * CH, MID), out_total.reshape(LAYERS * MID, CH), block_out, trunk_grad, table_total, gain_total, mid_total)
    return (block_out[None], trunk_grad[None], table_total, conv_total.reshape(LAYERS, 3, CH, MID),
            out_total.reshape(LAYERS, MID, CH), gain_total, mid_total)


def solution(mesh):
    placed = (P("dp", "ctx", None), P("dp", "ctx"), P(), P(), P(), P(), P(), P(), P(), P("dp", "ctx", None))
    return jax.shard_map(
        shards,
        mesh=mesh,
        in_specs=placed,
        out_specs=(P("dp", "ctx", None), P("dp", "ctx", None), P(), P(), P(), P(), P()),
        check_vma=False,
    )
```

```python
import jax
import jax.numpy as jnp
from jax import lax
from jax.experimental import pallas as pl
from jax.experimental.pallas import tpu as pltpu
from jax.sharding import PartitionSpec as P

LAYERS = 2
DMAX = 64

MESH = pl.DeviceIdType.MESH
GROWS = 3072
HALF = 1536
QUARTER = 384
EIGHTH = 96
SMALL = 16
LANES = 384


def place(core, y, z, x):
    return (lax.div(y, 2) * 2 + core, (lax.rem(y, 2) * 4 + z) * 4 + x)


def coordinates():
    dp = lax.axis_index("dp")
    ctx = lax.axis_index("ctx")
    y = lax.div(dp, 2) * 2 + lax.div(ctx, 16)
    return (lax.rem(dp, 2), y, lax.rem(lax.div(ctx, 4), 4), lax.rem(ctx, 4))


def ring_peer(spot, axis, distance):
    moved = list(spot)
    moved[axis] = lax.rem(spot[axis] + distance, 4)
    return place(*moved)


def core_peer(spot):
    return place(1 - spot[0], *spot[1:])


ORDERS = ((3, 1, 2), (1, 2, 3), (2, 3, 1))


class Copies:
    def __init__(self, send, recv):
        self.send, self.recv, self.open = send, recv, []

    def start(self, index, source, target, device):
        copy = pltpu.make_async_remote_copy(
            src_ref=source, dst_ref=target, send_sem=self.send.at[index],
            recv_sem=self.recv.at[index], device_id=device, device_id_type=MESH)
        copy.start()
        return copy


class Total:
    def __init__(self, spot, grads, result, core_in, sums0, in_a, sums1, in_b, sums2, in_c, send, recv):
        self.spot, self.grads, self.result = spot, grads, result
        self.core_in, self.sums0, self.in_a, self.sums1 = core_in, sums0, in_a, sums1
        self.in_b, self.sums2, self.in_c = in_b, sums2, in_c
        self.copies = Copies(send, recv)
        self.base = spot[0] * HALF

    def lanes(self, third):
        return pl.ds(third * 128, 128)

    def core_start(self):
        other = (1 - self.spot[0]) * HALF
        self.core = self.copies.start(0, self.grads.at[pl.ds(other, HALF)], self.core_in, core_peer(self.spot))

    def core_finish(self):
        self.core.wait()

        def body(step, carry):
            rows = pl.ds(pl.multiple_of(step * QUARTER, 32), QUARTER)
            mine = pl.ds(pl.multiple_of(self.base + step * QUARTER, 32), QUARTER)
            self.sums0[rows] = (self.grads[mine].astype(jnp.float32) + self.core_in[rows].astype(jnp.float32)).astype(jnp.bfloat16)
            return carry

        lax.fori_loop(0, 4, body, 0)

    def a_start(self):
        self.a = []
        for third, order in enumerate(ORDERS):
            for distance in (2, 1, 3):
                chunk = lax.rem(self.spot[order[0]] + distance, 4)
                self.a.append(self.copies.start(
                    1 + third * 3 + distance - 1,
                    self.sums0.at[pl.ds(chunk * QUARTER, QUARTER), self.lanes(third)],
                    self.in_a.at[third, distance - 1], ring_peer(self.spot, order[0], distance)))

    def a_to_b(self):
        self.b = []
        for third, order in enumerate(ORDERS):
            mine = pl.ds(pl.multiple_of(self.spot[order[0]] * QUARTER, 32), QUARTER)
            for copy in self.a[third * 3:third * 3 + 3]:
                copy.wait()
            total = self.sums0[mine, self.lanes(third)].astype(jnp.float32)
            for slot in range(3):
                total = total + self.in_a[third, slot].astype(jnp.float32)
            self.sums1[third] = total.astype(jnp.bfloat16)
            for distance in (2, 1, 3):
                chunk = lax.rem(self.spot[order[1]] + distance, 4)
                self.b.append(self.copies.start(
                    10 + third * 3 + distance - 1,
                    self.sums1.at[third, pl.ds(chunk * EIGHTH, EIGHTH)],
                    self.in_b.at[third, distance - 1], ring_peer(self.spot, order[1], distance)))

    def b_to_c(self):
        self.c = []
        for third, order in enumerate(ORDERS):
            mine = pl.ds(pl.multiple_of(self.spot[order[1]] * EIGHTH, 32), EIGHTH)
            for copy in self.b[third * 3:third * 3 + 3]:
                copy.wait()
            total = self.sums1[third, mine].astype(jnp.float32)
            for slot in range(3):
                total = total + self.in_b[third, slot].astype(jnp.float32)
            self.sums2[third] = total.astype(jnp.bfloat16)
            for distance in (2, 1, 3):
                self.c.append(self.copies.start(
                    19 + third * 3 + distance - 1, self.sums2.at[third],
                    self.in_c.at[third, self.spot[order[2]]], ring_peer(self.spot, order[2], distance)))
            self.in_c[third, self.spot[order[2]]] = self.sums2[third]

    def rows_of(self, third):
        order = ORDERS[third]
        quarter = self.base + self.spot[order[0]] * QUARTER
        return quarter, quarter + self.spot[order[1]] * EIGHTH

    def spread(self, third, which):
        order = ORDERS[third]
        quarter, eighth = self.rows_of(third)
        rows = pl.ds(eighth, EIGHTH) if which else pl.ds(quarter, QUARTER)
        piece = self.result.at[rows, self.lanes(third)]
        return [
            self.copies.start(28 + which * 9 + third * 3 + distance - 1, piece, piece, ring_peer(self.spot, order[which], distance))
            for distance in (1, 3, 2)]

    def c_to_gather(self):
        self.early = []
        for third in range(3):
            for copy in self.c[third * 3:third * 3 + 3]:
                copy.wait()
            total = self.in_c[third, 0].astype(jnp.float32)
            for slot in range(1, 4):
                total = total + self.in_c[third, slot].astype(jnp.float32)
            _, eighth = self.rows_of(third)
            self.result[pl.ds(pl.multiple_of(eighth, 32), EIGHTH), self.lanes(third)] = total.astype(jnp.bfloat16)
            self.early += self.spread(third, 1)

    def pass_on(self, third, distance):
        quarter = lax.rem(self.spot[ORDERS[third][0]] + 4 - distance, 4)
        piece = self.result.at[pl.ds(self.base + quarter * QUARTER, QUARTER), self.lanes(third)]
        self.last.append(self.copies.start(46 + third * 4 + distance, piece, piece, core_peer(self.spot)))

    def a_gather(self):
        self.late, self.last = [], []
        for third in range(3):
            for copy in self.early[third * 3:third * 3 + 3]:
                copy.wait()
            self.late += self.spread(third, 0)
        for third in range(3):
            self.pass_on(third, 0)

    def forward(self):
        for slot, distance in enumerate((1, 3, 2)):
            for third in range(3):
                self.late[third * 3 + slot].wait()
                self.pass_on(third, distance)

    def finish(self):
        for copy in self.last:
            copy.wait()


TOTAL_COPIES = 58


def total_scratch():
    return [
        pltpu.VMEM((HALF, LANES), jnp.bfloat16),
        pltpu.VMEM((HALF, LANES), jnp.bfloat16),
        pltpu.VMEM((3, 3, QUARTER, 128), jnp.bfloat16),
        pltpu.VMEM((3, QUARTER, 128), jnp.bfloat16),
        pltpu.VMEM((3, 3, EIGHTH, 128), jnp.bfloat16),
        pltpu.VMEM((3, EIGHTH, 128), jnp.bfloat16),
        pltpu.VMEM((3, 4, EIGHTH, 128), jnp.bfloat16),
        pltpu.SemaphoreType.DMA((TOTAL_COPIES,)),
        pltpu.SemaphoreType.DMA((TOTAL_COPIES,)),
    ]


class Small:
    def __init__(self, spot, value, core_in, ring_in, send, recv):
        self.spot, self.value, self.core_in, self.ring_in = spot, value, core_in, ring_in
        self.copies = Copies(send, recv)

    def core_start(self):
        self.core = self.copies.start(0, self.value, self.core_in, core_peer(self.spot))

    def core_finish(self):
        self.core.wait()
        own = self.spot[3]
        self.ring_in[0, own] = self.value[...] + self.core_in[...]

    def ring_start(self, stage):
        axis = (3, 1, 2)[stage]
        own = self.spot[axis]
        self.ring = [
            self.copies.start(1 + stage * 3 + distance - 1, self.ring_in.at[stage, own], self.ring_in.at[stage, own],
                              ring_peer(self.spot, axis, distance)) for distance in (2, 1, 3)]

    def ring_finish(self, stage):
        for copy in self.ring:
            copy.wait()
        total = self.ring_in[stage, 0] + self.ring_in[stage, 1] + self.ring_in[stage, 2] + self.ring_in[stage, 3]
        if stage < 2:
            self.ring_in[stage + 1, self.spot[(3, 1, 2)[stage + 1]]] = total
        return total


def small_scratch():
    return [
        pltpu.VMEM((SMALL, LANES), jnp.float32),
        pltpu.VMEM((3, 4, SMALL, LANES), jnp.float32),
        pltpu.SemaphoreType.DMA((10,)),
        pltpu.SemaphoreType.DMA((10,)),
    ]


def greet(spot, extra=()):
    barrier = pltpu.get_barrier_semaphore()
    peers = [core_peer(spot)] + [ring_peer(spot, axis, distance) for axis in (1, 2, 3) for distance in (1, 2, 3)]
    peers += list(extra)
    for peer in peers:
        pl.semaphore_signal(barrier, inc=1, device_id=peer, device_id_type=MESH)
    return lambda: pl.semaphore_wait(barrier, len(peers))


epsilon = 1e-05
OWN = 256
WIDE = OWN + 2 * DMAX
CH = 768
MID = 384
TILE = 64
BF = jnp.bfloat16
F32 = jnp.float32


def dot(left, right):
    return jnp.dot(left, right, preferred_element_type=F32)


def dot_t(left, right):
    return lax.dot_general(left, right, (((1,), (1,)), ((), ())), preferred_element_type=F32)


def dot_rows(left, right):
    return lax.dot_general(left, right, (((0,), (0,)), ((), ())), preferred_element_type=F32)


def strand(s, width=CH):
    return pl.ds(s * width, width)


def loop(count, body):
    def step(index, carry):
        body(index)
        return carry

    lax.fori_loop(0, count, step, 0, unroll=4 if count % 4 == 0 else 1)


def tile_at(index, base=0, size=TILE):
    return pl.ds(pl.multiple_of(base + index * size, size), size)


def standard(values):
    centre = jnp.mean(values, axis=-1, keepdims=True)
    shifted = values - centre
    scale = lax.rsqrt(jnp.mean(shifted * shifted, axis=-1, keepdims=True) + epsilon)
    return shifted * scale, centre, scale


def gelu_pair(z):
    size = 1.0 + 0.23164189 * jnp.abs(z)
    t = pl.reciprocal(size, approx=True)
    t = t * (2.0 - size * t)
    bell = jnp.exp(-0.5 * z * z)
    tail = t * (0.127414796 + t * (-0.142248368 + t * (0.7107068705 + t * (-0.7265760135 + t * 0.5307027145))))
    tail = tail * bell
    below = jnp.where(z >= 0.0, 1.0 - tail, tail)
    return z * below, below + z * (0.3989422804014327 * bell)


def norm_back(dz, hat, scale, gain):
    dhat = dz * gain
    return scale * (
        dhat - jnp.mean(dhat, axis=-1, keepdims=True) - hat * jnp.mean(dhat * hat, axis=-1, keepdims=True)
    )


def fold(values):
    return values.reshape(TILE // 8, 8, values.shape[-1]).sum(axis=0)


def step_kernel(
    dilation, trunk, tokens, table, norm_gain, mid_gain, perm, cotangent, conv_hbm, out_hbm,
    block_hbm, trunk_hbm, conv_grads, out_grads, table_hbm, gain_hbm, mid_hbm,
    block_out, table_grad, gain_grad, mid_grad, table_pad, result, result_sem,
    conv_w, out_w, matrix, move, hidden, relabelled, u_pad, u_low, u_high, hat, slope, scale, mid,
    mid_hat, mid_slope, mid_scale, q, wide, back, rounded, e, dm_pad, dm_low, dm_high, grad, gain_acc, mid_acc,
    weight_sem, halo_send, halo_recv, grads, *scratch,
):
    spot = coordinates()
    dp = lax.axis_index("dp")
    ctx = lax.axis_index("ctx")
    left = (dp, lax.rem(ctx + 31, 32))
    right = (dp, lax.rem(ctx + 1, 32))
    first_bin = jnp.where(ctx == 0, DMAX, 0)
    end_bin = jnp.where(ctx == 31, DMAX + OWN, WIDE)
    met = greet(spot, (left, right))
    weights = [
        pltpu.make_async_copy(conv_hbm, conv_w, weight_sem.at[0]),
        pltpu.make_async_copy(out_hbm, out_w, weight_sem.at[1]),
    ]
    for copy in weights:
        copy.start()
    each = len(total_scratch())
    totals = [Total(spot, grads.at[b], result.at[b], *scratch[b * each:(b + 1) * each]) for b in range(LAYERS)]
    small = Small(spot, *scratch[2 * each:])
    halos = Copies(halo_send, halo_recv)

    def trade(index, mine):
        return [
            halos.start(2 * index, mine.at[pl.ds(DMAX, DMAX)], mine.at[pl.ds(DMAX + OWN, DMAX)], left),
            halos.start(2 * index + 1, mine.at[pl.ds(OWN, DMAX)], mine.at[pl.ds(0, DMAX)], right),
        ]

    leaving = []

    def leave(source, target):
        copy = pltpu.make_async_copy(source, target, result_sem.at[len(leaving)])
        copy.start()
        leaving.append(copy)

    def leave_sums(b):
        leave(result.at[b, pl.ds(0, 2304)], conv_grads.at[b])
        for s in range(2):
            leave(result.at[b, pl.ds(2304 + s * MID, MID)], out_grads.at[b, :, strand(s, MID)])

    table_pad[...] = jnp.zeros_like(table_pad)
    rest = table[...]
    for part in range(3):
        piece = rest.astype(BF).astype(F32)
        table_pad[pl.ds(8 * part, 4)] = piece
        rest = rest - piece
    one_hot = (tokens[...] == lax.broadcasted_iota(jnp.int32, (8, OWN), 0)).astype(F32)
    three_hot = jnp.concatenate([one_hot] * 4, axis=0).astype(BF)
    added = dot_rows(three_hot, table_pad[...].astype(BF))
    hidden[0, pl.ds(DMAX, OWN)] = (trunk[...].astype(F32) + added).astype(BF)
    met()
    pending = trade(0, hidden.at[0])

    def fill_matrix(index):
        rows = tile_at(index)
        channel = lax.broadcasted_iota(jnp.int32, (TILE, CH), 0) + index * TILE
        matrix[rows] = jnp.where(channel == perm[...][None, :], 1.0, 0.0).astype(BF)

    loop(CH // TILE, fill_matrix)
    bin_from = lax.broadcasted_iota(jnp.int32, (OWN, WIDE), 1)
    bin_to = lax.broadcasted_iota(jnp.int32, (OWN, WIDE), 0) + DMAX
    inside = (bin_from >= first_bin) & (bin_from < end_bin)
    for b in range(LAYERS):
        for way in range(2):
            at = bin_to + (2 * way - 1) * dilation[b]
            move[b, way] = jnp.where(inside & (bin_from == at), 1.0, 0.0).astype(BF)
    e[pl.ds(0, OWN)] = (0.5 * cotangent[...].astype(F32)).astype(BF)

    for b in range(LAYERS):
        gain = norm_gain[pl.ds(b, 1)]
        mid_s = mid_gain[pl.ds(b, 1)]

        def front(rows, own):
            x = hidden[b, rows].astype(F32)
            hat_f, centre, inv = standard(x)
            hat_r = (relabelled[rows] - centre) * inv
            for s, normed in enumerate((hat_f, hat_r)):
                u, du = gelu_pair(normed * gain)
                u_pad[b, rows, strand(s)] = u.astype(BF)
                if own is not None:
                    hat[b, s, own] = normed
                    slope[b, s, own] = du
            if own is not None:
                scale[b, own] = jnp.broadcast_to(inv, (TILE, 128))

        relabelled[pl.ds(DMAX, OWN)] = dot(hidden[b, pl.ds(DMAX, OWN)], matrix[...])
        loop(OWN // TILE, lambda i: front(tile_at(i, DMAX), tile_at(i)))
        if b == 0:
            for copy in weights:
                copy.wait()
        for s in range(2):
            mid[s] = dot(u_pad[b, pl.ds(DMAX, OWN), strand(s)], conv_w[b, 1])
        for copy in pending:
            copy.wait()
        for base in (0, DMAX + OWN):
            relabelled[pl.ds(base, DMAX)] = dot(hidden[b, pl.ds(base, DMAX)], matrix[...])
            loop(DMAX // TILE, lambda i: front(tile_at(i, base), None))

        for s in range(2):
            u_low[b, s] = dot(move[b, s], u_pad[b, :, strand(s)]).astype(BF)
            u_high[b, s] = dot(move[b, 1 - s], u_pad[b, :, strand(s)]).astype(BF)
        for s in range(2):
            mid[s] += dot(u_low[b, s], conv_w[b, 0]) + dot(u_high[b, s], conv_w[b, 2])

        def middle(i):
            rows = tile_at(i)
            for s in range(2):
                normed, _, inv = standard(mid[s, rows])
                value, derivative = gelu_pair(normed * mid_s)
                q[b, s, rows] = value.astype(BF)
                mid_hat[b, s, rows] = normed
                mid_slope[b, s, rows] = derivative
                mid_scale[b, s, rows] = jnp.broadcast_to(inv, (TILE, 128))

        loop(OWN // TILE, middle)
        rounded[...] = dot(q[b, 1], out_w[b]).astype(BF)
        wide[0] = dot(q[b, 0], out_w[b])
        back[...] = dot_t(rounded[...], matrix[...])

        def join(i):
            rows = tile_at(i)
            total = wide[0, rows].astype(BF).astype(F32) + back[rows]
            following = (hidden[b, tile_at(i, DMAX)].astype(F32) + 0.5 * total).astype(BF)
            if b + 1 < LAYERS:
                hidden[b + 1, tile_at(i, DMAX)] = following
            else:
                block_out[rows] = following

        join(0)
        join(OWN // TILE - 1)
        if b + 1 < LAYERS:
            pending = trade(b + 1, hidden.at[b + 1])
        for i in range(1, OWN // TILE - 1):
            join(i)

    leave(block_out, block_hbm)
    grad[...] = cotangent[...]
    gain_acc[...] = jnp.zeros_like(gain_acc)
    mid_acc[...] = jnp.zeros_like(mid_acc)
    for b in (1, 0):
        gain = norm_gain[pl.ds(b, 1)]
        mid_s = mid_gain[pl.ds(b, 1)]
        sums = grads.at[b]
        if b == 0:
            e[pl.ds(0, OWN)] = (0.5 * grad[...].astype(F32)).astype(BF)
        e[pl.ds(OWN, OWN)] = dot(e[pl.ds(0, OWN)], matrix[...]).astype(BF)
        for s in range(2):
            mid[s] = dot_t(e[pl.ds(s * OWN, OWN)], out_w[b])

        def middle_back(i):
            rows = tile_at(i)
            total = jnp.zeros((8, MID), F32)
            for s in range(2):
                dz = mid[s, rows] * mid_slope[b, s, rows]
                normed = mid_hat[b, s, rows]
                total = total + fold(dz * normed)
                dm = norm_back(dz, normed, mid_scale[b, s, rows, 0:1], mid_s)
                dm_pad[b, tile_at(i, DMAX), strand(s, MID)] = dm.astype(BF)
            mid_acc[b] += total

        middle_back(0)
        middle_back(OWN // TILE - 1)
        pending = trade(LAYERS + b, dm_pad.at[b])
        for i in range(1, OWN // TILE - 1):
            middle_back(i)
        q_all = q[b].reshape(2 * OWN, MID)
        out_grad = dot_rows(q_all, e[...])
        sums[pl.ds(2304, MID)] = out_grad[:, :MID].astype(BF)
        sums[pl.ds(2688, MID)] = out_grad[:, MID:].astype(BF)
        own = pl.ds(DMAX, OWN)
        u_all = jnp.concatenate([u_pad[b, own, strand(s)] for s in range(2)], axis=0)
        dm_all = jnp.concatenate([dm_pad[b, own, strand(s, MID)] for s in range(2)], axis=0)
        for tap, left_side in enumerate((u_low[b].reshape(2 * OWN, CH), u_all, u_high[b].reshape(2 * OWN, CH))):
            sums[pl.ds(tap * CH, CH)] = dot_rows(left_side, dm_all).astype(BF)
        totals[b].core_start()
        for s in range(2):
            wide[s] = dot_t(dm_pad[b, own, strand(s, MID)], conv_w[b, 1])
        if b == 0:
            totals[1].a_to_b()
            totals[0].core_finish()
            totals[0].a_start()
        for copy in pending:
            copy.wait()
        for s in range(2):
            dm_low[s] = dot(move[b, 1 - s], dm_pad[b, :, strand(s, MID)]).astype(BF)
            dm_high[s] = dot(move[b, s], dm_pad[b, :, strand(s, MID)]).astype(BF)
        if b == 1:
            totals[1].core_finish()
            totals[1].a_start()
        for s in range(2):
            wide[s] += dot_t(dm_low[s], conv_w[b, 0]) + dot_t(dm_high[s], conv_w[b, 2])
        if b == 0:
            totals[1].b_to_c()

        def front_back(i):
            rows = tile_at(i)
            total = jnp.zeros((8, CH), F32)
            for s in range(2):
                dz = wide[s, rows] * slope[b, s, rows]
                normed = hat[b, s, rows]
                total = total + fold(dz * normed)
                dx = norm_back(dz, normed, scale[b, rows, 0:1], gain)
                if s == 0:
                    wide[0, rows] = dx
                else:
                    rounded[rows] = dx.astype(BF)
            gain_acc[b] += total

        loop(OWN // TILE, front_back)
        back[...] = dot_t(rounded[...], matrix[...])

        def join_back(i):
            rows = tile_at(i)
            total = grad[rows].astype(F32) + wide[0, rows].astype(BF).astype(F32) + back[rows]
            grad[rows] = total.astype(BF)

        loop(OWN // TILE, join_back)

    leave(grad, trunk_hbm)
    table_term = dot(one_hot.astype(BF), grad[...])
    small.value[pl.ds(0, 4)] = table_term[0:4, :MID]
    small.value[pl.ds(4, 4)] = table_term[0:4, MID:]
    for b in range(LAYERS):
        term = jnp.sum(gain_acc[b], axis=0, keepdims=True)
        small.value[pl.ds(8 + 2 * b, 1)] = term[:, :MID]
        small.value[pl.ds(9 + 2 * b, 1)] = term[:, MID:]
        small.value[pl.ds(12 + b, 1)] = jnp.sum(mid_acc[b], axis=0, keepdims=True)
    small.value[pl.ds(14, 2)] = jnp.zeros((2, MID), F32)
    small.core_start()
    totals[1].c_to_gather()
    totals[0].a_to_b()
    small.core_finish()
    small.ring_start(0)
    totals[1].a_gather()
    totals[0].b_to_c()
    small.ring_finish(0)
    small.ring_start(1)
    totals[0].c_to_gather()
    totals[1].forward()
    small.ring_finish(1)
    small.ring_start(2)
    totals[0].a_gather()
    totals[1].finish()
    leave_sums(1)
    sums = small.ring_finish(2)
    table_grad[:, pl.ds(0, MID)] = sums[0:4]
    table_grad[:, pl.ds(MID, MID)] = sums[4:8]
    for b in range(LAYERS):
        gain_grad[pl.ds(b, 1), pl.ds(0, MID)] = sums[8 + 2 * b:9 + 2 * b]
        gain_grad[pl.ds(b, 1), pl.ds(MID, MID)] = sums[9 + 2 * b:10 + 2 * b]
    mid_grad[...] = sums[12:14]
    leave(table_grad, table_hbm)
    leave(gain_grad, gain_hbm)
    leave(mid_grad, mid_hbm)
    totals[0].forward()
    totals[0].finish()
    leave_sums(0)
    for copy in leaving:
        copy.wait()


def whole_step(trunk, tokens, table, conv_w, out_w, norm_gain, mid_gain, perm, dilation, cotangent):
    vmem = pl.BlockSpec(memory_space=pltpu.VMEM)
    stay = pl.BlockSpec(memory_space=pl.ANY)
    smem = pl.BlockSpec(memory_space=pltpu.SMEM)
    scratch = [
        pltpu.VMEM((OWN, CH), BF),
        pltpu.VMEM((4, CH), F32),
        pltpu.VMEM((LAYERS, CH), F32),
        pltpu.VMEM((LAYERS, MID), F32),
        pltpu.VMEM((32, CH), F32),
        pltpu.VMEM((LAYERS, GROWS, LANES), BF),
        pltpu.SemaphoreType.DMA((11,)),
        pltpu.VMEM((LAYERS, 3, CH, MID), BF),
        pltpu.VMEM((LAYERS, MID, CH), BF),
        pltpu.VMEM((CH, CH), BF),
        pltpu.VMEM((LAYERS, 2, OWN, WIDE), BF),
        pltpu.VMEM((LAYERS, WIDE, CH), BF),
        pltpu.VMEM((WIDE, CH), F32),
        pltpu.VMEM((LAYERS, WIDE, 2 * CH), BF),
        pltpu.VMEM((LAYERS, 2, OWN, CH), BF),
        pltpu.VMEM((LAYERS, 2, OWN, CH), BF),
        pltpu.VMEM((LAYERS, 2, OWN, CH), F32),
        pltpu.VMEM((LAYERS, 2, OWN, CH), F32),
        pltpu.VMEM((LAYERS, OWN, 128), F32),
        pltpu.VMEM((2, OWN, MID), F32),
        pltpu.VMEM((LAYERS, 2, OWN, MID), F32),
        pltpu.VMEM((LAYERS, 2, OWN, MID), F32),
        pltpu.VMEM((LAYERS, 2, OWN, 128), F32),
        pltpu.VMEM((LAYERS, 2, OWN, MID), BF),
        pltpu.VMEM((2, OWN, CH), F32),
        pltpu.VMEM((OWN, CH), F32),
        pltpu.VMEM((OWN, CH), BF),
        pltpu.VMEM((2 * OWN, CH), BF),
        pltpu.VMEM((LAYERS, WIDE, 2 * MID), BF),
        pltpu.VMEM((2, OWN, MID), BF),
        pltpu.VMEM((2, OWN, MID), BF),
        pltpu.VMEM((OWN, CH), BF),
        pltpu.VMEM((LAYERS, 8, CH), F32),
        pltpu.VMEM((LAYERS, 8, MID), F32),
        pltpu.SemaphoreType.DMA((2,)),
        pltpu.SemaphoreType.DMA((8,)),
        pltpu.SemaphoreType.DMA((8,)),
        pltpu.VMEM((LAYERS, GROWS, LANES), BF),
    ]
    small = [pltpu.VMEM((SMALL, LANES), F32)] + small_scratch()
    return pl.pallas_call(
        step_kernel,
        out_shape=(
            jax.ShapeDtypeStruct((OWN, CH), BF),
            jax.ShapeDtypeStruct((OWN, CH), BF),
            jax.ShapeDtypeStruct((LAYERS, 3 * CH, MID), BF),
            jax.ShapeDtypeStruct((LAYERS, MID, CH), BF),
            jax.ShapeDtypeStruct((4, CH), F32),
            jax.ShapeDtypeStruct((LAYERS, CH), F32),
            jax.ShapeDtypeStruct((LAYERS, MID), F32),
        ),
        in_specs=[smem] + [vmem] * 7 + [stay] * 2,
        out_specs=(stay,) * 7,
        scratch_shapes=scratch + total_scratch() * 2 + small,
        compiler_params=pltpu.CompilerParams(collective_id=0, has_side_effects=True, vmem_limit_bytes=56 * 1024 * 1024),
        cost_estimate=pl.CostEstimate(flops=10**10, bytes_accessed=2 * 10**7, transcendentals=0),
        name="step",
    )(dilation, trunk, tokens, table, norm_gain, mid_gain, perm, cotangent, conv_w, out_w)


CONV_PIECES = 9
OUT_PIECES = 3


def widen_kernel(conv_in, out_in, block_in, trunk_in, table_in, gain_in, mid_in,
                 conv_out, out_out, block_out, trunk_out, table_out, gain_out, mid_out,
                 conv_narrow, out_narrow, conv_wide, out_wide, block_held, trunk_held, table_held, gain_held, mid_held,
                 in_sem, back_sem):
    work = []
    for source, target, narrow, broad, pieces in (
            (conv_in, conv_out, conv_narrow, conv_wide, CONV_PIECES), (out_in, out_out, out_narrow, out_wide, OUT_PIECES)):
        size = source.shape[0] // pieces
        for i in range(pieces):
            rows = pl.ds(i * size, size)
            index = len(work)
            work.append((
                pltpu.make_async_copy(source.at[rows], narrow.at[rows], in_sem.at[index]),
                pltpu.make_async_copy(broad.at[rows], target.at[rows], back_sem.at[index]),
                narrow, broad, rows))
    for source, target, held in (
            (block_in, block_out, block_held), (trunk_in, trunk_out, trunk_held), (table_in, table_out, table_held),
            (gain_in, gain_out, gain_held), (mid_in, mid_out, mid_held)):
        index = len(work)
        work.append((
            pltpu.make_async_copy(source, held, in_sem.at[index]),
            pltpu.make_async_copy(held, target, back_sem.at[index]), None, None, None))
    for fetch, *_ in work:
        fetch.start()
    for fetch, store, narrow, broad, rows in work:
        fetch.wait()
        if narrow is not None:
            broad[rows] = narrow[rows].astype(F32)
        store.start()
    for _, store, *_ in work:
        store.wait()


def widen(*arrays):
    stay = pl.BlockSpec(memory_space=pl.ANY)
    conv, out = arrays[:2]
    return pl.pallas_call(
        widen_kernel,
        out_shape=[jax.ShapeDtypeStruct(array.shape, F32 if i < 2 else array.dtype) for i, array in enumerate(arrays)],
        in_specs=[stay] * len(arrays),
        out_specs=[stay] * len(arrays),
        scratch_shapes=[
            pltpu.VMEM(conv.shape, BF), pltpu.VMEM(out.shape, BF), pltpu.VMEM(conv.shape, F32), pltpu.VMEM(out.shape, F32),
            *[pltpu.VMEM(array.shape, array.dtype) for array in arrays[2:]],
            pltpu.SemaphoreType.DMA((CONV_PIECES + OUT_PIECES + 5,)), pltpu.SemaphoreType.DMA((CONV_PIECES + OUT_PIECES + 5,)),
        ],
        compiler_params=pltpu.CompilerParams(vmem_limit_bytes=60 * 1024 * 1024),
        cost_estimate=pl.CostEstimate(flops=10**6, bytes_accessed=15 * 10**6, transcendentals=0),
        name="widen",
    )(*arrays)


def shards(trunk_input, tokens, token_table, conv_weight, out_weight, norm_gain, mid_gain, strand_perm, dilation, out_cotangent):
    block_out, trunk_grad, conv_total, out_total, table_total, gain_total, mid_total = whole_step(
        trunk_input[0], tokens, token_table, conv_weight, out_weight, norm_gain, mid_gain, strand_perm, dilation, out_cotangent[0])
    conv_total, out_total, block_out, trunk_grad, table_total, gain_total, mid_total = widen(
        conv_total.reshape(LAYERS * 3 * CH, MID), out_total.reshape(LAYERS * MID, CH), block_out, trunk_grad, table_total, gain_total, mid_total)
    return (block_out[None], trunk_grad[None], table_total, conv_total.reshape(LAYERS, 3, CH, MID),
            out_total.reshape(LAYERS, MID, CH), gain_total, mid_total)


def solution(mesh):
    placed = (P("dp", "ctx", None), P("dp", "ctx"), P(), P(), P(), P(), P(), P(), P(), P("dp", "ctx", None))
    return jax.shard_map(
        shards,
        mesh=mesh,
        in_specs=placed,
        out_specs=(P("dp", "ctx", None), P("dp", "ctx", None), P(), P(), P(), P(), P()),
        check_vma=False,
    )
```
